32 devices in a mesh: dp: 8 (over y, x, core), tensor: 4 (over z).
Axes of the slice: x: 2, y: 2, z: 4, core: 2. Of those that a mesh axis runs over, the one named last changes fastest.
Arguments:
- hidden_in: bfloat16 [16384, 768], P(('dp', 'tensor')), may hold values from -6 to 6
- lengths: int32 [128], P('dp'), may hold values from 96 to 128, as said below
- span_start: int32 [128], P('dp'), may hold values from 1 to 63
- span_len: int32 [128], P('dp'), may hold values from 2 to 17
- mask_embed: bfloat16 [768], replicated, may hold values from -6 to 6
- w_query: bfloat16 [768, 768], P(None, 'tensor'), may hold values from -0.21875 to 0.21875
- b_query: bfloat16 [768], P('tensor'), may hold values from -3 to 3
- w_key: bfloat16 [768, 768], P(None, 'tensor'), may hold values from -0.21875 to 0.21875
- w_value: bfloat16 [768, 768], P(None, 'tensor'), may hold values from -0.21875 to 0.21875
- b_value: bfloat16 [768], P('tensor'), may hold values from -3 to 3
- w_out: bfloat16 [768, 768], P('tensor'), may hold values from -1.25 to 1.25
- b_out: bfloat16 [768], replicated, may hold values from -3 to 3
- g_attn: bfloat16 [768], replicated, may hold values from 0.25 to 1.75
- s_attn: bfloat16 [768], replicated, may hold values from -2 to 2
- w_in: bfloat16 [768, 3072], P(None, 'tensor'), may hold values from -0.21875 to 0.21875
- b_in: bfloat16 [3072], P('tensor'), may hold values from -3 to 3
- w_back: bfloat16 [3072, 768], P('tensor'), may hold values from -0.15625 to 0.15625
- b_back: bfloat16 [768], replicated, may hold values from -3 to 3
- g_ffn: bfloat16 [768], replicated, may hold values from 0.25 to 1.75
- s_ffn: bfloat16 [768], replicated, may hold values from -2 to 2
- cotangent: bfloat16 [16384, 768], P(('dp', 'tensor')), may hold values from -6 to 6
Outputs:
- layer_out: bfloat16 [16384, 768], P(('dp', 'tensor'))
- grad_input: bfloat16 [16384, 768], P(('dp', 'tensor'))
- grad_mask_embed: float32 [768], replicated
- grad_w_query: float32 [768, 768], P(None, 'tensor')
- grad_b_query: float32 [768], P('tensor')
- grad_w_key: float32 [768, 768], P(None, 'tensor')
- grad_w_value: float32 [768, 768], P(None, 'tensor')
- grad_b_value: float32 [768], P('tensor')
- grad_w_out: float32 [768, 768], P('tensor')
- grad_b_out: float32 [768], replicated
- grad_g_attn: float32 [768], replicated
- grad_s_attn: float32 [768], replicated
- grad_w_in: float32 [768, 3072], P(None, 'tensor')
- grad_b_in: float32 [3072], P('tensor')
- grad_w_back: float32 [3072, 768], P('tensor')
- grad_b_back: float32 [768], replicated
- grad_g_ffn: float32 [768], replicated
- grad_s_ffn: float32 [768], replicated
The draws below stay inside these ranges and needn't reach their ends.
Inputs may be any that keep to these rules, and one draw needn't show every extreme that they name: `lengths`: real residues of each chain; one chain of the whole batch has all 128 positions real, and every chain's masked span lies within its real residues.
All inputs are finite; a program needn't handle non-finite values.
Results may differ from the reference program's by a relative error of at most 0.02.
Values may be sent and summed in bfloat16 or wider, within the bound.
No kernel may reach another device: no remote copies, remote signals or barrier semaphores. Data moves between devices by JAX's collectives and lax.ppermute only.
A program may use at most 128 MiB of HBM per device.

```python
import jax
import jax.numpy as jnp
from jax import lax

D = 768
FF = 3072
HEADS = 12
HEAD_DIM = 64
SEQ = 128
CHAIN_BLOCK = 4
CH = 16
CHAINS = 128
TOKENS = 16384


def draw_lengths(key, part):
    key = jax.random.fold_in(key, 11)
    length_key, choose_key = jax.random.split(key)
    drawn = jax.random.randint(length_key, (CHAINS,), SEQ * 3 // 4, SEQ + 1)
    chosen = jax.random.randint(choose_key, (), 0, CHAINS)
    return jnp.where(jnp.arange(CHAINS) == chosen, SEQ, drawn).astype(jnp.int32)


def touch_ends(values, key, least, largest):
    longest = values.shape.index(max(values.shape))
    spots = []
    for shift in (0, 1):
        where = [jax.random.randint(jax.random.fold_in(key, axis), (), 0, length) for axis, length in enumerate(values.shape)]
        where[longest] = (where[longest] + shift) % values.shape[longest]
        spots.append(tuple(where))
    return values.at[spots[0]].set(least).at[spots[1]].set(largest)


def block_scale(key, extent, cuts, smallest, top_value):
    def one(dim, parts):
        draws = jax.random.uniform(jax.random.fold_in(jax.random.fold_in(key, 6), dim), (parts,), jnp.float32, smallest / len(cuts), top_value / len(cuts))
        return jnp.repeat(jnp.exp(draws), extent[dim] // parts).reshape((-1,) + (1,) * (len(extent) - dim - 1))

    level = one(*cuts[0])
    for cut in cuts[1:]:
        level = level * one(*cut)
    return level


def gaussian(stream_key, extent, spread, most, cuts=(), kind=jnp.bfloat16):
    level = block_scale(stream_key, extent, cuts, -0.22, 0.18) if cuts else 1.0
    values = jax.random.normal(stream_key, extent, jnp.float32) * spread * level
    return jnp.minimum(jnp.maximum(values, -most), most).astype(kind)


def setup_inputs(seed: int = 0) -> dict:
    arg_keys = jax.random.split(jax.random.key(seed), 22)
    return {
        "hidden_in": gaussian(arg_keys[0], (TOKENS, D), 1.0, 6.0, ((0, 32),)),
        "lengths": draw_lengths(jax.random.fold_in(arg_keys[21], 71), 0),
        "span_start": touch_ends(jax.random.randint(arg_keys[2], (CHAINS,), 1, SEQ // 2), jax.random.fold_in(arg_keys[2], 1), 1, (SEQ // 2) - 1).astype(jnp.int32),
        "span_len": touch_ends(jax.random.randint(arg_keys[3], (CHAINS,), 2, SEQ // 8 + 2), jax.random.fold_in(arg_keys[3], 1), 2, (SEQ // 8 + 2) - 1).astype(jnp.int32),
        "mask_embed": gaussian(arg_keys[4], (D,), 1.0, 6.0),
        "w_query": gaussian(arg_keys[5], (D, D), D ** -0.5, 0.21875, ((1, 4),)),
        "b_query": gaussian(arg_keys[6], (D,), 0.5, 3.0, ((0, 4),)),
        "w_key": gaussian(arg_keys[7], (D, D), D ** -0.5, 0.21875, ((1, 4),)),
        "w_value": gaussian(arg_keys[8], (D, D), D ** -0.5, 0.21875, ((1, 4),)),
        "b_value": gaussian(arg_keys[9], (D,), 0.5, 3.0, ((0, 4),)),
        "w_out": gaussian(arg_keys[10], (D, D), (D // 32) ** -0.5, 1.25, ((0, 4),)),
        "b_out": gaussian(arg_keys[11], (D,), 0.5, 3.0),
        "g_attn": jnp.clip(1.0 + 0.15 * jax.random.normal(arg_keys[12], (D,), jnp.float32), 0.25, 1.75).astype(jnp.bfloat16),
        "s_attn": gaussian(arg_keys[13], (D,), 0.3, 2.0),
        "w_in": gaussian(arg_keys[14], (D, FF), D ** -0.5, 0.21875, ((1, 4),)),
        "b_in": gaussian(arg_keys[15], (FF,), 0.5, 3.0, ((0, 4),)),
        "w_back": gaussian(arg_keys[16], (FF, D), (FF // 2) ** -0.5, 0.15625, ((0, 4),)),
        "b_back": gaussian(arg_keys[17], (D,), 0.5, 3.0),
        "g_ffn": jnp.clip(1.0 + 0.15 * jax.random.normal(arg_keys[18], (D,), jnp.float32), 0.25, 1.75).astype(jnp.bfloat16),
        "s_ffn": gaussian(arg_keys[19], (D,), 0.3, 2.0),
        "cotangent": gaussian(arg_keys[20], (TOKENS, D), 1.0, 6.0, ((0, 32),)),
    }


@jax.custom_vjp
def low(v):
    return lax.optimization_barrier(v.astype(jnp.bfloat16)).astype(jnp.float32)

@jax.custom_vjp
def low_back(v):
    return v

def low_keep(v):
    return (low(v), None)

def low_pass(kept, grad):
    return (grad,)

def back_keep(v):
    return (v, None)

def back_low(kept, grad):
    return (low(grad),)
low.defvjp(low_keep, low_pass)
low_back.defvjp(back_keep, back_low)
EPSILON = 1e-05
MASKED = -1000000000.0

def product_hi(left, right):
    return jnp.dot(left, right, precision=lax.Precision.HIGHEST)

def layer_norm(values, scale_vec, shift_vec):
    row_mean = lax.optimization_barrier(jnp.mean(values, axis=-1, keepdims=True))
    centred = values - row_mean
    row_var = lax.optimization_barrier(jnp.mean(centred * centred, axis=-1, keepdims=True))
    return centred * lax.rsqrt(row_var + EPSILON) * scale_vec + shift_vec

def attend(block_in):
    queries, key_vecs, value_vecs, visible = block_in
    scores = jnp.einsum('cqhd,ckhd->chqk', queries, key_vecs, precision=lax.Precision.HIGHEST) * HEAD_DIM ** (-0.5)
    scores = low_back(scores)
    scores = jnp.where(visible[:, None, None, :], scores, MASKED)
    row_max = lax.optimization_barrier(jnp.max(scores, axis=-1, keepdims=True))
    shifted = jnp.exp(scores - row_max)
    probabilities = low(shifted / lax.optimization_barrier(jnp.sum(shifted, axis=-1, keepdims=True)))
    return jnp.einsum('chqk,ckhd->cqhd', probabilities, value_vecs, precision=lax.Precision.HIGHEST)

def reference(hidden_in, lengths, span_start, span_len, mask_embed, w_query, b_query, w_key, w_value, b_value, w_out, b_out, g_attn, s_attn, w_in, b_in, w_back, b_back, g_ffn, s_ffn, cotangent):
    position = jnp.arange(SEQ, dtype=jnp.int32)
    visible = position[None, :] < lengths[:, None]
    span_end = span_start + span_len
    in_span = ((position[None, :] >= span_start[:, None]) & (position[None, :] < span_end[:, None])).reshape(TOKENS)
    block_chains = min(CHAIN_BLOCK, CH)
    block_count = CHAINS // block_chains
    visible_blocks = visible.reshape(block_count, block_chains, SEQ)
    shape_five = (block_count, block_chains, SEQ, HEADS, HEAD_DIM)

    def forward(layer_in, embed_vec, query_mat, query_bias, key_mat, value_mat, value_bias, out_mat, out_bias, attn_gain, attn_shift, in_mat, in_bias, back_mat, back_bias, ffn_gain, ffn_shift):
        mixed_in = jnp.where(in_span[:, None], embed_vec[None, :], layer_in)
        queries = low_back(low(product_hi(mixed_in, query_mat) + query_bias))
        key_vecs = low_back(low(product_hi(mixed_in, key_mat)))
        value_vecs = low_back(low(product_hi(mixed_in, value_mat) + value_bias))
        context = lax.map(jax.checkpoint(attend), (queries.reshape(shape_five), key_vecs.reshape(shape_five), value_vecs.reshape(shape_five), visible_blocks))
        context = low_back(low(context.reshape(TOKENS, D)))
        first_sum = mixed_in + low_back(product_hi(context, out_mat)) + out_bias
        normed = layer_norm(first_sum, attn_gain, attn_shift)
        pre_act = low_back(product_hi(low(normed), in_mat) + in_bias)
        activated = low(jax.nn.gelu(pre_act, approximate=False))
        second_sum = normed + low_back(product_hi(activated, back_mat)) + back_bias
        return low(layer_norm(second_sum, ffn_gain, ffn_shift))
    floats = [array_in.astype(jnp.float32) for array_in in (hidden_in, mask_embed, w_query, b_query, w_key, w_value, b_value, w_out, b_out, g_attn, s_attn, w_in, b_in, w_back, b_back, g_ffn, s_ffn)]
    layer_out, pullback = jax.vjp(forward, *floats)
    gradients = pullback(cotangent.astype(jnp.float32))
    return (layer_out.astype(jnp.bfloat16), gradients[0].astype(jnp.bfloat16), gradients[1], gradients[2], gradients[3], gradients[4], gradients[5], gradients[6], gradients[7], gradients[8], gradients[9], gradients[10], gradients[11], gradients[12], gradients[13], gradients[14], gradients[15], gradients[16])
```

```python
import functools

import jax
import jax.numpy as jnp
from jax import lax
from jax.experimental import pallas as pl
from jax.experimental.pallas import tpu as pltpu
from jax.sharding import PartitionSpec as P

HEAD_DIM = 64
EPSILON = 1e-05
MASKED = -1000000000.0
AXES = ("dp", "tensor")
BF = jnp.bfloat16
F32 = jnp.float32
MIB = 1024 * 1024
BIAS_ROWS = 16


class Moves:
    def __init__(self, dp_size, group):
        self.dp_size, self.group = dp_size, group

    def build(self, source):
        pairs = []
        for d in range(self.dp_size):
            for t in range(self.group):
                sd, st = source(d, t)
                pairs.append((sd * self.group + st, d * self.group + t))
        return lambda value: lax.ppermute(value, AXES, pairs)

    def core(self, value):
        return self.build(lambda d, t: (d ^ 1, t))(value)

    def near(self, value):
        return self.build(lambda d, t: (d ^ (4 if d & 1 else 2), t))(value)

    def far(self, value):
        return self.build(lambda d, t: (d ^ (2 if d & 1 else 4), t))(value)

    def fetch(self, value, turn):
        return self.build(lambda d, t: (d, (t + turn) % self.group))(value)

    def give(self, value, turn):
        return self.build(lambda d, t: (d, (t - turn) % self.group))(value)

    def flip(self, value, mask_dp, mask_t):
        return self.build(lambda d, t: (d ^ mask_dp, t ^ mask_t))(value)


def spread(moves, mine):
    rows = mine.shape[0]
    other = moves.core(mine)
    near = moves.near(jnp.concatenate((mine, other), axis=0))
    far = moves.far(near[:rows])
    near_other = moves.core(near)
    far_other = moves.core(far)
    return (mine, other, near, near_other, far, far_other)


def gather_places(core, chip):
    near, over = chip ^ (1 + core), chip ^ (2 - core)
    return (
        (0, 0, core, chip),
        (1, 0, 1 - core, chip),
        (2, 0, core, near),
        (2, 1, 1 - core, near),
        (3, 0, 1 - core, over),
        (3, 1, core, over),
        (4, 0, core, chip ^ 3),
        (5, 0, 1 - core, chip ^ 3),
    )


def low_sum(*values):
    total = values[0].astype(F32)
    for value in values[1:]:
        total = total + value.astype(F32)
    return total.astype(BF)


def reduce_plane(moves, core, kept, given, more=None):
    rows = kept.shape[0] // 4
    come = moves.core(given)
    total = low_sum(kept, come) if more is None else low_sum(kept, come, more)
    diagonal = moves.far(total[2 * rows : 3 * rows])
    slots = lax.broadcasted_iota(jnp.int32, (2, 1, 1), 0)
    added = jnp.where(slots == core, diagonal.astype(F32)[None], 0.0)
    pair = (total[: 2 * rows].reshape(2, rows, -1).astype(F32) + added).astype(BF)
    come = moves.near(pair.reshape(2 * rows, -1))
    over = moves.core(lax.dynamic_slice_in_dim(come, (1 - core) * rows, rows))
    return low_sum(total[3 * rows :], lax.dynamic_slice_in_dim(come, core * rows, rows), over)


def dot_nn(left, right):
    return jnp.dot(left, right, preferred_element_type=F32)


def dot_nt(left, right):
    return lax.dot_general(left, right, (((1,), (1,)), ((), ())), preferred_element_type=F32)


def dot_tn(left, right):
    return lax.dot_general(left, right, (((0,), (0,)), ((), ())), preferred_element_type=F32)


def row_sum(values):
    return jnp.sum(values, axis=0, keepdims=True)


def copy_in(core, chip, refs, rows, turns, out_ref, sems, place):
    started = []
    for turn in range(turns):
        mine = []
        for index, (array, half, part, where) in enumerate(gather_places(core, chip)):
            ref = refs[array]
            start = (half * turns + turn) * rows
            copy = pltpu.make_async_copy(
                ref.at[pl.ds(start, rows)],
                out_ref.at[pl.ds(pl.multiple_of(place(turn, part, where), rows), rows)],
                sems.at[turn * 8 + index],
            )
            copy.start()
            mine.append(copy)
        started.append(mine)
    return started


def attn_place(rows):
    return lambda turn, part, where: turn * 8 * rows + (2 * where + part) * rows


def ffn_place(rows):
    return lambda turn, part, where: ((turn * 2 + part) * 4 + where) * rows


def scatter_out(core, chip, source_ref, rows, turns, turn, kept_ref, given_ref, place):
    for ref, mine in ((kept_ref, core), (given_ref, 1 - core)):
        near = chip ^ (1 + mine)
        slots = ((0, near), (1, near), (mine, chip ^ 3), (mine, chip))
        for slot, (part, where) in enumerate(slots):
            start = pl.multiple_of(place(0, part, where), rows)
            ref[(slot * turns + turn) * rows : (slot * turns + turn + 1) * rows, :] = source_ref[
                pl.ds(start, rows), :
            ]


def attend(width, scal_ref, mixed, mat, bias, qkv_ref, soft_ref, ctx_ref, seq):
    chains = mixed.shape[0] // seq
    heads = width // HEAD_DIM
    projected = dot_nn(mixed, mat[:, : 3 * width])
    qkv_ref[:, :width] = (projected[:, :width] + bias[:, :width]).astype(BF)
    qkv_ref[:, width : 2 * width] = projected[:, width : 2 * width].astype(BF)
    qkv_ref[:, 2 * width :] = (projected[:, 2 * width :] + bias[:, width : 2 * width]).astype(BF)
    column = lax.broadcasted_iota(jnp.int32, (1, seq), 1)
    for chain in range(chains):
        seen = column < scal_ref[2 + chain]
        rows = slice(chain * seq, (chain + 1) * seq)
        for head in range(heads):
            cut = slice(head * HEAD_DIM, (head + 1) * HEAD_DIM)
            queries = qkv_ref[rows, cut]
            keys = qkv_ref[rows, width + cut.start : width + cut.stop]
            values = qkv_ref[rows, 2 * width + cut.start : 2 * width + cut.stop]
            scores = dot_nt(queries, keys) * (HEAD_DIM**-0.5)
            scores = jnp.where(seen, scores, MASKED)
            shifted = jnp.exp(scores - jnp.max(scores, axis=1, keepdims=True))
            weights = (shifted / jnp.sum(shifted, axis=1, keepdims=True)).astype(BF)
            soft_ref[chain * heads + head] = weights
            ctx_ref[rows, cut] = dot_nn(weights, values).astype(BF)
    return dot_nt(ctx_ref[...], mat[:, 3 * width :])


def norm_back(grad, hat, inv, gain):
    scaled = grad * gain
    mean_one = jnp.mean(scaled, axis=1, keepdims=True)
    mean_two = jnp.mean(scaled * hat, axis=1, keepdims=True)
    return inv * (scaled - mean_one - hat * mean_two)


def norm_parts(values):
    centred = values - jnp.mean(values, axis=1, keepdims=True)
    inv = lax.rsqrt(jnp.mean(centred * centred, axis=1, keepdims=True) + EPSILON)
    return centred * inv, inv


def in_span(scal_ref, chain, chains, seq):
    position = lax.broadcasted_iota(jnp.int32, (seq, 1), 0)
    start = scal_ref[2 + chains + chain]
    return (position >= start) & (position < start + scal_ref[2 + 2 * chains + chain])


def attn_own_kernel(width, seq, scal, hidden, embed, mat, bias, mixed, qkv, soft, ctx, part):
    chains = hidden.shape[0] // seq
    for chain in range(chains):
        rows = slice(chain * seq, (chain + 1) * seq)
        mixed[rows, :] = jnp.where(in_span(scal, chain, chains, seq), embed[...], hidden[rows, :])
    part[...] = attend(
        width, scal, mixed[...], mat[...], bias[1:2, :].astype(F32), qkv, soft, ctx, seq
    )


def attn_rest_kernel(
    width, seq, turns, part_rows, scal, mixed, part, b_out, gain, shift, *refs
):
    firsts, refs = refs[:turns], refs[turns:]
    pieces, refs = refs[:6], refs[6:]
    qkvs, refs = refs[:turns], refs[turns:]
    softs, refs = refs[:turns], refs[turns:]
    ctxs, refs = refs[:turns], refs[turns:]
    hat, inv, normed, bias_in, mats, sems = refs
    core, chip = scal[0], scal[1]
    copies = copy_in(core, chip, pieces, part_rows, turns, mats, sems, attn_place(part_rows))
    total = part[...] + mixed[...].astype(F32) + b_out[...].astype(F32)
    height = 8 * part_rows
    for turn in range(turns):
        for copy in copies[turn]:
            copy.wait()
        bias_in[turn * 8 : turn * 8 + 8, :] = jnp.broadcast_to(
            firsts[turn][part_rows : part_rows + 1, :].astype(F32), (8, bias_in.shape[1])
        )
        total = total + attend(
            width,
            scal,
            mixed[...],
            mats[turn * height : (turn + 1) * height, :],
            firsts[turn][part_rows + 1 : part_rows + 2, :].astype(F32),
            qkvs[turn],
            softs[turn],
            ctxs[turn],
            seq,
        )
    ahat, ainv = norm_parts(total)
    hat[...] = ahat
    inv[...] = jnp.broadcast_to(ainv, inv.shape)
    normed[...] = (ahat * gain[...].astype(F32) + shift[...].astype(F32)).astype(BF)


def gelu_both(pre):
    cdf = 0.5 * (1.0 + lax.erf(pre * (0.5**0.5)))
    pdf = jnp.exp(-0.5 * pre * pre) * (0.5 / 3.141592653589793) ** 0.5
    return pre * cdf, cdf + pre * pdf


def ffn_step(normed, mat_in, mat_back, bias, act, slope):
    pre = dot_nn(normed[...], mat_in) + bias
    value, rate = gelu_both(pre)
    act[...] = value.astype(BF)
    slope[...] = rate.astype(BF)
    return dot_nn(act[...], mat_back)


def ffn_own_kernel(normed, mat_in, mat_back, bias, act, slope, total):
    total[...] = ffn_step(
        normed, mat_in[...], mat_back[...], bias[0:1, :].astype(F32), act, slope
    )


def ffn_rest_kernel(turns, part_rows, bias_rows, last, scal, normed, part, bias_in, *refs):
    if last:
        (hat1, gain1, shift1, b_back, gain2, shift2, cot), refs = refs[:7], refs[7:]
    pieces, refs = refs[:6], refs[6:]
    acts, refs = refs[:turns], refs[turns:]
    slopes, refs = refs[:turns], refs[turns:]
    if last:
        layer_out, grad_second, grad_low, small, mats, sems = refs
    else:
        total, mats, sems = refs
    core, chip = scal[0], scal[1]
    copies = copy_in(core, chip, pieces, part_rows, turns, mats, sems, ffn_place(part_rows))
    height = 4 * part_rows
    value = part[...]
    for turn in range(turns):
        for copy in copies[turn]:
            copy.wait()
        base = turn * 2 * height
        value = value + ffn_step(
            normed,
            mats[base : base + height, :],
            mats[base + height : base + 2 * height, :],
            bias_in[bias_rows[turn] * 8 : bias_rows[turn] * 8 + 1, :],
            acts[turn],
            slopes[turn],
        )
    if not last:
        total[...] = value
        return
    first = hat1[...] * gain1[...].astype(F32) + shift1[...].astype(F32)
    hat, inv = norm_parts(first + value + b_back[...].astype(F32))
    gain = gain2[...].astype(F32)
    layer_out[...] = (hat * gain + shift2[...].astype(F32)).astype(BF)
    grad = cot[...].astype(F32)
    back = norm_back(grad, hat, inv, gain)
    grad_second[...] = back
    grad_low[...] = back.astype(BF)
    small[0:1, :] = row_sum(grad * hat)
    small[1:2, :] = row_sum(grad)
    small[2:3, :] = row_sum(back)
    small[3:, :] = jnp.zeros_like(small[3:, :])


def ffn_back_kernel(turns, own, part_rows, scal, grad_low, normed, part, *refs):
    acts, refs = refs[:turns], refs[turns:]
    slopes, refs = refs[:turns], refs[turns:]
    count = 2 if own else 6
    pieces, refs = refs[:count], refs[count:]
    kept, given, total, bias_grad, whole = refs[:5]
    core, chip = scal[0], scal[1]
    if not own:
        mats, sems = refs[5:]
        copies = copy_in(core, chip, pieces, part_rows, turns, mats, sems, ffn_place(part_rows))
    height = 4 * part_rows
    value = part[...]
    bias_grad[...] = jnp.zeros_like(bias_grad)
    for turn in range(turns):
        whole[height:, :] = dot_tn(acts[turn][...], grad_low[...]).astype(BF)
        if own:
            mat_in, mat_back = pieces[0][...], pieces[1][...]
        else:
            for copy in copies[turn]:
                copy.wait()
            base = turn * 2 * height
            mat_in = mats[base : base + height, :]
            mat_back = mats[base + height : base + 2 * height, :]
        grad_act = dot_nt(grad_low[...], mat_back)
        grad_pre = (grad_act * slopes[turn][...].astype(F32)).astype(BF)
        bias_grad[turn : turn + 1, :] = row_sum(grad_pre.astype(F32))
        whole[:height, :] = dot_tn(normed[...], grad_pre).astype(BF)
        value = value + dot_nt(grad_pre, mat_in)
        scatter_out(
            core, chip, whole, part_rows, turns, turn, kept, given, ffn_place(part_rows)
        )
    total[...] = value


def attend_back(width, seq, grad_low, mat, mixed, qkv, soft, ctx, grad_qkv, whole):
    chains = grad_low.shape[0] // seq
    heads = width // HEAD_DIM
    scale = HEAD_DIM**-0.5
    whole[:, 3 * width :] = dot_tn(grad_low, ctx[...]).astype(BF)
    grad_ctx = dot_nn(grad_low, mat[:, 3 * width :]).astype(BF)
    for chain in range(chains):
        rows = slice(chain * seq, (chain + 1) * seq)
        for head in range(heads):
            cut = slice(head * HEAD_DIM, (head + 1) * HEAD_DIM)
            key_cut = slice(width + cut.start, width + cut.stop)
            value_cut = slice(2 * width + cut.start, 2 * width + cut.stop)
            weights = soft[chain * heads + head]
            grad_out = grad_ctx[rows, cut]
            grad_weights = dot_nt(grad_out, qkv[rows, value_cut])
            wide = weights.astype(F32)
            row_dot = jnp.sum(wide * grad_weights, axis=1, keepdims=True)
            grad_scores = (wide * (grad_weights - row_dot)).astype(BF)
            grad_qkv[rows, cut] = (dot_nn(grad_scores, qkv[rows, key_cut]) * scale).astype(BF)
            grad_qkv[rows, key_cut] = (dot_tn(grad_scores, qkv[rows, cut]) * scale).astype(BF)
            grad_qkv[rows, value_cut] = dot_tn(weights, grad_out).astype(BF)
    whole[:, : 3 * width] = dot_tn(mixed, grad_qkv[...]).astype(BF)
    sums = row_sum(grad_qkv[...].astype(F32))
    return dot_nt(grad_qkv[...], mat[:, : 3 * width]), sums


def attn_back_kernel(width, seq, turns, first, part_rows, scal, mixed, part, *refs):
    if first:
        (hat, inv, gain), refs = refs[:3], refs[3:]
    else:
        (grad_low_in,), refs = refs[:1], refs[1:]
    qkvs, refs = refs[:turns], refs[turns:]
    softs, refs = refs[:turns], refs[turns:]
    ctxs, refs = refs[:turns], refs[turns:]
    count = 6 if first else 1
    pieces, refs = refs[:count], refs[count:]
    kept, given, total, bias_grad = refs[:4]
    refs = refs[4:]
    core, chip = scal[0], scal[1]
    if first:
        grad_low, small, grad_qkv, whole, mats, sems = refs
        copies = copy_in(core, chip, pieces, part_rows, turns, mats, sems, attn_place(part_rows))
        grad = part[...]
        value = norm_back(grad, hat[...], inv[:, :1], gain[...].astype(F32))
        grad_low[...] = value.astype(BF)
        small[0:1, :] = row_sum(grad * hat[...])
        small[1:2, :] = row_sum(grad)
        small[2:3, :] = row_sum(value)
        small[3:, :] = jnp.zeros_like(small[3:, :])
    else:
        grad_low = grad_low_in
        grad_qkv, whole = refs
        value = part[...]
    height = 8 * part_rows
    bias_grad[...] = jnp.zeros_like(bias_grad)
    for turn in range(turns):
        if first:
            for copy in copies[turn]:
                copy.wait()
            mat = mats[turn * height : (turn + 1) * height, :]
        else:
            mat = pieces[0][...]
        back, sums = attend_back(
            width,
            seq,
            grad_low[...],
            mat,
            mixed[...],
            qkvs[turn],
            softs[turn],
            ctxs[turn],
            grad_qkv,
            whole,
        )
        value = value + back
        bias_grad[turn : turn + 1, :width] = sums[:, :width]
        bias_grad[turn : turn + 1, width : 2 * width] = sums[:, 2 * width :]
        scatter_out(
            core, chip, whole, part_rows, turns, turn, kept, given, attn_place(part_rows)
        )
    if first:
        total[...] = value
        return
    chains = value.shape[0] // seq
    embed_sum = jnp.zeros((1, value.shape[1]), F32)
    for chain in range(chains):
        rows = slice(chain * seq, (chain + 1) * seq)
        span = in_span(scal, chain, chains, seq)
        total[rows, :] = jnp.where(span, 0.0, value[rows, :]).astype(BF)
        embed_sum = embed_sum + row_sum(jnp.where(span, value[rows, :], 0.0))
    bias_grad[turns : turns + 1, :] = embed_sum


def ffn_out_kernel(part_rows, scal, *refs):
    pieces, outs = refs[:6], refs[6:]
    for array, half, part, where in gather_places(scal[0], scal[1]):
        block = pieces[array][half * part_rows : (half + 1) * part_rows, :].astype(F32)
        start = pl.multiple_of(where * part_rows, part_rows)
        for index in range(2):
            @pl.when(part == index)
            def _():
                outs[index][pl.ds(start, part_rows), :] = block


def attn_out_kernel(width, part_rows, scal, *refs):
    pieces, outs, whole = refs[:6], refs[6:10], refs[10]
    for array, half, part, where in gather_places(scal[0], scal[1]):
        block = pieces[array][half * part_rows : (half + 1) * part_rows, :]
        start = pl.multiple_of((2 * where + part) * part_rows, part_rows)
        whole[pl.ds(start, part_rows), :] = block.astype(F32)
    for index in range(3):
        outs[index][...] = whole[:, index * width : (index + 1) * width]
    outs[3][...] = whole[:, 3 * width :].T


SMEM = pl.BlockSpec(memory_space=pltpu.SMEM)
VMEM = pl.BlockSpec(memory_space=pltpu.VMEM)
ANY = pl.BlockSpec(memory_space=pl.ANY)


def call(kernel, ins, outs, scratch=(), flops=0, vmem=40, name=None):
    arrays = [array for array, _ in ins]
    moved = sum(a.size * a.dtype.itemsize for a in arrays) + sum(
        o.size * o.dtype.itemsize for o in outs
    )
    return pl.pallas_call(
        kernel,
        in_specs=[spec for _, spec in ins],
        out_specs=[VMEM] * len(outs),
        out_shape=list(outs),
        scratch_shapes=list(scratch),
        compiler_params=pltpu.CompilerParams(vmem_limit_bytes=vmem * MIB),
        cost_estimate=pl.CostEstimate(flops=flops, bytes_accessed=moved, transcendentals=0),
        name=name,
    )(*arrays)


def shape(rows, columns, kind=F32):
    return jax.ShapeDtypeStruct((rows, columns), kind)


def on_device(
    hidden_in,
    lengths,
    span_start,
    span_len,
    mask_embed,
    w_query,
    b_query,
    w_key,
    w_value,
    b_value,
    w_out,
    b_out,
    g_attn,
    s_attn,
    w_in,
    b_in,
    w_back,
    b_back,
    g_ffn,
    s_ffn,
    cotangent,
):
    group = lax.axis_size("tensor")
    dp_size = lax.axis_size("dp")
    moves = Moves(dp_size, group)
    dp = lax.axis_index("dp")
    rank = lax.axis_index("tensor")
    core, chip = dp & 1, (dp >> 1) & 3
    rows, model = hidden_in.shape
    seq = rows * group // lengths.shape[0]
    chains = rows // seq
    width = w_query.shape[1]
    heads = width // HEAD_DIM
    hidden = w_in.shape[1]
    piece = model // 4
    half = piece // 2
    turns = tuple(range(1, group))
    n_turns = len(turns)

    def local(values):
        return lax.dynamic_slice_in_dim(values, rank * chains, chains)

    scal = jnp.concatenate(
        (
            jnp.stack((core, chip)).astype(jnp.int32),
            local(lengths),
            local(span_start),
            local(span_len),
        )
    )
    row = lambda values: values.reshape(1, -1)

    own_attn = jnp.concatenate((w_query, w_key, w_value, w_out.T), axis=1)
    bias_pack = jnp.concatenate(
        (
            row(b_in),
            jnp.concatenate((row(b_query), row(b_value), jnp.zeros((1, model - 2 * width), BF)), axis=1),
            jnp.zeros((BIAS_ROWS - 2, model), BF),
        ),
        axis=0,
    )
    attn_mine = jnp.concatenate(
        (lax.dynamic_slice_in_dim(own_attn, chip * piece + core * half, half), bias_pack), axis=0
    )
    attn_firsts = [moves.fetch(attn_mine, turn) for turn in turns]
    attn_parts = spread(moves, jnp.concatenate([first[:half] for first in attn_firsts], axis=0))

    ffn_mine = jnp.where(
        core == 0,
        lax.dynamic_slice_in_dim(w_in, chip * piece, piece),
        lax.dynamic_slice_in_dim(w_back, chip * piece, piece),
    )
    chunk_one, chunk_two = (1, 3), (2,)
    ffn_one = spread(
        moves, jnp.concatenate([moves.fetch(ffn_mine, turn) for turn in chunk_one], axis=0)
    )
    ffn_two = spread(
        moves, jnp.concatenate([moves.fetch(ffn_mine, turn) for turn in chunk_two], axis=0)
    )

    dma = lambda count: pltpu.SemaphoreType.DMA((8 * count,))
    soft_shape = jax.ShapeDtypeStruct((chains * heads, seq, seq), BF)
    turn_flops = 2 * rows * model * 4 * width
    mixed, qkv_own, soft_own, ctx_own, attn_part = call(
        functools.partial(attn_own_kernel, width, seq),
        [(scal, SMEM), (hidden_in, VMEM), (row(mask_embed), VMEM), (own_attn, VMEM), (bias_pack, VMEM)],
        [shape(rows, model, BF), shape(rows, 3 * width, BF), soft_shape, shape(rows, width, BF), shape(rows, model)],
        flops=turn_flops,
        name="attn_own",
    )
    rest = call(
        functools.partial(attn_rest_kernel, width, seq, n_turns, half),
        [(scal, SMEM), (mixed, VMEM), (attn_part, VMEM), (row(b_out), VMEM), (row(g_attn), VMEM), (row(s_attn), VMEM)]
        + [(first, VMEM) for first in attn_firsts]
        + [(part, ANY) for part in attn_parts],
        [shape(rows, 3 * width, BF)] * n_turns
        + [soft_shape] * n_turns
        + [shape(rows, width, BF)] * n_turns
        + [shape(rows, model), shape(rows, 128), shape(rows, model, BF), shape(8 * n_turns, model)],
        [pltpu.VMEM((n_turns * model, model), BF), dma(n_turns)],
        flops=n_turns * turn_flops,
        name="attn_rest",
    )
    qkvs, softs, ctxs = rest[:n_turns], rest[n_turns : 2 * n_turns], rest[2 * n_turns : 3 * n_turns]
    hat1, inv1, normed, bias_in = rest[3 * n_turns :]

    ffn_flops = 2 * rows * model * hidden * 2
    act_own, slope_own, ffn_part = call(
        ffn_own_kernel,
        [(normed, VMEM), (w_in, VMEM), (w_back, VMEM), (bias_pack, VMEM)],
        [shape(rows, hidden, BF), shape(rows, hidden, BF), shape(rows, model)],
        flops=ffn_flops,
        name="ffn_own",
    )
    act_one1, act_one3, slope_one1, slope_one3, ffn_part = call(
        functools.partial(ffn_rest_kernel, 2, piece, (0, 2), False),
        [(scal, SMEM), (normed, VMEM), (ffn_part, VMEM), (bias_in, VMEM)] + [(part, ANY) for part in ffn_one],
        [shape(rows, hidden, BF)] * 4 + [shape(rows, model)],
        [pltpu.VMEM((4 * model, model), BF), dma(2)],
        flops=2 * ffn_flops,
        name="ffn_one",
    )
    act_two, slope_two, layer_out, grad_second, grad_low, small_ffn = call(
        functools.partial(ffn_rest_kernel, 1, piece, (1,), True),
        [(scal, SMEM), (normed, VMEM), (ffn_part, VMEM), (bias_in, VMEM), (hat1, VMEM)]
        + [(row(v), VMEM) for v in (g_attn, s_attn, b_back, g_ffn, s_ffn)]
        + [(cotangent, VMEM)]
        + [(part, ANY) for part in ffn_two],
        [shape(rows, hidden, BF)] * 2
        + [shape(rows, model, BF), shape(rows, model), shape(rows, model, BF), shape(8, model)],
        [pltpu.VMEM((2 * model, model), BF), dma(1)],
        flops=ffn_flops,
        name="ffn_two",
    )

    def ffn_back(count, acts, slopes, weights, part, own, name):
        scratch = [pltpu.VMEM((2 * model, model), BF)]
        if not own:
            scratch += [pltpu.VMEM((2 * count * model, model), BF), dma(count)]
        return call(
            functools.partial(ffn_back_kernel, count, own, piece),
            [(scal, SMEM), (grad_low, VMEM), (normed, VMEM), (part, VMEM)]
            + [(v, VMEM) for v in acts]
            + [(v, VMEM) for v in slopes]
            + [(v, VMEM if own else ANY) for v in weights],
            [shape(4 * count * piece, model, BF)] * 2 + [shape(rows, model), shape(8, model)],
            scratch,
            flops=2 * count * ffn_flops,
            name=name,
        )

    kept_two, given_two, grad_part, bias_two = ffn_back(
        1, (act_two,), (slope_two,), ffn_two, grad_second, False, "ffn_back_two"
    )
    kept_one, given_one, grad_part, bias_one = ffn_back(
        2, (act_one1, act_one3), (slope_one1, slope_one3), ffn_one, grad_part, False, "ffn_back_one"
    )
    kept_own, given_own, grad_part, bias_own = ffn_back(
        1, (act_own,), (slope_own,), (w_in, w_back), grad_part, True, "ffn_back_own"
    )
    done_two = moves.give(reduce_plane(moves, core, kept_two, given_two), 2)
    sums_one = reduce_plane(moves, core, kept_one, given_one)
    done_one = [
        moves.give(sums_one[index * piece : (index + 1) * piece], turn)
        for index, turn in enumerate(chunk_one)
    ]
    done_own = reduce_plane(moves, core, kept_own, given_own)
    ffn_final = low_sum(done_own, done_two, *done_one)

    back = call(
        functools.partial(attn_back_kernel, width, seq, n_turns, True, half),
        [(scal, SMEM), (mixed, VMEM), (grad_part, VMEM), (hat1, VMEM), (inv1, VMEM), (row(g_attn), VMEM)]
        + [(v, VMEM) for v in (*qkvs, *softs, *ctxs)]
        + [(part, ANY) for part in attn_parts],
        [shape(4 * n_turns * half, model, BF)] * 2
        + [shape(rows, model), shape(8, model), shape(rows, model, BF), shape(8, model)],
        [
            pltpu.VMEM((rows, 3 * width), BF),
            pltpu.VMEM((model, model), BF),
            pltpu.VMEM((n_turns * model, model), BF),
            dma(n_turns),
        ],
        flops=2 * n_turns * turn_flops,
        name="attn_back_rest",
    )
    kept_rest, given_rest, grad_mixed, bias_rest, attn_low, small_attn = back
    kept_mine, given_mine, grad_input, bias_mine = call(
        functools.partial(attn_back_kernel, width, seq, 1, False, half),
        [(scal, SMEM), (mixed, VMEM), (grad_mixed, VMEM), (attn_low, VMEM), (qkv_own, VMEM), (soft_own, VMEM), (ctx_own, VMEM), (own_attn, VMEM)],
        [shape(4 * half, model, BF)] * 2 + [shape(rows, model, BF), shape(8, model)],
        [pltpu.VMEM((rows, 3 * width), BF), pltpu.VMEM((model, model), BF)],
        flops=2 * turn_flops,
        name="attn_back_own",
    )
    sums_rest = reduce_plane(moves, core, kept_rest, given_rest)
    done_rest = [
        moves.give(sums_rest[index * half : (index + 1) * half], turn)
        for index, turn in enumerate(turns)
    ]
    done_mine = reduce_plane(moves, core, kept_mine, given_mine)
    attn_final = low_sum(done_mine, *done_rest)

    by_turn_ffn = jnp.concatenate((bias_own[:1], bias_one[:1], bias_two[:1], bias_one[1:2]), axis=0)
    by_turn_attn = jnp.concatenate((bias_mine[:1], bias_rest[:n_turns]), axis=0)
    small = jnp.concatenate(
        (
            small_ffn[:3],
            small_attn[:3],
            bias_mine[1:2],
            jnp.zeros((1, model), F32),
            jnp.roll(by_turn_ffn, rank, axis=0),
            jnp.roll(by_turn_attn, rank, axis=0),
        ),
        axis=0,
    )
    step = 1
    while step < dp_size:
        small = small + moves.flip(small, step, 0)
        step *= 2
    step = 1
    while step < group:
        small = small + moves.flip(small, 0, step)
        step *= 2

    if dp_size > 8:
        groups = [list(range(i, dp_size, 8)) for i in range(8)]
        ffn_final, attn_final = (
            lax.psum(v.astype(F32), "dp", axis_index_groups=groups).astype(BF)
            for v in (ffn_final, attn_final)
        )
    grad_w_in, grad_w_back = call(
        functools.partial(ffn_out_kernel, piece),
        [(scal, SMEM)] + [(part, VMEM) for part in spread(moves, ffn_final)],
        [shape(model, hidden), shape(hidden, model)],
        name="ffn_out",
    )
    grad_w_query, grad_w_key, grad_w_value, grad_w_out = call(
        functools.partial(attn_out_kernel, width, half),
        [(scal, SMEM)] + [(part, VMEM) for part in spread(moves, attn_final)],
        [shape(model, width)] * 3 + [shape(width, model)],
        [pltpu.VMEM((model, model), F32)],
        name="attn_out",
    )
    my_in = lax.dynamic_index_in_dim(small, 8 + rank, keepdims=False)
    my_attn = lax.dynamic_index_in_dim(small, 8 + group + rank, keepdims=False)
    return (
        layer_out,
        grad_input,
        small[6],
        grad_w_query,
        my_attn[:width],
        grad_w_key,
        grad_w_value,
        my_attn[width : 2 * width],
        grad_w_out,
        small[5],
        small[3],
        small[4],
        grad_w_in,
        my_in,
        grad_w_back,
        small[2],
        small[0],
        small[1],
    )


def solution(mesh):
    rows = P(("dp", "tensor"), None)
    placed = (
        rows,
        P("dp"),
        P("dp"),
        P("dp"),
        P(),
        P(None, "tensor"),
        P("tensor"),
        P(None, "tensor"),
        P(None, "tensor"),
        P("tensor"),
        P("tensor", None),
        P(),
        P(),
        P(),
        P(None, "tensor"),
        P("tensor"),
        P("tensor", None),
        P(),
        P(),
        P(),
        rows,
    )
    return jax.shard_map(
        on_device,
        mesh=mesh,
        in_specs=placed,
        out_specs=(
            rows,
            rows,
            P(),
            P(None, "tensor"),
            P("tensor"),
            P(None, "tensor"),
            P(None, "tensor"),
            P("tensor"),
            P("tensor", None),
            P(),
            P(),
            P(),
            P(None, "tensor"),
            P("tensor"),
            P("tensor", None),
            P(),
            P(),
            P(),
        ),
        check_vma=False,
    )
```

```python
import functools

import jax
import jax.numpy as jnp
from jax import lax
from jax.experimental import pallas as pl
from jax.experimental.pallas import tpu as pltpu
from jax.sharding import PartitionSpec as P

HEAD_DIM = 64
EPSILON = 1e-05
MASKED = -1000000000.0
AXES = ("dp", "tensor")
BF = jnp.bfloat16
F32 = jnp.float32
MIB = 1024 * 1024
BIAS_ROWS = 16


class Moves:
    def __init__(self, dp_size, group):
        self.dp_size, self.group = dp_size, group

    def build(self, value, source):
        pairs = []
        for d in range(self.dp_size):
            for t in range(self.group):
                sd, st = source(d, t)
                pairs.append((sd * self.group + st, d * self.group + t))
        return lax.ppermute(value, AXES, pairs)

    def core(self, value):
        return self.build(value, lambda d, t: (d ^ 1, t))

    def near(self, value):
        return self.build(value, lambda d, t: (d ^ (4 if d & 1 else 2), t))

    def far(self, value):
        return self.build(value, lambda d, t: (d ^ (2 if d & 1 else 4), t))

    def fetch(self, value, turn):
        return self.build(value, lambda d, t: (d, (t + turn) % self.group))

    def give(self, value, turn):
        return self.build(value, lambda d, t: (d, (t - turn) % self.group))

    def flip(self, value, mask_dp, mask_t):
        return self.build(value, lambda d, t: (d ^ mask_dp, t ^ mask_t))


def after(value, *first):
    return lax.optimization_barrier((value, *first))[0]


def over_rest(values, dp_size):
    groups = [list(range(i, dp_size, 8)) for i in range(8)]
    return lax.psum(values.astype(F32), "dp", axis_index_groups=groups).astype(BF)


def sync(*values):
    return lax.optimization_barrier(values)


def gather_places(core, chip):
    near, over = chip ^ (1 + core), chip ^ (2 - core)
    own = ((core, chip), (core, near), (core, over), (core, chip ^ 3))
    return own + ((1 - core, chip), (1 - core, over), (1 - core, near), (1 - core, chip ^ 3))


class Block:
    def __init__(self, array, row=0, rows=None):
        self.array, self.row = array, row
        self.rows = array.shape[0] - row if rows is None else rows

    def at(self, row, rows):
        return Block(self.array, self.row + row, rows)


class Refs:
    def __init__(self):
        self.arrays = []

    def add(self, block):
        for index, array in enumerate(self.arrays):
            if array is block.array:
                return index, block.row
        self.arrays.append(block.array)
        return len(self.arrays) - 1, block.row


def dot_nn(left, right):
    return jnp.dot(left, right, preferred_element_type=F32)


def dot_nt(left, right):
    return lax.dot_general(left, right, (((1,), (1,)), ((), ())), preferred_element_type=F32)


def dot_tn(left, right):
    return lax.dot_general(left, right, (((0,), (0,)), ((), ())), preferred_element_type=F32)


def row_sum(values):
    return jnp.sum(values, axis=0, keepdims=True)


def where_am_i():
    dp = lax.axis_index("dp")
    return dp & 1, (dp >> 1) & 3


def copy_in(refs, layout, rows, out_ref, sems, place):
    started = []
    for index, ((part, where), (array, row)) in enumerate(zip(gather_places(*where_am_i()), layout)):
        start = pl.multiple_of(place(part, where), rows)
        copy = pltpu.make_async_copy(
            refs[array].at[pl.ds(row, rows)], out_ref.at[pl.ds(start, rows)], sems.at[index]
        )
        copy.start()
        started.append(copy)
    return started


def attn_place(rows):
    return lambda part, where: (2 * where + part) * rows


def ffn_place(rows):
    return lambda part, where: (part * 4 + where) * rows


def scatter_out(source_ref, rows, kept_ref, given_ref, base, place):
    core, chip = where_am_i()
    for ref, mine, first in ((kept_ref, core, 0), (given_ref, 1 - core, base)):
        for slot, where in enumerate((chip ^ (1 + mine), chip ^ (2 - mine), chip ^ 3, chip)):
            start = pl.multiple_of(place(mine, where), rows)
            begin = first + slot * rows
            ref[begin : begin + rows, :] = source_ref[pl.ds(start, rows), :]


def block_of(values, chain, head, seq):
    return values[head * HEAD_DIM : (head + 1) * HEAD_DIM, chain * seq : (chain + 1) * seq]


def attend(width, seq, lengths, mixed, mats, bias, qkv, soft, ctx):
    chains = mixed.shape[0] // seq
    heads = width // HEAD_DIM
    base = lax.axis_index("tensor") * chains
    column = jnp.broadcast_to(bias, (8, bias.shape[1])).T[:, :1]
    scale = HEAD_DIM**-0.5
    parts = []
    for index in range(3):
        cut = slice(index * width, (index + 1) * width)
        values = dot_nt(mats[index], mixed)
        if index != 1:
            values = values + column[cut]
        parts.append(values.astype(BF))
    scaled = (parts[0].astype(F32) * scale).astype(BF)
    for index, values in enumerate((scaled, parts[1], parts[2])):
        qkv[index * width : (index + 1) * width, :] = values
    position = lax.broadcasted_iota(jnp.int32, (seq, 1), 0)
    blocks = [(chain, head) for chain in range(chains) for head in range(heads)]
    scores = [
        jnp.where(
            position < lengths[base + chain],
            dot_tn(block_of(parts[1], chain, head, seq), block_of(scaled, chain, head, seq)),
            MASKED,
        )
        for chain, head in blocks
    ]
    shifted = [jnp.exp(value - jnp.max(value, axis=0, keepdims=True)) for value in scores]
    weights = [(value * (1.0 / row_sum(value))).astype(BF) for value in shifted]
    for index, (chain, head) in enumerate(blocks):
        soft[index] = weights[index]
        ctx[head * HEAD_DIM : (head + 1) * HEAD_DIM, chain * seq : (chain + 1) * seq] = dot_nn(
            block_of(parts[2], chain, head, seq), weights[index]
        ).astype(BF)
    return dot_tn(ctx[...], mats[3])


def norm_back(grad, hat, inv, gain):
    scaled = grad * gain
    mean_one = jnp.mean(scaled, axis=1, keepdims=True)
    mean_two = jnp.mean(scaled * hat, axis=1, keepdims=True)
    return inv * (scaled - mean_one - hat * mean_two)


def norm_parts(values):
    centred = values - jnp.mean(values, axis=1, keepdims=True)
    inv = lax.rsqrt(jnp.mean(centred * centred, axis=1, keepdims=True) + EPSILON)
    return centred * inv, inv


def in_span(starts, counts, chain, chains, seq):
    index = lax.axis_index("tensor") * chains + chain
    position = lax.broadcasted_iota(jnp.int32, (seq, 1), 0)
    return (position >= starts[index]) & (position < starts[index] + counts[index])


EMBED, B_OUT, G_ATTN, S_ATTN, B_BACK, G_FFN, S_FFN = range(7)


def prep_kernel(half, piece, bias, wq, wk, wv, wo, w_in, w_back, attn_mine, ffn_mine, sems):
    core, chip = where_am_i()
    copies = [pltpu.make_async_copy(bias, attn_mine.at[pl.ds(half, BIAS_ROWS)], sems.at[0])]
    copies[0].start()
    for index, ref in enumerate((wq, wk, wv, wo)):
        start = pl.multiple_of(core * half, half)
        copy = pltpu.make_async_copy(
            ref.at[pl.ds(start, half)], attn_mine.at[pl.ds(0, half)], sems.at[1]
        )
        pl.when(chip == index)(copy.start)
    copies.append(copy)
    for index, ref in enumerate((w_in, w_back)):
        start = pl.multiple_of(chip * piece, piece)
        copy = pltpu.make_async_copy(ref.at[pl.ds(start, piece)], ffn_mine, sems.at[2])
        pl.when(core == index)(copy.start)
    copies.append(copy)
    for copy in copies:
        copy.wait()


def attn_own_kernel(
    width, seq, lengths, starts, counts, hidden, vecs, bias, wq, wk, wv, wo, mixed, qkv, soft, ctx, part
):
    chains = hidden.shape[0] // seq
    for chain in range(chains):
        rows = slice(chain * seq, (chain + 1) * seq)
        span = in_span(starts, counts, chain, chains, seq)
        mixed[rows, :] = jnp.where(span, vecs[EMBED : EMBED + 1, :], hidden[rows, :].astype(F32)).astype(BF)
    mats = (wq[...], wk[...], wv[...], wo[...])
    part[...] = attend(
        width, seq, lengths, mixed[...], mats, bias[1:2, :].astype(F32), qkv, soft, ctx
    )


def attn_mats(mats, width):
    return [mats[i * width : (i + 1) * width, :] for i in range(4)]


def attn_turn_kernel(
    width, seq, layout, last, part_rows, count, lengths, mixed, part, vecs, first, *refs
):
    pieces, refs = refs[:count], refs[count:]
    qkv, soft, ctx, bias_in, mats = refs[:5]
    sems = refs[-1]
    copies = copy_in(pieces, layout, part_rows, mats, sems, attn_place(part_rows))
    bias_in[...] = jnp.broadcast_to(first[part_rows : part_rows + 1, :].astype(F32), bias_in.shape)
    for copy in copies:
        copy.wait()
    bias = first[part_rows + 1 : part_rows + 2, :].astype(F32)
    total = part[...] + attend(
        width, seq, lengths, mixed[...], attn_mats(mats, width), bias, qkv, soft, ctx
    )
    if not last:
        refs[5][...] = total
        return
    hat, inv, normed = refs[5:8]
    ahat, ainv = norm_parts(total + mixed[...].astype(F32) + vecs[B_OUT : B_OUT + 1, :])
    hat[...] = ahat
    inv[...] = jnp.broadcast_to(ainv, inv.shape)
    normed[...] = (ahat * vecs[G_ATTN : G_ATTN + 1, :] + vecs[S_ATTN : S_ATTN + 1, :]).astype(BF)


def gelu_both(pre):
    cdf = 0.5 * (1.0 + lax.erf(pre * (0.5**0.5)))
    pdf = jnp.exp(-0.5 * pre * pre) * (0.5 / 3.141592653589793) ** 0.5
    return pre * cdf, cdf + pre * pdf


def ffn_step(normed, mat_in, mat_back, bias, act, slope):
    pre = dot_nn(normed[...], mat_in) + bias
    value, rate = gelu_both(pre)
    act[...] = value.astype(BF)
    slope[...] = rate.astype(BF)
    return dot_nn(act[...], mat_back)


def ffn_own_kernel(normed, mat_in, mat_back, bias, act, slope, total):
    total[...] = ffn_step(
        normed, mat_in[...], mat_back[...], bias[0:1, :].astype(F32), act, slope
    )


def ffn_rest_kernel(part_rows, layout, last, count, normed, part, bias_in, *refs):
    if last:
        (hat1, vecs, cot), refs = refs[:3], refs[3:]
    pieces, refs = refs[:count], refs[count:]
    act, slope, mats = refs[:3]
    sems = refs[-1]
    copies = copy_in(pieces, layout, part_rows, mats, sems, ffn_place(part_rows))
    height = 4 * part_rows
    for copy in copies:
        copy.wait()
    value = part[...] + ffn_step(
        normed, mats[:height, :], mats[height:, :], bias_in[0:1, :], act, slope
    )
    if not last:
        refs[3][...] = value
        return
    layer_out, grad_second, grad_low, small = refs[3:7]
    first = hat1[...] * vecs[G_ATTN : G_ATTN + 1, :] + vecs[S_ATTN : S_ATTN + 1, :]
    hat, inv = norm_parts(first + value + vecs[B_BACK : B_BACK + 1, :])
    gain = vecs[G_FFN : G_FFN + 1, :]
    layer_out[...] = (hat * gain + vecs[S_FFN : S_FFN + 1, :]).astype(BF)
    grad = cot[...].astype(F32)
    back = norm_back(grad, hat, inv, gain)
    grad_second[...] = back
    grad_low[...] = back.astype(BF)
    small[0:1, :] = row_sum(grad * hat)
    small[1:2, :] = row_sum(grad)
    small[2:3, :] = row_sum(back)
    small[3:, :] = jnp.zeros_like(small[3:, :])


def ffn_back_kernel(counts, part_rows, grad_low, normed, part, *refs):
    turns = []
    for count in counts:
        act, slope, *mats = refs[: 2 + count]
        refs = refs[2 + count :]
        turns.append((act, slope, mats))
    kepts, refs = refs[: len(turns)], refs[len(turns) :]
    given, total, bias_grad, whole = refs
    height = 4 * part_rows
    value = part[...]
    bias_grad[...] = jnp.zeros_like(bias_grad)
    for index, (act, slope, mats) in enumerate(turns):
        if len(mats) == 2:
            mat_in, mat_back = mats[0][...], mats[1][...]
        else:
            mat_in, mat_back = mats[0][:height, :], mats[0][height:, :]
        whole[height:, :] = dot_tn(act[...], grad_low[...]).astype(BF)
        grad_act = dot_nt(grad_low[...], mat_back)
        grad_pre = (grad_act * slope[...].astype(F32)).astype(BF)
        bias_grad[index : index + 1, :] = row_sum(grad_pre.astype(F32))
        whole[:height, :] = dot_tn(normed[...], grad_pre).astype(BF)
        value = value + dot_nt(grad_pre, mat_in)
        base = index * 4 * part_rows
        scatter_out(whole, part_rows, kepts[index], given, base, ffn_place(part_rows))
    total[...] = value


def attend_back(width, seq, grad_low, mats, mixed, qkv, soft, ctx, grad_qkv, whole):
    chains = grad_low.shape[0] // seq
    heads = width // HEAD_DIM
    scale = HEAD_DIM**-0.5
    whole[3 * width :, :] = dot_nn(ctx[...], grad_low).astype(BF)
    grad_ctx = dot_nt(mats[3], grad_low).astype(BF)
    queries, keys, values = (qkv[i * width : (i + 1) * width, :] for i in range(3))
    blocks = [(chain, head) for chain in range(chains) for head in range(heads)]
    grad_weights = [
        dot_tn(block_of(values, chain, head, seq), block_of(grad_ctx, chain, head, seq))
        for chain, head in blocks
    ]
    grad_scores = []
    for index, value in enumerate(grad_weights):
        wide = soft[index].astype(F32)
        product = wide * value
        grad_scores.append((product - wide * row_sum(product)).astype(BF))
    for index, (chain, head) in enumerate(blocks):
        columns = slice(chain * seq, (chain + 1) * seq)
        for slot, value in enumerate(
            (
                dot_nn(block_of(keys, chain, head, seq), grad_scores[index]) * scale,
                dot_nt(block_of(queries, chain, head, seq), grad_scores[index]),
                dot_nt(block_of(grad_ctx, chain, head, seq), soft[index]),
            )
        ):
            start = slot * width + head * HEAD_DIM
            grad_qkv[start : start + HEAD_DIM, columns] = value.astype(BF)
    whole[: 3 * width, :] = dot_nn(grad_qkv[...], mixed).astype(BF)
    ones = jnp.ones((8, grad_low.shape[0]), BF)
    back = dot_tn(grad_qkv[:width, :], mats[0])
    back = back + dot_tn(grad_qkv[width : 2 * width, :], mats[1])
    back = back + dot_tn(grad_qkv[2 * width :, :], mats[2])
    return back, dot_nt(ones, grad_qkv[...])


def attn_back_kernel(width, seq, own, first, part_rows, counts, mixed, part, *refs):
    if first:
        (hat, inv, vecs), refs = refs[:3], refs[3:]
    else:
        (grad_low,), refs = refs[:1], refs[1:]
    if own:
        (starts, counts_ref), refs = refs[:2], refs[2:]
    turns = []
    for count in counts:
        qkv, soft, ctx, *mats = refs[: 3 + count]
        refs = refs[3 + count :]
        turns.append((qkv, soft, ctx, mats))
    kepts, refs = refs[: len(turns)], refs[len(turns) :]
    given, total, bias_grad = refs[:3]
    refs = refs[3:]
    if first:
        (grad_low, small), refs = refs[:2], refs[2:]
    grad_qkv, whole = refs
    if first:
        grad = part[...]
        value = norm_back(grad, hat[...], inv[:, :1], vecs[G_ATTN : G_ATTN + 1, :])
        grad_low[...] = value.astype(BF)
        small[0:1, :] = row_sum(grad * hat[...])
        small[1:2, :] = row_sum(grad)
        small[2:3, :] = row_sum(value)
        small[3:, :] = jnp.zeros_like(small[3:, :])
    else:
        value = part[...]
    bias_grad[...] = jnp.zeros_like(bias_grad)
    for index, (qkv, soft, ctx, refs_in) in enumerate(turns):
        mats = [ref[...] for ref in refs_in] if len(refs_in) == 4 else attn_mats(refs_in[0], width)
        back, sums = attend_back(
            width, seq, grad_low[...], mats, mixed[...], qkv, soft, ctx, grad_qkv, whole
        )
        value = value + back
        bias_grad[index : index + 1, :width] = sums[0:1, :width]
        bias_grad[index : index + 1, width : 2 * width] = sums[0:1, 2 * width :]
        base = index * 4 * part_rows
        scatter_out(whole, part_rows, kepts[index], given, base, attn_place(part_rows))
    if not own:
        total[...] = value
        return
    chains = value.shape[0] // seq
    embed_sum = jnp.zeros((1, value.shape[1]), F32)
    for chain in range(chains):
        rows = slice(chain * seq, (chain + 1) * seq)
        span = in_span(starts, counts_ref, chain, chains, seq)
        total[rows, :] = jnp.where(span, 0.0, value[rows, :]).astype(BF)
        embed_sum = embed_sum + row_sum(jnp.where(span, value[rows, :], 0.0))
    bias_grad[1:2, :] = embed_sum


def mix_kernel(count, plan, *refs):
    for out, blocks in zip(refs[count:], plan):
        start = 0
        for rows, sources in blocks:
            array, row = sources[0]
            value = refs[array][row : row + rows, :]
            if len(sources) > 1:
                value = value.astype(F32)
                for array, row in sources[1:]:
                    value = value + refs[array][row : row + rows, :].astype(F32)
                value = value.astype(BF)
            out[start : start + rows, :] = value
            start += rows


def ffn_out_kernel(part_rows, layout, count, *refs):
    outs = refs[count:]
    for (array, row), (part, where) in zip(layout, gather_places(*where_am_i())):
        start = pl.multiple_of(where * part_rows, part_rows)
        for index in range(2):

            @pl.when(part == index)
            def _():
                block = refs[array][row : row + part_rows, :]
                outs[index][pl.ds(start, part_rows), :] = block.astype(F32)


def attn_out_kernel(part_rows, layout, count, *refs):
    outs = refs[count:]
    for (array, row), (part, where) in zip(layout, gather_places(*where_am_i())):
        start = pl.multiple_of(part * part_rows, part_rows)
        for index in range(4):

            @pl.when(where == index)
            def _():
                block = refs[array][row : row + part_rows, :]
                outs[index][pl.ds(start, part_rows), :] = block.astype(F32)


def small_kernel(group, rows_of, small_ffn, small_attn, *refs):
    out = refs[-1]
    rank = lax.axis_index("tensor")
    out[...] = jnp.zeros_like(out)
    out[0:3, :] = small_ffn[0:3, :]
    out[3:6, :] = small_attn[0:3, :]
    for index, (array, source) in enumerate(rows_of[:-1]):
        row = 8 + index // group * group + lax.rem(index % group + rank, group)
        out[pl.ds(row, 1), :] = refs[array][source : source + 1, :]
    array, source = rows_of[-1]
    out[6:7, :] = refs[array][source : source + 1, :]


SMEM = pl.BlockSpec(memory_space=pltpu.SMEM)
VMEM = pl.BlockSpec(memory_space=pltpu.VMEM)
ANY = pl.BlockSpec(memory_space=pl.ANY)


def call(kernel, ins, outs, scratch=(), flops=0, vmem=16, name=None):
    arrays = [array for array, _ in ins]
    moved = sum(a.size * a.dtype.itemsize for a in arrays) + sum(
        o.size * o.dtype.itemsize for o in outs
    )
    return pl.pallas_call(
        kernel,
        in_specs=[spec for _, spec in ins],
        out_specs=[VMEM] * len(outs),
        out_shape=list(outs),
        scratch_shapes=list(scratch),
        compiler_params=pltpu.CompilerParams(vmem_limit_bytes=vmem * MIB),
        cost_estimate=pl.CostEstimate(flops=flops // 100, bytes_accessed=moved // 100, transcendentals=0),
        name=name,
    )(*arrays)


def shape(rows, columns, kind=F32):
    return jax.ShapeDtypeStruct((rows, columns), kind)


def mix(*outs, name=None):
    refs, plan, shapes = Refs(), [], []
    for blocks in outs:
        mine = []
        for block in blocks:
            sources = block if isinstance(block, list) else [block]
            mine.append((sources[0].rows, tuple(refs.add(source) for source in sources)))
        plan.append(tuple(mine))
        first = blocks[0][0] if isinstance(blocks[0], list) else blocks[0]
        shapes.append(shape(sum(rows for rows, _ in mine), first.array.shape[1], BF))
    return call(
        functools.partial(mix_kernel, len(refs.arrays), tuple(plan)),
        [(array, VMEM) for array in refs.arrays],
        shapes,
        vmem=4,
        name=name,
    )


def on_device(
    hidden_in,
    lengths,
    span_start,
    span_len,
    mask_embed,
    w_query,
    b_query,
    w_key,
    w_value,
    b_value,
    w_out,
    b_out,
    g_attn,
    s_attn,
    w_in,
    b_in,
    w_back,
    b_back,
    g_ffn,
    s_ffn,
    cotangent,
):
    group = lax.axis_size("tensor")
    dp_size = lax.axis_size("dp")
    moves = Moves(dp_size, group)
    rank = lax.axis_index("tensor")
    rows, model = hidden_in.shape
    seq = rows * group // lengths.shape[0]
    chains = rows // seq
    width = w_query.shape[1]
    heads = width // HEAD_DIM
    hidden = w_in.shape[1]
    piece = model // 4
    half = piece // 2
    turns = (1, 3, 2)
    count = len(turns)

    vecs = jnp.stack(
        (mask_embed, b_out, g_attn, s_attn, b_back, g_ffn, s_ffn, jnp.zeros_like(b_out))
    ).astype(F32)
    none = jnp.zeros((width,), BF)
    bias_pack = jnp.pad(
        jnp.stack((b_in, jnp.concatenate((b_query, none, b_value, none)))),
        ((0, BIAS_ROWS - 2), (0, 0)),
    )
    own_mats = (w_query.T, w_key.T, w_value.T, w_out)
    dma = lambda n: pltpu.SemaphoreType.DMA((8 * n,))

    attn_mine, ffn_mine = call(
        functools.partial(prep_kernel, half, piece),
        [(v, ANY) for v in (bias_pack, *own_mats, w_in, w_back)],
        [shape(half + BIAS_ROWS, model, BF), shape(piece, model, BF)],
        [pltpu.SemaphoreType.DMA((3,))],
        vmem=60,
        name="prep",
    )
    first1, first3 = (moves.fetch(attn_mine, turn) for turn in turns[:2])

    soft_shape = jax.ShapeDtypeStruct((chains * heads, seq, seq), BF)
    turn_flops = 2 * rows * model * 4 * width
    mixed, qkv_own, soft_own, ctx_own, attn_part = call(
        functools.partial(attn_own_kernel, width, seq),
        [(v, SMEM) for v in (lengths, span_start, span_len)]
        + [(v, VMEM) for v in (hidden_in, vecs, bias_pack, *own_mats)],
        [
            shape(rows, model, BF),
            shape(3 * width, rows, BF),
            soft_shape,
            shape(width, rows, BF),
            shape(rows, model),
        ],
        flops=turn_flops,
        name="attn_own",
    )
    first1, first3, mixed, attn_mine, ffn_mine = sync(first1, first3, mixed, attn_mine, ffn_mine)
    first2 = moves.fetch(attn_mine, 2)
    (mine13,) = mix([Block(first1, 0, half), Block(first3, 0, half)], name="mix_1")
    near13, over13 = moves.near(mine13), moves.far(mine13)

    first2, near13, over13, ffn_mine = sync(first2, near13, over13, ffn_mine)
    ffn1 = moves.fetch(ffn_mine, 1)
    mine2, far = mix([Block(first2, 0, half)], [Block(near13), Block(first2, 0, half)], name="mix_2")
    near2, far13_2 = moves.near(mine2), moves.far(far)

    ffn1, near2, far13_2, ffn_mine = sync(ffn1, near2, far13_2, ffn_mine)
    ffn3 = moves.fetch(ffn_mine, 3)
    own13 = (Block(mine13), Block(near13), Block(over13), Block(far13_2, 0, 2 * half))
    far, other13 = mix([Block(near2), Block(ffn1)], own13, name="mix_3")
    near_f1, far2_f1, other13 = moves.near(ffn1), moves.far(far), moves.core(other13)

    ffn3, near_f1, far2_f1, other13, ffn_mine = sync(ffn3, near_f1, far2_f1, other13, ffn_mine)
    ffn2 = moves.fetch(ffn_mine, 2)
    own2 = (Block(mine2), Block(near2), Block(far13_2, 2 * half, half), Block(far2_f1, 0, half))
    far, other2 = mix([Block(near_f1), Block(ffn3)], own2, name="mix_4")
    near_f3, far_f1_f3, other2 = moves.near(ffn3), moves.far(far), moves.core(other2)

    def parts(own, other, turn=0, rows=None):
        rows = own[0].rows if rows is None else rows
        blocks = [block.at(turn * rows, rows) for block in own]
        count_turns = own[0].rows // rows
        return blocks + [Block(other, (i * count_turns + turn) * rows, rows) for i in range(4)]

    qkvs, softs, ctxs, bias_ins, attn_wholes = [], [], [], [], []
    for index, first in enumerate((first1, first3, first2)):
        last = index == count - 1
        if last:
            ffn2, near_f3, far_f1_f3, other2, attn_part = sync(ffn2, near_f3, far_f1_f3, other2, attn_part)
            own_f1 = (Block(ffn1), Block(near_f1), Block(far2_f1, half, piece), Block(far_f1_f3, 0, piece))
            far, other_f1 = mix([Block(near_f3), Block(ffn2)], own_f1, name="mix_5")
            near_f2, far_f3_f2, other_f1 = moves.near(ffn2), moves.far(far), moves.core(other_f1)
        blocks = parts(own2, other2) if last else parts(own13, other13, index, half)
        refs = Refs()
        layout = tuple(refs.add(block) for block in blocks)
        outs = [shape(3 * width, rows, BF), soft_shape, shape(width, rows, BF), shape(8, model)]
        outs += [shape(model, model, BF), shape(rows, model)]
        if last:
            outs += [shape(rows, 128), shape(rows, model, BF)]
        qkv, soft, ctx, bias_in, whole, *others = call(
            functools.partial(attn_turn_kernel, width, seq, layout, last, half, len(refs.arrays)),
            [(lengths, SMEM), (mixed, VMEM), (attn_part, VMEM), (vecs, VMEM), (first, VMEM)]
            + [(array, ANY) for array in refs.arrays],
            outs,
            [dma(1)],
            flops=turn_flops,
            name=f"attn_{turns[index]}",
        )
        for values, value in zip((qkvs, softs, ctxs, bias_ins, attn_wholes), (qkv, soft, ctx, bias_in, whole)):
            values.append(value)
        attn_part = others[0]
    hat1, inv1, normed = others

    ffn_flops = 2 * rows * model * hidden * 2
    act_own, slope_own, ffn_part = call(
        ffn_own_kernel,
        [(normed, VMEM), (w_in, VMEM), (w_back, VMEM), (bias_pack, VMEM)],
        [shape(rows, hidden, BF), shape(rows, hidden, BF), shape(rows, model)],
        flops=ffn_flops,
        name="ffn_own",
    )
    near_f2, far_f3_f2, other_f1, ffn_part = sync(near_f2, far_f3_f2, other_f1, ffn_part)
    own_f3 = (Block(ffn3), Block(near_f3), Block(far_f1_f3, piece, piece), Block(far_f3_f2, 0, piece))
    (other_f3,) = mix(own_f3, name="mix_6")
    far_f2, other_f3 = moves.far(near_f2), moves.core(other_f3)
    acts, slopes, ffn_wholes = [], [], []
    for index in range(count):
        last = index == count - 1
        if index == 0:
            blocks = parts(own_f1, other_f1)
        elif index == 1:
            far_f2, other_f3, ffn_part = sync(far_f2, other_f3, ffn_part)
            own_f2 = (Block(ffn2), Block(near_f2), Block(far_f3_f2, piece, piece), Block(far_f2))
            (other_f2,) = mix(own_f2, name="mix_7")
            other_f2 = moves.core(other_f2)
            blocks = parts(own_f3, other_f3)
        else:
            blocks = parts(own_f2, other_f2)
        refs = Refs()
        layout = tuple(refs.add(block) for block in blocks)
        ins = [(normed, VMEM), (ffn_part, VMEM), (bias_ins[index], VMEM)]
        outs = [shape(rows, hidden, BF)] * 2 + [shape(2 * model, model, BF)]
        if last:
            ins += [(hat1, VMEM), (vecs, VMEM), (cotangent, VMEM)]
            outs += [shape(rows, model, BF), shape(rows, model), shape(rows, model, BF), shape(8, model)]
        else:
            outs += [shape(rows, model)]
        act, slope, whole, *others = call(
            functools.partial(ffn_rest_kernel, piece, layout, last, len(refs.arrays)),
            ins + [(array, ANY) for array in refs.arrays],
            outs,
            [dma(1)],
            flops=ffn_flops,
            name=f"ffn_{turns[index]}",
        )
        for values, value in zip((acts, slopes, ffn_wholes), (act, slope, whole)):
            values.append(value)
        if last:
            layer_out, grad_second, grad_low, small_ffn = others
        else:
            (ffn_part,) = others

    def ffn_back(part, *turns_in, name):
        kinds = tuple(len(turn) - 2 for turn in turns_in)
        *kepts, given, part, bias = call(
            functools.partial(ffn_back_kernel, kinds, piece),
            [(v, VMEM) for v in (grad_low, normed, part)] + [(v, VMEM) for turn in turns_in for v in turn],
            [shape(4 * piece, model, BF)] * len(kinds)
            + [shape(4 * len(kinds) * piece, model, BF), shape(rows, model), shape(8, model)],
            [pltpu.VMEM((2 * model, model), BF)],
            flops=2 * len(kinds) * ffn_flops,
            name=name,
        )
        return kepts, given, part, bias

    def attn_back(part, grad_low, *turns_in, own=False, name):
        first = grad_low is None
        kinds = tuple(len(turn) - 3 for turn in turns_in)
        ins = [(mixed, VMEM), (part, VMEM)]
        ins += [(v, VMEM) for v in (hat1, inv1, vecs)] if first else [(grad_low, VMEM)]
        if own:
            ins += [(span_start, SMEM), (span_len, SMEM)]
        ins += [(v, VMEM) for turn in turns_in for v in turn]
        outs = [shape(4 * half, model, BF)] * len(kinds)
        outs += [shape(4 * len(kinds) * half, model, BF)]
        outs += [shape(rows, model, BF if own else F32), shape(8, model)]
        if first:
            outs += [shape(rows, model, BF), shape(8, model)]
        return call(
            functools.partial(attn_back_kernel, width, seq, own, first, half, kinds),
            ins,
            outs,
            [pltpu.VMEM((3 * width, rows), BF), pltpu.VMEM((model, model), BF)],
            flops=2 * len(kinds) * turn_flops,
            name=name,
        )

    def ffn_turn(index):
        return (acts[index], slopes[index], ffn_wholes[index])

    def attn_turn(index):
        return (qkvs[index], softs[index], ctxs[index], attn_wholes[index])

    class Slots:
        def __init__(self, kept, come, row=0, more=()):
            self.rows = kept.shape[0] // 4
            self.pieces = [(kept, 0), (come, row), *more]

        def slot(self, index):
            start = index * self.rows
            return [Block(array, row + start, self.rows) for array, row in self.pieces]

    (kept1,), given1, part, bias1 = ffn_back(grad_second, ffn_turn(0), name="ffn_back_1")
    come1 = moves.core(given1)
    (kept3,), given3, part, bias3 = ffn_back(part, ffn_turn(1), name="ffn_back_3")
    come1, kept3, given3, part = sync(come1, kept3, given3, part)

    cut_rows = (2 * piece, 2 * piece)
    early = mix(
        *([[Block(kept1, i * 2 * piece, n), Block(come1, i * 2 * piece, n)]] for i, n in enumerate(cut_rows)),
        name="mix_8",
    )
    part, given3, *early = sync(part, given3, *early)
    early[0] = moves.give(early[0], 1)
    come3 = moves.core(given3)
    (kept2, kept0), given20, part, bias20 = ffn_back(
        part, ffn_turn(2), (act_own, slope_own, w_in, w_back), name="ffn_back_20"
    )
    come3, given20, part, *early = sync(come3, given20, part, *early)

    f3 = Slots(kept3, come3)
    (far,) = mix([f3.slot(2), f3.slot(1)], name="mix_9")
    far, given20, part = sync(far, given20, part)
    far_f3 = moves.far(far)
    come20 = moves.core(given20)
    a_kept2, a_given2, part, a_bias2, attn_low, small_attn = attn_back(
        part, None, attn_turn(2), name="attn_back_2"
    )
    far_f3, come20, a_given2, part, *early = sync(far_f3, come20, a_given2, part, *early)

    f2 = Slots(kept2, come20)
    near, far = mix(
        [[*f3.slot(0), Block(far_f3, 0, piece)]],
        [f2.slot(2), f2.slot(1)],
        name="mix_10",
    )
    near, far, early[1], part, a_given2 = sync(near, far, early[1], part, a_given2)
    early[1] = moves.give(early[1], 1)
    near_f3, far_f2, a_come2 = moves.near(near), moves.far(far), moves.core(a_given2)
    a_kept1, a_kept3, a_given13, part, a_bias13 = attn_back(
        part, attn_low, attn_turn(0), attn_turn(1), name="attn_back_13"
    )
    near_f3, far_f2, a_come2, a_given13, part, *early = sync(
        near_f3, far_f2, a_come2, a_given13, part, *early
    )

    class Early:
        def slot(self, index):
            return Block(early[index // 2], index % 2 * piece, piece)

    f0 = Slots(kept0, come20, 4 * piece)
    a2 = Slots(a_kept2, a_come2)
    f0_slot = lambda index: f0.slot(index) + [Early().slot(index)]
    done3, near, far = mix(
        [[*f3.slot(3), Block(near_f3), Block(far_f3, piece, piece)]],
        [[*f2.slot(0), Block(far_f2, 0, piece)]],
        [f0_slot(2), a2.slot(2), f0_slot(1), a2.slot(1)],
        name="mix_11",
    )
    done3, near, far, part, a_given13 = sync(done3, near, far, part, a_given13)
    done3 = moves.give(done3, 3)
    near_f2, far_f0_a2, a_come13 = moves.near(near), moves.far(far), moves.core(a_given13)
    a_kept0, a_given0, grad_input, a_bias0 = attn_back(
        part, attn_low, (qkv_own, soft_own, ctx_own, *own_mats), own=True, name="attn_back_0"
    )
    near_f2, far_f0_a2, a_come13, done3, a_given0, grad_input, a_bias0 = sync(
        near_f2, far_f0_a2, a_come13, done3, a_given0, grad_input, a_bias0
    )

    wide = piece + half
    a1, a3 = Slots(a_kept1, a_come13), Slots(a_kept3, a_come13, 4 * half)
    done2, near, far = mix(
        [[*f2.slot(3), Block(near_f2), Block(far_f2, piece, piece)]],
        [[*f0_slot(0), Block(far_f0_a2, 0, piece)], [*a2.slot(0), Block(far_f0_a2, piece, half)]],
        [a1.slot(2), a3.slot(2), a1.slot(1), a3.slot(1)],
        name="mix_12",
    )
    biases = (bias20, bias1, bias3, a_bias0, a_bias13, a_bias2)
    rows_of = ((0, 1), (1, 0), (0, 0), (2, 0), (3, 0), (4, 0), (5, 0), (4, 1), (3, 1))
    (small,) = call(
        functools.partial(small_kernel, group, rows_of),
        [(v, VMEM) for v in (small_ffn, small_attn, *biases)],
        [shape(8 + 2 * group, model)],
        vmem=4,
        name="small",
    )
    flips = [(1 << bit, 0) for bit in range(dp_size.bit_length() - 1)]
    flips += [(0, 1 << bit) for bit in range(group.bit_length() - 1)]

    def small_step(value):
        return value + moves.flip(value, *flips.pop(0))

    done2, near, far, a_given0 = sync(done2, near, far, a_given0)
    done2 = moves.give(done2, 2)
    near_f0_a2, far_a13, a_come0 = moves.near(near), moves.far(far), moves.core(a_given0)
    small = small_step(small)
    near_f0_a2, far_a13, a_come0, done2, small = sync(near_f0_a2, far_a13, a_come0, done2, small)

    a0 = Slots(a_kept0, a_come0)
    over0 = Block(far_f0_a2, wide, piece)
    ffn_final, a_done2, near, far = mix(
        [[*f0_slot(3), Block(near_f0_a2, 0, piece), over0, Block(done3), Block(done2)]],
        [[*a2.slot(3), Block(near_f0_a2, piece, half), Block(far_f0_a2, wide + piece, half)]],
        [[*a1.slot(0), Block(far_a13, 0, half)], [*a3.slot(0), Block(far_a13, half, half)]],
        [a0.slot(2), a0.slot(1)],
        name="mix_13",
    )
    if dp_size > 8:
        ffn_final = over_rest(ffn_final, dp_size)
    near, far = mix([Block(near), Block(ffn_final)], [Block(far), Block(ffn_final)], name="mix_14")
    a_done2, near, far = sync(a_done2, near, far)
    a_done2 = moves.give(a_done2, 2)
    near_a13_f, far_a0_f = moves.near(near), moves.far(far)
    small = small_step(small)
    near_a13_f, far_a0_f, a_done2, small = sync(near_a13_f, far_a0_f, a_done2, small)

    a_done1, a_done3, near, far = mix(
        [[*a1.slot(3), Block(near_a13_f, 0, half), Block(far_a13, 2 * half, half)]],
        [[*a3.slot(3), Block(near_a13_f, half, half), Block(far_a13, 3 * half, half)]],
        [[*a0.slot(0), Block(far_a0_f, 0, half)]],
        [Block(near_a13_f, 2 * half, piece)],
        name="mix_15",
    )
    a_done1, a_done3, near, far = sync(a_done1, a_done3, near, far)
    a_done1, a_done3 = moves.give(a_done1, 1), moves.give(a_done3, 3)
    near_a0, ffn_corner = moves.near(near), moves.far(far)
    small = small_step(small)
    a_done1, a_done3, near_a0, ffn_corner, small = sync(a_done1, a_done3, near_a0, ffn_corner, small)

    own_ffn = (
        Block(ffn_final),
        Block(near_a13_f, 2 * half, piece),
        Block(far_a0_f, 2 * half, piece),
        Block(ffn_corner),
    )
    attn_final, other_ffn = mix(
        [[*a0.slot(3), Block(near_a0), Block(far_a0_f, half, half), *map(Block, (a_done1, a_done2, a_done3))]],
        own_ffn,
        name="mix_16",
    )
    if dp_size > 8:
        attn_final = over_rest(attn_final, dp_size)
    attn_final, other_ffn = sync(attn_final, other_ffn)
    attn_near, attn_over, other_ffn = moves.near(attn_final), moves.far(attn_final), moves.core(other_ffn)
    small = small_step(small)
    attn_near, attn_over, other_ffn, small = sync(attn_near, attn_over, other_ffn, small)

    attn_corner = moves.far(attn_near)
    while flips:
        small = small_step(small)

    def out(kernel, rows_in, own, other, outs, name):
        refs = Refs()
        layout = tuple(refs.add(block) for block in parts(own, other))
        return call(
            functools.partial(kernel, rows_in, layout, len(refs.arrays)),
            [(array, VMEM) for array in refs.arrays],
            outs,
            name=name,
        )

    outs = [shape(model, hidden), shape(hidden, model)]
    grad_w_in, grad_w_back = out(ffn_out_kernel, piece, own_ffn, other_ffn, outs, "ffn_out")
    attn_corner, grad_w_in, grad_w_back, small = sync(attn_corner, grad_w_in, grad_w_back, small)
    own_attn = tuple(map(Block, (attn_final, attn_near, attn_over, attn_corner)))
    (other_attn,) = mix(own_attn, name="mix_17")
    other_attn = moves.core(other_attn)
    attn_grads = out(attn_out_kernel, half, own_attn, other_attn, [shape(width, model)] * 4, "attn_out")
    grad_w_query, grad_w_key, grad_w_value = (v.T for v in attn_grads[:3])
    my_in = lax.dynamic_index_in_dim(small, 8 + rank, keepdims=False)
    my_attn = lax.dynamic_index_in_dim(small, 8 + group + rank, keepdims=False)
    return (
        layer_out,
        grad_input,
        small[6],
        grad_w_query,
        my_attn[:width],
        grad_w_key,
        grad_w_value,
        my_attn[width : 2 * width],
        attn_grads[3],
        small[5],
        small[3],
        small[4],
        grad_w_in,
        my_in,
        grad_w_back,
        small[2],
        small[0],
        small[1],
    )


def solution(mesh):
    rows = P(("dp", "tensor"), None)
    placed = (
        rows,
        P("dp"),
        P("dp"),
        P("dp"),
        P(),
        P(None, "tensor"),
        P("tensor"),
        P(None, "tensor"),
        P(None, "tensor"),
        P("tensor"),
        P("tensor", None),
        P(),
        P(),
        P(),
        P(None, "tensor"),
        P("tensor"),
        P("tensor", None),
        P(),
        P(),
        P(),
        rows,
    )
    return jax.shard_map(
        on_device,
        mesh=mesh,
        in_specs=placed,
        out_specs=(
            rows,
            rows,
            P(),
            P(None, "tensor"),
            P("tensor"),
            P(None, "tensor"),
            P(None, "tensor"),
            P("tensor"),
            P("tensor", None),
            P(),
            P(),
            P(),
            P(None, "tensor"),
            P("tensor"),
            P("tensor", None),
            P(),
            P(),
            P(),
        ),
        check_vma=False,
    )
```

```python
import functools

import jax
import jax.numpy as jnp
from jax import lax
from jax.experimental import pallas as pl
from jax.experimental.pallas import tpu as pltpu
from jax.sharding import PartitionSpec as P

HEAD_DIM = 64
EPSILON = 1e-05
MASKED = -1000000000.0
AXES = ("dp", "tensor")
BF = jnp.bfloat16
F32 = jnp.float32
MIB = 1024 * 1024
BIAS_ROWS = 16


class Moves:
    def __init__(self, dp_size, group):
        self.dp_size, self.group = dp_size, group

    def build(self, value, source):
        pairs = []
        for d in range(self.dp_size):
            for t in range(self.group):
                sd, st = source(d, t)
                pairs.append((sd * self.group + st, d * self.group + t))
        return lax.ppermute(value, AXES, pairs)

    def core(self, value):
        return self.build(value, lambda d, t: (d ^ 1, t))

    def near(self, value):
        return self.build(value, lambda d, t: (d ^ (4 if d & 1 else 2), t))

    def far(self, value):
        return self.build(value, lambda d, t: (d ^ (2 if d & 1 else 4), t))

    def fetch(self, value, turn):
        return self.build(value, lambda d, t: (d, (t + turn) % self.group))

    def pass_on(self, value):
        return self.build(value, lambda d, t: (d, (t + (-1 if d & 1 else 1)) % self.group))

    def hand_on(self, value):
        return self.build(value, lambda d, t: (d, (t + (1 if d & 1 else -1)) % self.group))

    def give(self, value, turn):
        return self.build(value, lambda d, t: (d, (t - turn) % self.group))

    def flip(self, value, mask_dp, mask_t):
        return self.build(value, lambda d, t: (d ^ mask_dp, t ^ mask_t))


def after(value, *first):
    return lax.optimization_barrier((value, *first))[0]


def over_rest(values, dp_size):
    groups = [list(range(i, dp_size, 8)) for i in range(8)]
    return lax.psum(values.astype(F32), "dp", axis_index_groups=groups).astype(BF)


def sync(*values):
    return lax.optimization_barrier(values)


def gather_places(core, chip):
    near, over = chip ^ (1 + core), chip ^ (2 - core)
    own = ((core, chip), (core, near), (core, over), (core, chip ^ 3))
    return own + ((1 - core, chip), (1 - core, over), (1 - core, near), (1 - core, chip ^ 3))


class Block:
    def __init__(self, array, row=0, rows=None):
        self.array, self.row = array, row
        self.rows = array.shape[0] - row if rows is None else rows

    def at(self, row, rows):
        return Block(self.array, self.row + row, rows)


class Refs:
    def __init__(self):
        self.arrays = []

    def add(self, block):
        for index, array in enumerate(self.arrays):
            if array is block.array:
                return index, block.row
        self.arrays.append(block.array)
        return len(self.arrays) - 1, block.row


def dot_nn(left, right):
    return jnp.dot(left, right, preferred_element_type=F32)


def dot_nt(left, right):
    return lax.dot_general(left, right, (((1,), (1,)), ((), ())), preferred_element_type=F32)


def dot_tn(left, right):
    return lax.dot_general(left, right, (((0,), (0,)), ((), ())), preferred_element_type=F32)


def row_sum(values):
    return jnp.sum(values, axis=0, keepdims=True)


def where_am_i():
    dp = lax.axis_index("dp")
    return dp & 1, (dp >> 1) & 3


def copy_in(refs, layout, rows, out_ref, sems, place):
    started = []
    for index, ((part, where), (array, row)) in enumerate(zip(gather_places(*where_am_i()), layout)):
        start = pl.multiple_of(place(part, where), rows)
        copy = pltpu.make_async_copy(
            refs[array].at[pl.ds(row, rows)], out_ref.at[pl.ds(start, rows)], sems.at[index]
        )
        copy.start()
        started.append(copy)
    return started


def attn_place(rows):
    return lambda part, where: (2 * where + part) * rows


def ffn_place(rows):
    return lambda part, where: (part * 4 + where) * rows


def scatter_out(source_ref, rows, kept_ref, given_ref, base, place):
    core, chip = where_am_i()
    for ref, mine, first in ((kept_ref, core, 0), (given_ref, 1 - core, base)):
        for slot, where in enumerate((chip ^ (1 + mine), chip ^ (2 - mine), chip ^ 3, chip)):
            start = pl.multiple_of(place(mine, where), rows)
            begin = first + slot * rows
            ref[begin : begin + rows, :] = source_ref[pl.ds(start, rows), :]


def block_of(values, chain, head, seq):
    return values[head * HEAD_DIM : (head + 1) * HEAD_DIM, chain * seq : (chain + 1) * seq]


def attend(width, seq, lengths, mixed, mats, bias, qkv, soft, ctx):
    chains = mixed.shape[0] // seq
    heads = width // HEAD_DIM
    base = lax.axis_index("tensor") * chains
    column = jnp.broadcast_to(bias, (8, bias.shape[1])).T[:, :1]
    scale = HEAD_DIM**-0.5
    parts = []
    for index in range(3):
        cut = slice(index * width, (index + 1) * width)
        values = dot_nt(mats[index], mixed)
        if index != 1:
            values = values + column[cut]
        parts.append(values.astype(BF))
    scaled = (parts[0].astype(F32) * scale).astype(BF)
    for index, values in enumerate((scaled, parts[1], parts[2])):
        qkv[index * width : (index + 1) * width, :] = values
    position = lax.broadcasted_iota(jnp.int32, (seq, 1), 0)
    blocks = [(chain, head) for chain in range(chains) for head in range(heads)]
    scores = [
        jnp.where(
            position < lengths[base + chain],
            dot_tn(block_of(parts[1], chain, head, seq), block_of(scaled, chain, head, seq)),
            MASKED,
        )
        for chain, head in blocks
    ]
    shifted = [jnp.exp(value - jnp.max(value, axis=0, keepdims=True)) for value in scores]
    weights = [(value * (1.0 / row_sum(value))).astype(BF) for value in shifted]
    for index, (chain, head) in enumerate(blocks):
        soft[index] = weights[index]
        ctx[head * HEAD_DIM : (head + 1) * HEAD_DIM, chain * seq : (chain + 1) * seq] = dot_nn(
            block_of(parts[2], chain, head, seq), weights[index]
        ).astype(BF)
    return dot_tn(ctx[...], mats[3])


def norm_back(grad, hat, inv, gain):
    scaled = grad * gain
    mean_one = jnp.mean(scaled, axis=1, keepdims=True)
    mean_two = jnp.mean(scaled * hat, axis=1, keepdims=True)
    return inv * (scaled - mean_one - hat * mean_two)


def norm_parts(values):
    centred = values - jnp.mean(values, axis=1, keepdims=True)
    inv = lax.rsqrt(jnp.mean(centred * centred, axis=1, keepdims=True) + EPSILON)
    return centred * inv, inv


def in_span(starts, counts, chain, chains, seq):
    index = lax.axis_index("tensor") * chains + chain
    position = lax.broadcasted_iota(jnp.int32, (seq, 1), 0)
    return (position >= starts[index]) & (position < starts[index] + counts[index])


EMBED, B_OUT, G_ATTN, S_ATTN, B_BACK, G_FFN, S_FFN = range(7)


def prep_kernel(
    width, half, piece, b_in, b_query, b_value, *refs
):
    vectors, refs = refs[:7], refs[7:]
    wq, wk, wv, wo, w_in, w_back, attn_mine, ffn_mine, bias, vecs, rows, sems = refs
    core, chip = where_am_i()
    copies = []
    for index, ref in enumerate((wq, wk, wv, wo)):
        start = pl.multiple_of(core * half, half)
        copy = pltpu.make_async_copy(
            ref.at[pl.ds(start, half)], attn_mine.at[pl.ds(0, half)], sems.at[0]
        )
        pl.when(chip == index)(copy.start)
    copies.append(copy)
    for index, ref in enumerate((w_in, w_back)):
        start = pl.multiple_of(chip * piece, piece)
        copy = pltpu.make_async_copy(ref.at[pl.ds(start, piece)], ffn_mine, sems.at[1])
        pl.when(core == index)(copy.start)
    copies.append(copy)
    as_row = lambda ref: ref[...].astype(F32).reshape(1, -1)
    rows[...] = jnp.zeros_like(rows)
    rows[0:1, :] = as_row(b_in)
    rows[1:2, :width] = as_row(b_query)
    rows[1:2, 2 * width : 3 * width] = as_row(b_value)
    bias[...] = rows[...].astype(BF)
    for index, ref in enumerate(vectors):
        vecs[index : index + 1, :] = as_row(ref)
    vecs[7:8, :] = rows[2:3, :]
    for copy in copies:
        copy.wait()
    attn_mine[half : half + BIAS_ROWS, :] = rows[...].astype(BF)


def pick_kernel(own, other, out):
    core, _ = where_am_i()

    @pl.when(core == 0)
    def _():
        out[...] = own[...]

    @pl.when(core == 1)
    def _():
        out[...] = other[...]


def attn_own_kernel(
    width, seq, lengths, starts, counts, hidden, vecs, bias, wq, wk, wv, wo, mixed, qkv, soft, ctx, part
):
    chains = hidden.shape[0] // seq
    for chain in range(chains):
        rows = slice(chain * seq, (chain + 1) * seq)
        span = in_span(starts, counts, chain, chains, seq)
        mixed[rows, :] = jnp.where(span, vecs[EMBED : EMBED + 1, :], hidden[rows, :].astype(F32)).astype(BF)
    mats = (wq[...], wk[...], wv[...], wo[...])
    part[...] = attend(
        width, seq, lengths, mixed[...], mats, bias[1:2, :].astype(F32), qkv, soft, ctx
    )


def attn_mats(mats, width):
    return [mats[i * width : (i + 1) * width, :] for i in range(4)]


def attn_turn_kernel(
    width, seq, layout, last, part_rows, count, lengths, mixed, part, vecs, first, *refs
):
    pieces, refs = refs[:count], refs[count:]
    qkv, soft, ctx, bias_in, mats = refs[:5]
    sems = refs[-1]
    copies = copy_in(pieces, layout, part_rows, mats, sems, attn_place(part_rows))
    bias_in[...] = jnp.broadcast_to(first[part_rows : part_rows + 1, :].astype(F32), bias_in.shape)
    for copy in copies:
        copy.wait()
    bias = first[part_rows + 1 : part_rows + 2, :].astype(F32)
    total = part[...] + attend(
        width, seq, lengths, mixed[...], attn_mats(mats, width), bias, qkv, soft, ctx
    )
    if not last:
        refs[5][...] = total
        return
    hat, inv, normed = refs[5:8]
    ahat, ainv = norm_parts(total + mixed[...].astype(F32) + vecs[B_OUT : B_OUT + 1, :])
    hat[...] = ahat
    inv[...] = jnp.broadcast_to(ainv, inv.shape)
    normed[...] = (ahat * vecs[G_ATTN : G_ATTN + 1, :] + vecs[S_ATTN : S_ATTN + 1, :]).astype(BF)


def gelu_both(pre):
    cdf = 0.5 * (1.0 + lax.erf(pre * (0.5**0.5)))
    pdf = jnp.exp(-0.5 * pre * pre) * (0.5 / 3.141592653589793) ** 0.5
    return pre * cdf, cdf + pre * pdf


def ffn_step(normed, mat_in, mat_back, bias, act, slope):
    pre = dot_nn(normed[...], mat_in) + bias
    value, rate = gelu_both(pre)
    act[...] = value.astype(BF)
    slope[...] = rate.astype(BF)
    return dot_nn(act[...], mat_back)


def ffn_own_kernel(normed, mat_in, mat_back, bias, act, slope, total):
    total[...] = ffn_step(
        normed, mat_in[...], mat_back[...], bias[0:1, :].astype(F32), act, slope
    )


def ffn_rest_kernel(part_rows, layout, last, count, normed, part, bias_in, *refs):
    if last:
        (hat1, vecs, cot), refs = refs[:3], refs[3:]
    pieces, refs = refs[:count], refs[count:]
    act, slope, mats = refs[:3]
    sems = refs[-1]
    copies = copy_in(pieces, layout, part_rows, mats, sems, ffn_place(part_rows))
    height = 4 * part_rows
    for copy in copies:
        copy.wait()
    value = part[...] + ffn_step(
        normed, mats[:height, :], mats[height:, :], bias_in[0:1, :], act, slope
    )
    if not last:
        refs[3][...] = value
        return
    layer_out, grad_second, grad_low, small = refs[3:7]
    first = hat1[...] * vecs[G_ATTN : G_ATTN + 1, :] + vecs[S_ATTN : S_ATTN + 1, :]
    hat, inv = norm_parts(first + value + vecs[B_BACK : B_BACK + 1, :])
    gain = vecs[G_FFN : G_FFN + 1, :]
    layer_out[...] = (hat * gain + vecs[S_FFN : S_FFN + 1, :]).astype(BF)
    grad = cot[...].astype(F32)
    back = norm_back(grad, hat, inv, gain)
    grad_second[...] = back
    grad_low[...] = back.astype(BF)
    small[0:1, :] = row_sum(grad * hat)
    small[1:2, :] = row_sum(grad)
    small[2:3, :] = row_sum(back)
    small[3:, :] = jnp.zeros_like(small[3:, :])


def ffn_back_kernel(counts, part_rows, grad_low, normed, part, *refs):
    turns = []
    for count in counts:
        act, slope, *mats = refs[: 2 + count]
        refs = refs[2 + count :]
        turns.append((act, slope, mats))
    kepts, refs = refs[: len(turns)], refs[len(turns) :]
    given, total, bias_grad, whole = refs
    height = 4 * part_rows
    value = part[...]
    bias_grad[...] = jnp.zeros_like(bias_grad)
    for index, (act, slope, mats) in enumerate(turns):
        if len(mats) == 2:
            mat_in, mat_back = mats[0][...], mats[1][...]
        else:
            mat_in, mat_back = mats[0][:height, :], mats[0][height:, :]
        whole[height:, :] = dot_tn(act[...], grad_low[...]).astype(BF)
        grad_act = dot_nt(grad_low[...], mat_back)
        grad_pre = (grad_act * slope[...].astype(F32)).astype(BF)
        bias_grad[index : index + 1, :] = row_sum(grad_pre.astype(F32))
        whole[:height, :] = dot_tn(normed[...], grad_pre).astype(BF)
        value = value + dot_nt(grad_pre, mat_in)
        base = index * 4 * part_rows
        scatter_out(whole, part_rows, kepts[index], given, base, ffn_place(part_rows))
    total[...] = value


def attend_back(width, seq, grad_low, mats, mixed, qkv, soft, ctx, grad_qkv, whole):
    chains = grad_low.shape[0] // seq
    heads = width // HEAD_DIM
    scale = HEAD_DIM**-0.5
    whole[3 * width :, :] = dot_nn(ctx[...], grad_low).astype(BF)
    grad_ctx = dot_nt(mats[3], grad_low).astype(BF)
    queries, keys, values = (qkv[i * width : (i + 1) * width, :] for i in range(3))
    blocks = [(chain, head) for chain in range(chains) for head in range(heads)]
    grad_weights = [
        dot_tn(block_of(values, chain, head, seq), block_of(grad_ctx, chain, head, seq))
        for chain, head in blocks
    ]
    grad_scores = []
    for index, value in enumerate(grad_weights):
        wide = soft[index].astype(F32)
        product = wide * value
        grad_scores.append((product - wide * row_sum(product)).astype(BF))
    for index, (chain, head) in enumerate(blocks):
        columns = slice(chain * seq, (chain + 1) * seq)
        for slot, value in enumerate(
            (
                dot_nn(block_of(keys, chain, head, seq), grad_scores[index]) * scale,
                dot_nt(block_of(queries, chain, head, seq), grad_scores[index]),
                dot_nt(block_of(grad_ctx, chain, head, seq), soft[index]),
            )
        ):
            start = slot * width + head * HEAD_DIM
            grad_qkv[start : start + HEAD_DIM, columns] = value.astype(BF)
    whole[: 3 * width, :] = dot_nn(grad_qkv[...], mixed).astype(BF)
    ones = jnp.ones((8, grad_low.shape[0]), BF)
    back = dot_tn(grad_qkv[:width, :], mats[0])
    back = back + dot_tn(grad_qkv[width : 2 * width, :], mats[1])
    back = back + dot_tn(grad_qkv[2 * width :, :], mats[2])
    return back, dot_nt(ones, grad_qkv[...])


def attn_back_kernel(width, seq, own, first, part_rows, counts, mixed, part, *refs):
    if first:
        (hat, inv, vecs), refs = refs[:3], refs[3:]
    else:
        (grad_low,), refs = refs[:1], refs[1:]
    if own:
        (starts, counts_ref), refs = refs[:2], refs[2:]
    turns = []
    for count in counts:
        qkv, soft, ctx, *mats = refs[: 3 + count]
        refs = refs[3 + count :]
        turns.append((qkv, soft, ctx, mats))
    kepts, refs = refs[: len(turns)], refs[len(turns) :]
    given, total, bias_grad = refs[:3]
    refs = refs[3:]
    if first:
        (grad_low, small), refs = refs[:2], refs[2:]
    grad_qkv, whole = refs
    if first:
        grad = part[...]
        value = norm_back(grad, hat[...], inv[:, :1], vecs[G_ATTN : G_ATTN + 1, :])
        grad_low[...] = value.astype(BF)
        small[0:1, :] = row_sum(grad * hat[...])
        small[1:2, :] = row_sum(grad)
        small[2:3, :] = row_sum(value)
        small[3:, :] = jnp.zeros_like(small[3:, :])
    else:
        value = part[...]
    bias_grad[...] = jnp.zeros_like(bias_grad)
    for index, (qkv, soft, ctx, refs_in) in enumerate(turns):
        mats = [ref[...] for ref in refs_in] if len(refs_in) == 4 else attn_mats(refs_in[0], width)
        back, sums = attend_back(
            width, seq, grad_low[...], mats, mixed[...], qkv, soft, ctx, grad_qkv, whole
        )
        value = value + back
        bias_grad[index : index + 1, :width] = sums[0:1, :width]
        bias_grad[index : index + 1, width : 2 * width] = sums[0:1, 2 * width :]
        base = index * 4 * part_rows
        scatter_out(whole, part_rows, kepts[index], given, base, attn_place(part_rows))
    if not own:
        total[...] = value
        return
    chains = value.shape[0] // seq
    embed_sum = jnp.zeros((1, value.shape[1]), F32)
    for chain in range(chains):
        rows = slice(chain * seq, (chain + 1) * seq)
        span = in_span(starts, counts_ref, chain, chains, seq)
        total[rows, :] = jnp.where(span, 0.0, value[rows, :]).astype(BF)
        embed_sum = embed_sum + row_sum(jnp.where(span, value[rows, :], 0.0))
    bias_grad[1:2, :] = embed_sum


def split_kernel(value, at_zero, at_one):
    core, _ = where_am_i()
    for index, out in enumerate((at_zero, at_one)):

        @pl.when(core == index)
        def _():
            out[...] = value[...]

        @pl.when(core != index)
        def _():
            out[...] = jnp.zeros_like(out)


def mix_kernel(count, plan, *refs):
    for out, blocks in zip(refs[count:], plan):
        start = 0
        for rows, sources in blocks:
            array, row = sources[0]
            value = refs[array][row : row + rows, :]
            if len(sources) > 1:
                value = value.astype(F32)
                for array, row in sources[1:]:
                    value = value + refs[array][row : row + rows, :].astype(F32)
                value = value.astype(BF)
            out[start : start + rows, :] = value
            start += rows


def ffn_out_kernel(part_rows, layout, count, *refs):
    outs = refs[count:]
    for (array, row), (part, where) in zip(layout, gather_places(*where_am_i())):
        start = pl.multiple_of(where * part_rows, part_rows)
        for index in range(2):

            @pl.when(part == index)
            def _():
                block = refs[array][row : row + part_rows, :]
                outs[index][pl.ds(start, part_rows), :] = block.astype(F32)


def attn_out_kernel(part_rows, layout, count, *refs):
    outs = refs[count:]
    for (array, row), (part, where) in zip(layout, gather_places(*where_am_i())):
        start = pl.multiple_of(part * part_rows, part_rows)
        for index in range(4):

            @pl.when(where == index)
            def _():
                block = refs[array][row : row + part_rows, :]
                outs[index][pl.ds(start, part_rows), :] = block.astype(F32)


def small_kernel(group, rows_of, small_ffn, small_attn, *refs):
    out = refs[-1]
    rank = lax.axis_index("tensor")
    out[...] = jnp.zeros_like(out)
    out[0:3, :] = small_ffn[0:3, :]
    out[3:6, :] = small_attn[0:3, :]
    for index, (array, source) in enumerate(rows_of[:-1]):
        row = 8 + index // group * group + lax.rem(index % group + rank, group)
        out[pl.ds(row, 1), :] = refs[array][source : source + 1, :]
    array, source = rows_of[-1]
    out[6:7, :] = refs[array][source : source + 1, :]


SMEM = pl.BlockSpec(memory_space=pltpu.SMEM)
VMEM = pl.BlockSpec(memory_space=pltpu.VMEM)
ANY = pl.BlockSpec(memory_space=pl.ANY)


def call(kernel, ins, outs, scratch=(), flops=0, vmem=16, name=None):
    arrays = [array for array, _ in ins]
    moved = sum(a.size * a.dtype.itemsize for a in arrays) + sum(
        o.size * o.dtype.itemsize for o in outs
    )
    return pl.pallas_call(
        kernel,
        in_specs=[spec for _, spec in ins],
        out_specs=[VMEM] * len(outs),
        out_shape=list(outs),
        scratch_shapes=list(scratch),
        compiler_params=pltpu.CompilerParams(vmem_limit_bytes=vmem * MIB),
        cost_estimate=pl.CostEstimate(flops=flops // 100, bytes_accessed=moved // 100, transcendentals=0),
        name=name,
    )(*arrays)


def shape(rows, columns, kind=F32):
    return jax.ShapeDtypeStruct((rows, columns), kind)


def pick(own, other):
    return call(
        pick_kernel,
        [(own, VMEM), (other, VMEM)],
        [shape(*own.shape, own.dtype)],
        vmem=4,
        name="pick",
    )[0]


def split(value):
    return call(
        split_kernel,
        [(value, VMEM)],
        [shape(*value.shape, value.dtype)] * 2,
        vmem=4,
        name="split",
    )


def mix(*outs, first=(), name=None):
    refs, plan, shapes = Refs(), [], []
    for blocks in outs:
        mine = []
        for block in blocks:
            sources = block if isinstance(block, list) else [block]
            mine.append((sources[0].rows, tuple(refs.add(source) for source in sources)))
        plan.append(tuple(mine))
        top = blocks[0][0] if isinstance(blocks[0], list) else blocks[0]
        shapes.append(shape(sum(rows for rows, _ in mine), top.array.shape[1], BF))
    if first:
        refs.arrays[0] = after(refs.arrays[0], *first)
    return call(
        functools.partial(mix_kernel, len(refs.arrays), tuple(plan)),
        [(array, VMEM) for array in refs.arrays],
        shapes,
        vmem=4,
        name=name,
    )


def on_device(
    hidden_in,
    lengths,
    span_start,
    span_len,
    mask_embed,
    w_query,
    b_query,
    w_key,
    w_value,
    b_value,
    w_out,
    b_out,
    g_attn,
    s_attn,
    w_in,
    b_in,
    w_back,
    b_back,
    g_ffn,
    s_ffn,
    cotangent,
):
    group = lax.axis_size("tensor")
    dp_size = lax.axis_size("dp")
    moves = Moves(dp_size, group)
    rank = lax.axis_index("tensor")
    rows, model = hidden_in.shape
    seq = rows * group // lengths.shape[0]
    chains = rows // seq
    width = w_query.shape[1]
    heads = width // HEAD_DIM
    hidden = w_in.shape[1]
    piece = model // 4
    half = piece // 2
    turns = (1, 3, 2)
    count = len(turns)

    own_mats = (w_query.T, w_key.T, w_value.T, w_out)
    dma = lambda n: pltpu.SemaphoreType.DMA((8 * n,))

    attn_mine, ffn_mine, bias_pack, vecs = call(
        functools.partial(prep_kernel, width, half, piece),
        [(v, VMEM) for v in (b_in, b_query, b_value)]
        + [(v, VMEM) for v in (mask_embed, b_out, g_attn, s_attn, b_back, g_ffn, s_ffn)]
        + [(v, ANY) for v in (*own_mats, w_in, w_back)],
        [
            shape(half + BIAS_ROWS, model, BF),
            shape(piece, model, BF),
            shape(BIAS_ROWS, model, BF),
            shape(8, model),
        ],
        [pltpu.VMEM((BIAS_ROWS, model), F32), pltpu.SemaphoreType.DMA((2,))],
        vmem=60,
        name="prep",
    )
    first1, first3 = (moves.fetch(attn_mine, turn) for turn in turns[:2])

    soft_shape = jax.ShapeDtypeStruct((chains * heads, seq, seq), BF)
    turn_flops = 2 * rows * model * 4 * width
    mixed, qkv_own, soft_own, ctx_own, attn_part = call(
        functools.partial(attn_own_kernel, width, seq),
        [(v, SMEM) for v in (lengths, span_start, span_len)]
        + [(v, VMEM) for v in (hidden_in, vecs, bias_pack, *own_mats)],
        [
            shape(rows, model, BF),
            shape(3 * width, rows, BF),
            soft_shape,
            shape(width, rows, BF),
            shape(rows, model),
        ],
        flops=turn_flops,
        name="attn_own",
    )
    first1, first3, mixed, attn_mine, ffn_mine = sync(first1, first3, mixed, attn_mine, ffn_mine)
    first2 = moves.pass_on(pick(first1, first3))
    (mine13,) = mix([Block(first1, 0, half), Block(first3, 0, half)], name="mix_1")
    near13, over13 = moves.near(mine13), moves.far(mine13)

    first2, near13, over13, ffn_mine = sync(first2, near13, over13, ffn_mine)
    ffn1 = moves.fetch(ffn_mine, 1)
    mine2, far = mix([Block(first2, 0, half)], [Block(near13), Block(first2, 0, half)], name="mix_2")
    near2, far13_2 = moves.near(mine2), moves.far(far)

    ffn1, near2, far13_2, ffn_mine = sync(ffn1, near2, far13_2, ffn_mine)
    ffn3 = moves.fetch(ffn_mine, 3)
    own13 = (Block(mine13), Block(near13), Block(over13), Block(far13_2, 0, 2 * half))
    far, other13 = mix([Block(near2), Block(ffn1)], own13, name="mix_3")
    near_f1, far2_f1, other13 = moves.near(ffn1), moves.far(far), moves.core(other13)

    ffn3, near_f1, far2_f1, other13, ffn_mine = sync(ffn3, near_f1, far2_f1, other13, ffn_mine)
    ffn2 = moves.pass_on(pick(ffn1, ffn3))
    own2 = (Block(mine2), Block(near2), Block(far13_2, 2 * half, half), Block(far2_f1, 0, half))
    far, other2 = mix([Block(near_f1), Block(ffn3)], own2, name="mix_4")
    near_f3, far_f1_f3, other2 = moves.near(ffn3), moves.far(far), moves.core(other2)

    def parts(own, other, turn=0, rows=None):
        rows = own[0].rows if rows is None else rows
        blocks = [block.at(turn * rows, rows) for block in own]
        count_turns = own[0].rows // rows
        return blocks + [Block(other, (i * count_turns + turn) * rows, rows) for i in range(4)]

    qkvs, softs, ctxs, bias_ins, attn_wholes = [], [], [], [], []
    for index, first in enumerate((first1, first3, first2)):
        last = index == count - 1
        if last:
            ffn2, near_f3, far_f1_f3, other2, attn_part = sync(ffn2, near_f3, far_f1_f3, other2, attn_part)
            own_f1 = (Block(ffn1), Block(near_f1), Block(far2_f1, half, piece), Block(far_f1_f3, 0, piece))
            far, other_f1 = mix([Block(near_f3), Block(ffn2)], own_f1, name="mix_5")
            near_f2, far_f3_f2, other_f1 = moves.near(ffn2), moves.far(far), moves.core(other_f1)
        blocks = parts(own2, other2) if last else parts(own13, other13, index, half)
        refs = Refs()
        layout = tuple(refs.add(block) for block in blocks)
        outs = [shape(3 * width, rows, BF), soft_shape, shape(width, rows, BF), shape(8, model)]
        outs += [shape(model, model, BF), shape(rows, model)]
        if last:
            outs += [shape(rows, 128), shape(rows, model, BF)]
        qkv, soft, ctx, bias_in, whole, *others = call(
            functools.partial(attn_turn_kernel, width, seq, layout, last, half, len(refs.arrays)),
            [(lengths, SMEM), (mixed, VMEM), (attn_part, VMEM), (vecs, VMEM), (first, VMEM)]
            + [(array, ANY) for array in refs.arrays],
            outs,
            [dma(1)],
            flops=turn_flops,
            name=f"attn_{turns[index]}",
        )
        for values, value in zip((qkvs, softs, ctxs, bias_ins, attn_wholes), (qkv, soft, ctx, bias_in, whole)):
            values.append(value)
        attn_part = others[0]
    hat1, inv1, normed = others

    ffn_flops = 2 * rows * model * hidden * 2
    act_own, slope_own, ffn_part = call(
        ffn_own_kernel,
        [(normed, VMEM), (w_in, VMEM), (w_back, VMEM), (bias_pack, VMEM)],
        [shape(rows, hidden, BF), shape(rows, hidden, BF), shape(rows, model)],
        flops=ffn_flops,
        name="ffn_own",
    )
    near_f2, far_f3_f2, other_f1, ffn_part = sync(near_f2, far_f3_f2, other_f1, ffn_part)
    own_f3 = (Block(ffn3), Block(near_f3), Block(far_f1_f3, piece, piece), Block(far_f3_f2, 0, piece))
    (other_f3,) = mix(own_f3, name="mix_6")
    far_f2, other_f3 = moves.far(near_f2), moves.core(other_f3)
    acts, slopes, ffn_wholes = [], [], []
    for index in range(count):
        last = index == count - 1
        if index == 0:
            blocks = parts(own_f1, other_f1)
        elif index == 1:
            far_f2, other_f3, ffn_part = sync(far_f2, other_f3, ffn_part)
            own_f2 = (Block(ffn2), Block(near_f2), Block(far_f3_f2, piece, piece), Block(far_f2))
            (other_f2,) = mix(own_f2, name="mix_7")
            other_f2 = moves.core(other_f2)
            blocks = parts(own_f3, other_f3)
        else:
            blocks = parts(own_f2, other_f2)
        refs = Refs()
        layout = tuple(refs.add(block) for block in blocks)
        ins = [(normed, VMEM), (ffn_part, VMEM), (bias_ins[index], VMEM)]
        outs = [shape(rows, hidden, BF)] * 2 + [shape(2 * model, model, BF)]
        if last:
            ins += [(hat1, VMEM), (vecs, VMEM), (cotangent, VMEM)]
            outs += [shape(rows, model, BF), shape(rows, model), shape(rows, model, BF), shape(8, model)]
        else:
            outs += [shape(rows, model)]
        act, slope, whole, *others = call(
            functools.partial(ffn_rest_kernel, piece, layout, last, len(refs.arrays)),
            ins + [(array, ANY) for array in refs.arrays],
            outs,
            [dma(1)],
            flops=ffn_flops,
            name=f"ffn_{turns[index]}",
        )
        for values, value in zip((acts, slopes, ffn_wholes), (act, slope, whole)):
            values.append(value)
        if last:
            layer_out, grad_second, grad_low, small_ffn = others
        else:
            (ffn_part,) = others

    def ffn_back(part, *turns_in, name):
        kinds = tuple(len(turn) - 2 for turn in turns_in)
        *kepts, given, part, bias = call(
            functools.partial(ffn_back_kernel, kinds, piece),
            [(v, VMEM) for v in (grad_low, normed, part)] + [(v, VMEM) for turn in turns_in for v in turn],
            [shape(4 * piece, model, BF)] * len(kinds)
            + [shape(4 * len(kinds) * piece, model, BF), shape(rows, model), shape(8, model)],
            [pltpu.VMEM((2 * model, model), BF)],
            flops=2 * len(kinds) * ffn_flops,
            name=name,
        )
        return kepts, given, part, bias

    def attn_back(part, grad_low, *turns_in, own=False, name):
        first = grad_low is None
        kinds = tuple(len(turn) - 3 for turn in turns_in)
        ins = [(mixed, VMEM), (part, VMEM)]
        ins += [(v, VMEM) for v in (hat1, inv1, vecs)] if first else [(grad_low, VMEM)]
        if own:
            ins += [(span_start, SMEM), (span_len, SMEM)]
        ins += [(v, VMEM) for turn in turns_in for v in turn]
        outs = [shape(4 * half, model, BF)] * len(kinds)
        outs += [shape(4 * len(kinds) * half, model, BF)]
        outs += [shape(rows, model, BF if own else F32), shape(8, model)]
        if first:
            outs += [shape(rows, model, BF), shape(8, model)]
        return call(
            functools.partial(attn_back_kernel, width, seq, own, first, half, kinds),
            ins,
            outs,
            [pltpu.VMEM((3 * width, rows), BF), pltpu.VMEM((model, model), BF)],
            flops=2 * len(kinds) * turn_flops,
            name=name,
        )

    def ffn_turn(index):
        return (acts[index], slopes[index], ffn_wholes[index])

    def attn_turn(index):
        return (qkvs[index], softs[index], ctxs[index], attn_wholes[index])

    class Slots:
        def __init__(self, kept, come, row=0, more=()):
            self.rows = kept.shape[0] // 4
            self.pieces = [(kept, 0), (come, row), *more]

        def slot(self, index):
            start = index * self.rows
            return [Block(array, row + start, self.rows) for array, row in self.pieces]

        def passed(self, index, *arrived):
            return [self.slot(index) + [Block(array, row, self.rows) for array, row in arrived]]

    (kept2,), given2, part, bias2 = ffn_back(grad_second, ffn_turn(2), name="ffn_back_2")
    come2 = moves.core(given2)
    (kept1,), given1, part, bias1 = ffn_back(part, ffn_turn(0), name="ffn_back_1")
    come2, given1, part = sync(come2, given1, part)

    f2 = Slots(kept2, come2)
    (far,) = mix([f2.slot(2), f2.slot(1)], name="mix_8")
    far, part, given1 = sync(far, part, given1)
    far_f2, come1 = moves.far(far), moves.core(given1)
    (kept3, kept0), given30, part, bias30 = ffn_back(
        part, ffn_turn(1), (act_own, slope_own, w_in, w_back), name="ffn_back_30"
    )
    far_f2, come1, given30, part = sync(far_f2, come1, given30, part)

    f1 = Slots(kept1, come1)
    near, far = mix(f2.passed(0, (far_f2, 0)), [f1.slot(2), f1.slot(1)], name="mix_9")
    near, far, given30, part = sync(near, far, given30, part)
    near_f2, far_f1, come30 = moves.near(near), moves.far(far), moves.core(given30)
    a_kept2, a_kept3, a_given23, part, a_bias23, attn_low, small_attn = attn_back(
        part, None, attn_turn(2), attn_turn(1), name="attn_back_23"
    )
    near_f2, far_f1, come30, a_given23, part = sync(near_f2, far_f1, come30, a_given23, part)

    f3, f0 = Slots(kept3, come30), Slots(kept0, come30, 4 * piece)
    done2, near, far = mix(
        f2.passed(3, (near_f2, 0), (far_f2, piece)),
        f1.passed(0, (far_f1, 0)),
        [f3.slot(2), f3.slot(1)],
        name="mix_10",
    )
    done2, near, far, a_given23, part = sync(done2, near, far, a_given23, part)
    done2, near_f1, far_f3 = moves.hand_on(done2), moves.near(near), moves.far(far)
    a_come23 = moves.core(a_given23)
    a_kept1, a_given1, part, a_bias1 = attn_back(part, attn_low, attn_turn(0), name="attn_back_1")
    near_f1, far_f3, a_come23, done2, a_given1, part = sync(near_f1, far_f3, a_come23, done2, a_given1, part)

    for_one, for_three = split(done2)
    a2, a3 = Slots(a_kept2, a_come23), Slots(a_kept3, a_come23, 4 * half)
    done1, near, far = mix(
        f1.passed(3, (near_f1, 0), (far_f1, piece), (for_one, 0)),
        f3.passed(0, (far_f3, 0)),
        [a2.slot(2), a3.slot(2), a2.slot(1), a3.slot(1)],
        name="mix_11",
    )
    done1, near, far, a_given1, part = sync(done1, near, far, a_given1, part)
    done1, near_f3, far_a23 = moves.give(done1, 1), moves.near(near), moves.far(far)
    a_come1 = moves.core(a_given1)
    a_kept0, a_given0, grad_input, a_bias0 = attn_back(
        part, attn_low, (qkv_own, soft_own, ctx_own, *own_mats), own=True, name="attn_back_0"
    )
    near_f3, far_a23, a_come1, done1, a_given0, grad_input, a_bias0 = sync(
        near_f3, far_a23, a_come1, done1, a_given0, grad_input, a_bias0
    )

    done3, near, far = mix(
        f3.passed(3, (near_f3, 0), (far_f3, piece), (for_three, 0)),
        a2.passed(0, (far_a23, 0)) + a3.passed(0, (far_a23, half)),
        [f0.slot(2), f0.slot(1)],
        name="mix_12",
    )
    biases = (bias30, bias1, bias2, a_bias0, a_bias1, a_bias23)
    rows_of = ((0, 1), (1, 0), (2, 0), (0, 0), (3, 0), (4, 0), (5, 0), (5, 1), (3, 1))
    (small,) = call(
        functools.partial(small_kernel, group, rows_of),
        [(v, VMEM) for v in (small_ffn, small_attn, *biases)],
        [shape(8 + 2 * group, model)],
        vmem=4,
        name="small",
    )
    flips = [(1 << bit, 0) for bit in range(dp_size.bit_length() - 1)]
    flips += [(0, 1 << bit) for bit in range(group.bit_length() - 1)]

    def small_step(value):
        return value + moves.flip(value, *flips.pop(0))

    done3, near, far, a_given0, small = sync(done3, near, far, a_given0, small)
    done3, near_a23, far_f0 = moves.give(done3, 3), moves.near(near), moves.far(far)
    a_come0 = moves.core(a_given0)
    small = small_step(small)
    done3, near_a23, far_f0, a_come0, small = sync(done3, near_a23, far_f0, a_come0, small)

    a1, a0 = Slots(a_kept1, a_come1), Slots(a_kept0, a_come0)
    a_done2, near, far = mix(
        a2.passed(3, (near_a23, 0), (far_a23, 2 * half)),
        f0.passed(0, (far_f0, 0)),
        [a1.slot(2), a0.slot(2), a1.slot(1), a0.slot(1)],
        name="mix_13",
    )
    a_done2, near, far, small = sync(a_done2, near, far, small)
    a_done2, near_f0, far_a10 = moves.hand_on(a_done2), moves.near(near), moves.far(far)
    small = small_step(small)
    a_done2, near_f0, far_a10, small = sync(a_done2, near_f0, far_a10, small)

    a_for_one, a_for_three = split(a_done2)
    arrived = ((near_f0, 0), (far_f0, piece), (done1, 0), (done3, 0))
    (ffn_final,) = mix(f0.passed(3, *arrived), name="mix_14")
    if dp_size > 8:
        ffn_final = over_rest(ffn_final, dp_size)
    a_done3, near = mix(
        a3.passed(3, (near_a23, half), (far_a23, 3 * half), (a_for_three, 0)),
        a1.passed(0, (far_a10, 0)) + a0.passed(0, (far_a10, half)) + [Block(ffn_final)],
        name="mix_15",
    )
    ffn_final, near, a_done3, small = sync(ffn_final, near, a_done3, small)
    near_a10_f, ffn_over, a_done3 = moves.near(near), moves.far(ffn_final), moves.give(a_done3, 3)
    small = small_step(small)
    near_a10_f, ffn_over, a_done3, small = sync(near_a10_f, ffn_over, a_done3, small)

    a_done1, far = mix(
        a1.passed(3, (near_a10_f, 0), (far_a10, 2 * half), (a_for_one, 0)),
        [Block(near_a10_f, 2 * half, piece)],
        name="mix_16",
    )
    a_done1, far, small = sync(a_done1, far, small)
    ffn_corner, a_done1 = moves.far(far), moves.give(a_done1, 1)
    small = small_step(small)
    ffn_corner, a_done1, small = sync(ffn_corner, a_done1, small)

    own_ffn = (Block(ffn_final), Block(near_a10_f, 2 * half, piece), Block(ffn_over), Block(ffn_corner))
    arrived = ((near_a10_f, half), (far_a10, 3 * half), (a_done1, 0), (a_done3, 0))
    attn_final, other_ffn = mix(a0.passed(3, *arrived), own_ffn, name="mix_18")
    if dp_size > 8:
        attn_final = over_rest(attn_final, dp_size)
    attn_final, other_ffn, small = sync(attn_final, other_ffn, small)
    attn_near, attn_over, other_ffn = moves.near(attn_final), moves.far(attn_final), moves.core(other_ffn)
    while flips:
        small = small_step(small)
    attn_near, attn_over, other_ffn, small = sync(attn_near, attn_over, other_ffn, small)

    attn_corner = moves.far(attn_near)

    def out(kernel, rows_in, own, other, outs, name):
        refs = Refs()
        layout = tuple(refs.add(block) for block in parts(own, other))
        return call(
            functools.partial(kernel, rows_in, layout, len(refs.arrays)),
            [(array, VMEM) for array in refs.arrays],
            outs,
            name=name,
        )

    outs = [shape(model, hidden), shape(hidden, model)]
    grad_w_in, grad_w_back = out(ffn_out_kernel, piece, own_ffn, other_ffn, outs, "ffn_out")
    attn_corner, grad_w_in, grad_w_back, small = sync(attn_corner, grad_w_in, grad_w_back, small)
    own_attn = tuple(map(Block, (attn_final, attn_near, attn_over, attn_corner)))
    (other_attn,) = mix(own_attn, name="mix_17")
    other_attn = moves.core(other_attn)
    attn_grads = out(attn_out_kernel, half, own_attn, other_attn, [shape(width, model)] * 4, "attn_out")
    grad_w_query, grad_w_key, grad_w_value = (v.T for v in attn_grads[:3])
    my_in = lax.dynamic_index_in_dim(small, 8 + rank, keepdims=False)
    my_attn = lax.dynamic_index_in_dim(small, 8 + group + rank, keepdims=False)
    return (
        layer_out,
        grad_input,
        small[6],
        grad_w_query,
        my_attn[:width],
        grad_w_key,
        grad_w_value,
        my_attn[width : 2 * width],
        attn_grads[3],
        small[5],
        small[3],
        small[4],
        grad_w_in,
        my_in,
        grad_w_back,
        small[2],
        small[0],
        small[1],
    )


def solution(mesh):
    rows = P(("dp", "tensor"), None)
    placed = (
        rows,
        P("dp"),
        P("dp"),
        P("dp"),
        P(),
        P(None, "tensor"),
        P("tensor"),
        P(None, "tensor"),
        P(None, "tensor"),
        P("tensor"),
        P("tensor", None),
        P(),
        P(),
        P(),
        P(None, "tensor"),
        P("tensor"),
        P("tensor", None),
        P(),
        P(),
        P(),
        rows,
    )
    return jax.shard_map(
        on_device,
        mesh=mesh,
        in_specs=placed,
        out_specs=(
            rows,
            rows,
            P(),
            P(None, "tensor"),
            P("tensor"),
            P(None, "tensor"),
            P(None, "tensor"),
            P("tensor"),
            P("tensor", None),
            P(),
            P(),
            P(),
            P(None, "tensor"),
            P("tensor"),
            P("tensor", None),
            P(),
            P(),
            P(),
        ),
        check_vma=False,
    )
```

```python
import functools

import jax
import jax.numpy as jnp
from jax import lax
from jax.experimental import pallas as pl
from jax.experimental.pallas import tpu as pltpu
from jax.sharding import PartitionSpec as P

HEAD_DIM = 64
EPSILON = 1e-05
MASKED = -1000000000.0
AXES = ("dp", "tensor")
BF = jnp.bfloat16
F32 = jnp.float32
MIB = 1024 * 1024
BIAS_ROWS = 16


class Moves:
    def __init__(self, dp_size, group):
        self.dp_size, self.group = dp_size, group

    def build(self, value, source):
        pairs = []
        for d in range(self.dp_size):
            for t in range(self.group):
                sd, st = source(d, t)
                pairs.append((sd * self.group + st, d * self.group + t))
        return lax.ppermute(value, AXES, pairs)

    def core(self, value):
        return self.build(value, lambda d, t: (d ^ 1, t))

    def near(self, value):
        return self.build(value, lambda d, t: (d ^ (4 if d & 1 else 2), t))

    def far(self, value):
        return self.build(value, lambda d, t: (d ^ (2 if d & 1 else 4), t))

    def fetch(self, value, turn):
        return self.build(value, lambda d, t: (d, (t + turn) % self.group))

    def pass_on(self, value):
        return self.build(value, lambda d, t: (d, (t + (-1 if d & 1 else 1)) % self.group))

    def hand_on(self, value):
        return self.build(value, lambda d, t: (d, (t + (1 if d & 1 else -1)) % self.group))

    def give(self, value, turn):
        return self.build(value, lambda d, t: (d, (t - turn) % self.group))

    def flip(self, value, mask_dp, mask_t):
        return self.build(value, lambda d, t: (d ^ mask_dp, t ^ mask_t))


def after(value, *first):
    return lax.optimization_barrier((value, *first))[0]


def over_rest(values, dp_size):
    groups = [list(range(i, dp_size, 8)) for i in range(8)]
    return lax.psum(values.astype(F32), "dp", axis_index_groups=groups).astype(BF)


def sync(*values):
    return lax.optimization_barrier(values)


def gather_places(core, chip):
    near, over = chip ^ (1 + core), chip ^ (2 - core)
    own = ((core, chip), (core, near), (core, over), (core, chip ^ 3))
    return own + ((1 - core, chip), (1 - core, over), (1 - core, near), (1 - core, chip ^ 3))


class Block:
    def __init__(self, array, row=0, rows=None):
        self.array, self.row = array, row
        self.rows = array.shape[0] - row if rows is None else rows

    def at(self, row, rows):
        return Block(self.array, self.row + row, rows)


class Refs:
    def __init__(self):
        self.arrays = []

    def add(self, block):
        for index, array in enumerate(self.arrays):
            if array is block.array:
                return index, block.row
        self.arrays.append(block.array)
        return len(self.arrays) - 1, block.row


def dot_nn(left, right):
    return jnp.dot(left, right, preferred_element_type=F32)


def dot_nt(left, right):
    return lax.dot_general(left, right, (((1,), (1,)), ((), ())), preferred_element_type=F32)


def dot_tn(left, right):
    return lax.dot_general(left, right, (((0,), (0,)), ((), ())), preferred_element_type=F32)


def row_sum(values):
    return jnp.sum(values, axis=0, keepdims=True)


def where_am_i():
    dp = lax.axis_index("dp")
    return dp & 1, (dp >> 1) & 3


def copy_in(refs, layout, rows, out_ref, sems, place):
    started = []
    for index, ((part, where), (array, row)) in enumerate(zip(gather_places(*where_am_i()), layout)):
        start = pl.multiple_of(place(part, where), rows)
        copy = pltpu.make_async_copy(
            refs[array].at[pl.ds(row, rows)], out_ref.at[pl.ds(start, rows)], sems.at[index]
        )
        copy.start()
        started.append(copy)
    return started


def attn_place(rows):
    return lambda part, where: (2 * where + part) * rows


def ffn_place(rows):
    return lambda part, where: (part * 4 + where) * rows


def scatter_out(source_ref, rows, kept_ref, given_ref, base, place):
    core, chip = where_am_i()
    for ref, mine, first in ((kept_ref, core, 0), (given_ref, 1 - core, base)):
        for slot, where in enumerate((chip ^ (1 + mine), chip ^ (2 - mine), chip ^ 3, chip)):
            start = pl.multiple_of(place(mine, where), rows)
            begin = first + slot * rows
            ref[begin : begin + rows, :] = source_ref[pl.ds(start, rows), :]


def block_of(values, chain, head, seq):
    return values[head * HEAD_DIM : (head + 1) * HEAD_DIM, chain * seq : (chain + 1) * seq]


def attend(width, seq, lengths, mixed, mats, bias, qkv, soft, ctx):
    chains = mixed.shape[0] // seq
    heads = width // HEAD_DIM
    base = lax.axis_index("tensor") * chains
    column = jnp.broadcast_to(bias, (8, bias.shape[1])).T[:, :1]
    scale = HEAD_DIM**-0.5
    parts = []
    for index in range(3):
        cut = slice(index * width, (index + 1) * width)
        values = dot_nt(mats[index], mixed)
        if index != 1:
            values = values + column[cut]
        parts.append(values.astype(BF))
    scaled = (parts[0].astype(F32) * scale).astype(BF)
    for index, values in enumerate((scaled, parts[1], parts[2])):
        qkv[index * width : (index + 1) * width, :] = values
    position = lax.broadcasted_iota(jnp.int32, (seq, 1), 0)
    blocks = [(chain, head) for chain in range(chains) for head in range(heads)]
    scores = [
        jnp.where(
            position < lengths[base + chain],
            dot_tn(block_of(parts[1], chain, head, seq), block_of(scaled, chain, head, seq)),
            MASKED,
        )
        for chain, head in blocks
    ]
    shifted = [jnp.exp(value - jnp.max(value, axis=0, keepdims=True)) for value in scores]
    weights = [(value * (1.0 / row_sum(value))).astype(BF) for value in shifted]
    for index, (chain, head) in enumerate(blocks):
        soft[index] = weights[index]
        ctx[head * HEAD_DIM : (head + 1) * HEAD_DIM, chain * seq : (chain + 1) * seq] = dot_nn(
            block_of(parts[2], chain, head, seq), weights[index]
        ).astype(BF)
    return dot_tn(ctx[...], mats[3])


def norm_back(grad, hat, inv, gain):
    scaled = grad * gain
    mean_one = jnp.mean(scaled, axis=1, keepdims=True)
    mean_two = jnp.mean(scaled * hat, axis=1, keepdims=True)
    return inv * (scaled - mean_one - hat * mean_two)


def norm_parts(values):
    centred = values - jnp.mean(values, axis=1, keepdims=True)
    inv = lax.rsqrt(jnp.mean(centred * centred, axis=1, keepdims=True) + EPSILON)
    return centred * inv, inv


def in_span(starts, counts, chain, chains, seq):
    index = lax.axis_index("tensor") * chains + chain
    position = lax.broadcasted_iota(jnp.int32, (seq, 1), 0)
    return (position >= starts[index]) & (position < starts[index] + counts[index])


EMBED, B_OUT, G_ATTN, S_ATTN, B_BACK, G_FFN, S_FFN = range(7)


def prep_kernel(width, half, b_in, b_query, b_value, wq, wk, wv, wo, attn_mine, bias, rows, sems):
    core, chip = where_am_i()
    for index, ref in enumerate((wq, wk, wv, wo)):
        start = pl.multiple_of(core * half, half)
        copy = pltpu.make_async_copy(
            ref.at[pl.ds(start, half)], attn_mine.at[pl.ds(0, half)], sems.at[0]
        )
        pl.when(chip == index)(copy.start)
    as_row = lambda ref: ref[...].astype(F32).reshape(1, -1)
    rows[...] = jnp.zeros_like(rows)
    rows[0:1, :] = as_row(b_in)
    rows[1:2, :width] = as_row(b_query)
    rows[1:2, 2 * width : 3 * width] = as_row(b_value)
    bias[...] = rows[...].astype(BF)
    copy.wait()
    attn_mine[half : half + BIAS_ROWS, :] = rows[...].astype(BF)


def more_kernel(piece, *refs):
    vectors = refs[:7]
    w_in, w_back, ffn_mine, vecs, sems = refs[7:]
    core, chip = where_am_i()
    for index, ref in enumerate((w_in, w_back)):
        start = pl.multiple_of(chip * piece, piece)
        copy = pltpu.make_async_copy(ref.at[pl.ds(start, piece)], ffn_mine, sems.at[0])
        pl.when(core == index)(copy.start)
    for index, ref in enumerate(vectors):
        vecs[index : index + 1, :] = ref[...].astype(F32).reshape(1, -1)
    vecs[7:8, :] = jnp.zeros((1, vecs.shape[1]), F32)
    copy.wait()


def pick_kernel(own, other, out):
    core, _ = where_am_i()

    @pl.when(core == 0)
    def _():
        out[...] = own[...]

    @pl.when(core == 1)
    def _():
        out[...] = other[...]


def attn_own_kernel(
    width, seq, lengths, starts, counts, hidden, vecs, bias, wq, wk, wv, wo, mixed, qkv, soft, ctx, part
):
    chains = hidden.shape[0] // seq
    for chain in range(chains):
        rows = slice(chain * seq, (chain + 1) * seq)
        span = in_span(starts, counts, chain, chains, seq)
        mixed[rows, :] = jnp.where(span, vecs[EMBED : EMBED + 1, :], hidden[rows, :].astype(F32)).astype(BF)
    mats = (wq[...], wk[...], wv[...], wo[...])
    part[...] = attend(
        width, seq, lengths, mixed[...], mats, bias[1:2, :].astype(F32), qkv, soft, ctx
    )


def attn_mats(mats, width):
    return [mats[i * width : (i + 1) * width, :] for i in range(4)]


def attn_turn_kernel(width, seq, layouts, last, part_rows, count, lengths, mixed, part, vecs, *refs):
    turns = len(layouts)
    firsts, refs = refs[:turns], refs[turns:]
    pieces, refs = refs[:count], refs[count:]
    results, refs = refs[: 5 * turns], refs[5 * turns :]
    all_sems = refs[-turns:]
    started = [
        copy_in(pieces, layouts[turn], part_rows, results[5 * turn + 4], all_sems[turn], attn_place(part_rows))
        for turn in range(turns)
    ]
    total = part[...]
    for turn in range(turns):
        qkv, soft, ctx, bias_in, mats = results[5 * turn : 5 * turn + 5]
        first = firsts[turn]
        bias_in[...] = jnp.broadcast_to(first[part_rows : part_rows + 1, :].astype(F32), bias_in.shape)
        for copy in started[turn]:
            copy.wait()
        bias = first[part_rows + 1 : part_rows + 2, :].astype(F32)
        total = total + attend(
            width, seq, lengths, mixed[...], attn_mats(mats, width), bias, qkv, soft, ctx
        )
    if not last:
        refs[0][...] = total
        return
    hat, inv, normed = refs[:3]
    ahat, ainv = norm_parts(total + mixed[...].astype(F32) + vecs[B_OUT : B_OUT + 1, :])
    hat[...] = ahat
    inv[...] = jnp.broadcast_to(ainv, inv.shape)
    normed[...] = (ahat * vecs[G_ATTN : G_ATTN + 1, :] + vecs[S_ATTN : S_ATTN + 1, :]).astype(BF)


def gelu_both(pre):
    cdf = 0.5 * (1.0 + lax.erf(pre * (0.5**0.5)))
    pdf = jnp.exp(-0.5 * pre * pre) * (0.5 / 3.141592653589793) ** 0.5
    return pre * cdf, cdf + pre * pdf


def ffn_step(normed, mat_in, mat_back, bias, act, slope):
    pre = dot_nn(normed[...], mat_in) + bias
    value, rate = gelu_both(pre)
    act[...] = value.astype(BF)
    slope[...] = rate.astype(BF)
    return dot_nn(act[...], mat_back)


def ffn_own_kernel(normed, mat_in, mat_back, bias, act, slope, total):
    total[...] = ffn_step(
        normed, mat_in[...], mat_back[...], bias[0:1, :].astype(F32), act, slope
    )


def ffn_rest_kernel(part_rows, layout, last, count, normed, part, bias_in, *refs):
    if last:
        (hat1, vecs, cot), refs = refs[:3], refs[3:]
    pieces, refs = refs[:count], refs[count:]
    act, slope, mats = refs[:3]
    sems = refs[-1]
    copies = copy_in(pieces, layout, part_rows, mats, sems, ffn_place(part_rows))
    height = 4 * part_rows
    for copy in copies:
        copy.wait()
    value = part[...] + ffn_step(
        normed, mats[:height, :], mats[height:, :], bias_in[0:1, :], act, slope
    )
    if not last:
        refs[3][...] = value
        return
    layer_out, grad_second, grad_low, small = refs[3:7]
    first = hat1[...] * vecs[G_ATTN : G_ATTN + 1, :] + vecs[S_ATTN : S_ATTN + 1, :]
    hat, inv = norm_parts(first + value + vecs[B_BACK : B_BACK + 1, :])
    gain = vecs[G_FFN : G_FFN + 1, :]
    layer_out[...] = (hat * gain + vecs[S_FFN : S_FFN + 1, :]).astype(BF)
    grad = cot[...].astype(F32)
    back = norm_back(grad, hat, inv, gain)
    grad_second[...] = back
    grad_low[...] = back.astype(BF)
    small[0:1, :] = row_sum(grad * hat)
    small[1:2, :] = row_sum(grad)
    small[2:3, :] = row_sum(back)
    small[3:, :] = jnp.zeros_like(small[3:, :])


def ffn_back_kernel(counts, part_rows, grad_low, normed, part, *refs):
    turns = []
    for count in counts:
        act, slope, *mats = refs[: 2 + count]
        refs = refs[2 + count :]
        turns.append((act, slope, mats))
    kepts, refs = refs[: len(turns)], refs[len(turns) :]
    given, total, bias_grad, whole = refs
    height = 4 * part_rows
    value = part[...]
    bias_grad[...] = jnp.zeros_like(bias_grad)
    for index, (act, slope, mats) in enumerate(turns):
        if len(mats) == 2:
            mat_in, mat_back = mats[0][...], mats[1][...]
        else:
            mat_in, mat_back = mats[0][:height, :], mats[0][height:, :]
        whole[height:, :] = dot_tn(act[...], grad_low[...]).astype(BF)
        grad_act = dot_nt(grad_low[...], mat_back)
        grad_pre = (grad_act * slope[...].astype(F32)).astype(BF)
        bias_grad[index : index + 1, :] = row_sum(grad_pre.astype(F32))
        whole[:height, :] = dot_tn(normed[...], grad_pre).astype(BF)
        value = value + dot_nt(grad_pre, mat_in)
        base = index * 4 * part_rows
        scatter_out(whole, part_rows, kepts[index], given, base, ffn_place(part_rows))
    total[...] = value


def attend_back(width, seq, grad_low, mats, mixed, qkv, soft, ctx, grad_qkv, whole):
    chains = grad_low.shape[0] // seq
    heads = width // HEAD_DIM
    scale = HEAD_DIM**-0.5
    whole[3 * width :, :] = dot_nn(ctx[...], grad_low).astype(BF)
    grad_ctx = dot_nt(mats[3], grad_low).astype(BF)
    queries, keys, values = (qkv[i * width : (i + 1) * width, :] for i in range(3))
    blocks = [(chain, head) for chain in range(chains) for head in range(heads)]
    grad_weights = [
        dot_tn(block_of(values, chain, head, seq), block_of(grad_ctx, chain, head, seq))
        for chain, head in blocks
    ]
    grad_scores = []
    for index, value in enumerate(grad_weights):
        wide = soft[index].astype(F32)
        product = wide * value
        grad_scores.append((product - wide * row_sum(product)).astype(BF))
    for index, (chain, head) in enumerate(blocks):
        columns = slice(chain * seq, (chain + 1) * seq)
        for slot, value in enumerate(
            (
                dot_nn(block_of(keys, chain, head, seq), grad_scores[index]) * scale,
                dot_nt(block_of(queries, chain, head, seq), grad_scores[index]),
                dot_nt(block_of(grad_ctx, chain, head, seq), soft[index]),
            )
        ):
            start = slot * width + head * HEAD_DIM
            grad_qkv[start : start + HEAD_DIM, columns] = value.astype(BF)
    whole[: 3 * width, :] = dot_nn(grad_qkv[...], mixed).astype(BF)
    ones = jnp.ones((8, grad_low.shape[0]), BF)
    back = dot_tn(grad_qkv[:width, :], mats[0])
    back = back + dot_tn(grad_qkv[width : 2 * width, :], mats[1])
    back = back + dot_tn(grad_qkv[2 * width :, :], mats[2])
    return back, dot_nt(ones, grad_qkv[...])


def attn_back_kernel(width, seq, own, first, part_rows, counts, mixed, part, *refs):
    if first:
        (hat, inv, vecs), refs = refs[:3], refs[3:]
    else:
        (grad_low,), refs = refs[:1], refs[1:]
    if own:
        (starts, counts_ref), refs = refs[:2], refs[2:]
    turns = []
    for count in counts:
        qkv, soft, ctx, *mats = refs[: 3 + count]
        refs = refs[3 + count :]
        turns.append((qkv, soft, ctx, mats))
    kepts, refs = refs[: len(turns)], refs[len(turns) :]
    given, total, bias_grad = refs[:3]
    refs = refs[3:]
    if first:
        (grad_low, small), refs = refs[:2], refs[2:]
    grad_qkv, whole = refs
    if first:
        grad = part[...]
        value = norm_back(grad, hat[...], inv[:, :1], vecs[G_ATTN : G_ATTN + 1, :])
        grad_low[...] = value.astype(BF)
        small[0:1, :] = row_sum(grad * hat[...])
        small[1:2, :] = row_sum(grad)
        small[2:3, :] = row_sum(value)
        small[3:, :] = jnp.zeros_like(small[3:, :])
    else:
        value = part[...]
    bias_grad[...] = jnp.zeros_like(bias_grad)
    for index, (qkv, soft, ctx, refs_in) in enumerate(turns):
        mats = [ref[...] for ref in refs_in] if len(refs_in) == 4 else attn_mats(refs_in[0], width)
        back, sums = attend_back(
            width, seq, grad_low[...], mats, mixed[...], qkv, soft, ctx, grad_qkv, whole
        )
        value = value + back
        bias_grad[index : index + 1, :width] = sums[0:1, :width]
        bias_grad[index : index + 1, width : 2 * width] = sums[0:1, 2 * width :]
        base = index * 4 * part_rows
        scatter_out(whole, part_rows, kepts[index], given, base, attn_place(part_rows))
    if not own:
        total[...] = value
        return
    chains = value.shape[0] // seq
    embed_sum = jnp.zeros((1, value.shape[1]), F32)
    for chain in range(chains):
        rows = slice(chain * seq, (chain + 1) * seq)
        span = in_span(starts, counts_ref, chain, chains, seq)
        total[rows, :] = jnp.where(span, 0.0, value[rows, :]).astype(BF)
        embed_sum = embed_sum + row_sum(jnp.where(span, value[rows, :], 0.0))
    bias_grad[1:2, :] = embed_sum


def split_kernel(value, at_zero, at_one):
    core, _ = where_am_i()
    for index, out in enumerate((at_zero, at_one)):

        @pl.when(core == index)
        def _():
            out[...] = value[...]

        @pl.when(core != index)
        def _():
            out[...] = jnp.zeros_like(out)


def mix_kernel(count, plan, *refs):
    for out, blocks in zip(refs[count:], plan):
        start = 0
        for rows, sources in blocks:
            array, row = sources[0]
            value = refs[array][row : row + rows, :]
            if len(sources) > 1:
                value = value.astype(F32)
                for array, row in sources[1:]:
                    value = value + refs[array][row : row + rows, :].astype(F32)
                value = value.astype(BF)
            out[start : start + rows, :] = value
            start += rows


def ffn_out_kernel(part_rows, layout, count, *refs):
    outs = refs[count:]
    for (array, row), (part, where) in zip(layout, gather_places(*where_am_i())):
        start = pl.multiple_of(where * part_rows, part_rows)
        for index in range(2):

            @pl.when(part == index)
            def _():
                block = refs[array][row : row + part_rows, :]
                outs[index][pl.ds(start, part_rows), :] = block.astype(F32)


def attn_out_kernel(part_rows, layout, count, *refs):
    outs = refs[count:]
    for (array, row), (part, where) in zip(layout, gather_places(*where_am_i())):
        start = pl.multiple_of(part * part_rows, part_rows)
        for index in range(4):

            @pl.when(where == index)
            def _():
                block = refs[array][row : row + part_rows, :]
                outs[index][pl.ds(start, part_rows), :] = block.astype(F32)


def small_kernel(group, rows_of, small_ffn, small_attn, *refs):
    out = refs[-1]
    rank = lax.axis_index("tensor")
    out[...] = jnp.zeros_like(out)
    out[0:3, :] = small_ffn[0:3, :]
    out[3:6, :] = small_attn[0:3, :]
    for index, (array, source) in enumerate(rows_of[:-1]):
        row = 8 + index // group * group + lax.rem(index % group + rank, group)
        out[pl.ds(row, 1), :] = refs[array][source : source + 1, :]
    array, source = rows_of[-1]
    out[6:7, :] = refs[array][source : source + 1, :]


SMEM = pl.BlockSpec(memory_space=pltpu.SMEM)
VMEM = pl.BlockSpec(memory_space=pltpu.VMEM)
ANY = pl.BlockSpec(memory_space=pl.ANY)


def call(kernel, ins, outs, scratch=(), flops=0, vmem=16, name=None):
    arrays = [array for array, _ in ins]
    moved = sum(a.size * a.dtype.itemsize for a in arrays) + sum(
        o.size * o.dtype.itemsize for o in outs
    )
    return pl.pallas_call(
        kernel,
        in_specs=[spec for _, spec in ins],
        out_specs=[VMEM] * len(outs),
        out_shape=list(outs),
        scratch_shapes=list(scratch),
        compiler_params=pltpu.CompilerParams(vmem_limit_bytes=vmem * MIB),
        cost_estimate=pl.CostEstimate(flops=flops // 100, bytes_accessed=moved // 100, transcendentals=0),
        name=name,
    )(*arrays)


def shape(rows, columns, kind=F32):
    return jax.ShapeDtypeStruct((rows, columns), kind)


def pick(own, other):
    return call(
        pick_kernel,
        [(own, VMEM), (other, VMEM)],
        [shape(*own.shape, own.dtype)],
        vmem=4,
        name="pick",
    )[0]


def split(value):
    return call(
        split_kernel,
        [(value, VMEM)],
        [shape(*value.shape, value.dtype)] * 2,
        vmem=4,
        name="split",
    )


def mix(*outs, first=(), name=None):
    refs, plan, shapes = Refs(), [], []
    for blocks in outs:
        mine = []
        for block in blocks:
            sources = block if isinstance(block, list) else [block]
            mine.append((sources[0].rows, tuple(refs.add(source) for source in sources)))
        plan.append(tuple(mine))
        top = blocks[0][0] if isinstance(blocks[0], list) else blocks[0]
        shapes.append(shape(sum(rows for rows, _ in mine), top.array.shape[1], BF))
    if first:
        refs.arrays[0] = after(refs.arrays[0], *first)
    return call(
        functools.partial(mix_kernel, len(refs.arrays), tuple(plan)),
        [(array, VMEM) for array in refs.arrays],
        shapes,
        vmem=4,
        name=name,
    )


def on_device(
    hidden_in,
    lengths,
    span_start,
    span_len,
    mask_embed,
    w_query,
    b_query,
    w_key,
    w_value,
    b_value,
    w_out,
    b_out,
    g_attn,
    s_attn,
    w_in,
    b_in,
    w_back,
    b_back,
    g_ffn,
    s_ffn,
    cotangent,
):
    group = lax.axis_size("tensor")
    dp_size = lax.axis_size("dp")
    moves = Moves(dp_size, group)
    rank = lax.axis_index("tensor")
    rows, model = hidden_in.shape
    seq = rows * group // lengths.shape[0]
    chains = rows // seq
    width = w_query.shape[1]
    heads = width // HEAD_DIM
    hidden = w_in.shape[1]
    piece = model // 4
    half = piece // 2
    turns = (1, 3, 2)
    count = len(turns)

    own_mats = (w_query.T, w_key.T, w_value.T, w_out)
    dma = lambda n: pltpu.SemaphoreType.DMA((8 * n,))

    attn_mine, bias_pack = call(
        functools.partial(prep_kernel, width, half),
        [(v, VMEM) for v in (b_in, b_query, b_value)] + [(v, ANY) for v in own_mats],
        [shape(half + BIAS_ROWS, model, BF), shape(BIAS_ROWS, model, BF)],
        [pltpu.VMEM((BIAS_ROWS, model), F32), pltpu.SemaphoreType.DMA((1,))],
        vmem=60,
        name="prep",
    )
    ffn_mine, vecs = call(
        functools.partial(more_kernel, piece),
        [(v, VMEM) for v in (mask_embed, after(b_out, attn_mine), g_attn, s_attn, b_back, g_ffn, s_ffn)]
        + [(v, ANY) for v in (w_in, w_back)],
        [shape(piece, model, BF), shape(8, model)],
        [pltpu.SemaphoreType.DMA((1,))],
        vmem=60,
        name="more",
    )
    first1, first3 = (moves.fetch(attn_mine, turn) for turn in turns[:2])

    soft_shape = jax.ShapeDtypeStruct((chains * heads, seq, seq), BF)
    turn_flops = 2 * rows * model * 4 * width
    mixed, qkv_own, soft_own, ctx_own, attn_part = call(
        functools.partial(attn_own_kernel, width, seq),
        [(v, SMEM) for v in (lengths, span_start, span_len)]
        + [(v, VMEM) for v in (hidden_in, vecs, bias_pack, *own_mats)],
        [
            shape(rows, model, BF),
            shape(3 * width, rows, BF),
            soft_shape,
            shape(width, rows, BF),
            shape(rows, model),
        ],
        flops=turn_flops,
        name="attn_own",
    )
    first1, first3, mixed, attn_mine, ffn_mine = sync(first1, first3, mixed, attn_mine, ffn_mine)
    first2 = moves.pass_on(pick(first1, first3))
    (mine13,) = mix([Block(first1, 0, half), Block(first3, 0, half)], name="mix_1")
    near13, over13 = moves.near(mine13), moves.far(mine13)

    first2, near13, over13, ffn_mine = sync(first2, near13, over13, ffn_mine)
    ffn1 = moves.fetch(ffn_mine, 1)
    mine2, far = mix([Block(first2, 0, half)], [Block(near13), Block(first2, 0, half)], name="mix_2")
    near2, far13_2 = moves.near(mine2), moves.far(far)

    ffn1, near2, far13_2, ffn_mine = sync(ffn1, near2, far13_2, ffn_mine)
    ffn3 = moves.fetch(ffn_mine, 3)
    own13 = (Block(mine13), Block(near13), Block(over13), Block(far13_2, 0, 2 * half))
    far, other13 = mix([Block(near2), Block(ffn1)], own13, name="mix_3")
    near_f1, far2_f1, other13 = moves.near(ffn1), moves.far(far), moves.core(other13)

    ffn3, near_f1, far2_f1, other13, ffn_mine = sync(ffn3, near_f1, far2_f1, other13, ffn_mine)
    ffn2 = moves.pass_on(pick(ffn1, ffn3))
    own2 = (Block(mine2), Block(near2), Block(far13_2, 2 * half, half), Block(far2_f1, 0, half))
    far, other2 = mix([Block(near_f1), Block(ffn3)], own2, name="mix_4")
    near_f3, far_f1_f3, other2 = moves.near(ffn3), moves.far(far), moves.core(other2)

    def parts(own, other, turn=0, rows=None):
        rows = own[0].rows if rows is None else rows
        blocks = [block.at(turn * rows, rows) for block in own]
        count_turns = own[0].rows // rows
        return blocks + [Block(other, (i * count_turns + turn) * rows, rows) for i in range(4)]

    qkvs, softs, ctxs, bias_ins, attn_wholes = [], [], [], [], []
    for last, firsts in ((False, (first1, first3)), (True, (first2,))):
        if last:
            ffn2, near_f3, far_f1_f3, other2, attn_part = sync(ffn2, near_f3, far_f1_f3, other2, attn_part)
            own_f1 = (Block(ffn1), Block(near_f1), Block(far2_f1, half, piece), Block(far_f1_f3, 0, piece))
            far, other_f1 = mix([Block(near_f3), Block(ffn2)], own_f1, name="mix_5")
            near_f2, far_f3_f2, other_f1 = moves.near(ffn2), moves.far(far), moves.core(other_f1)
        refs = Refs()
        layouts = []
        for index in range(len(firsts)):
            blocks = parts(own2, other2) if last else parts(own13, other13, index, half)
            layouts.append(tuple(refs.add(block) for block in blocks))
        outs = [
            shape(3 * width, rows, BF),
            soft_shape,
            shape(width, rows, BF),
            shape(8, model),
            shape(model, model, BF),
        ] * len(firsts)
        outs += [shape(rows, model)]
        if last:
            outs += [shape(rows, 128), shape(rows, model, BF)]
        results = call(
            functools.partial(attn_turn_kernel, width, seq, tuple(layouts), last, half, len(refs.arrays)),
            [(lengths, SMEM), (mixed, VMEM), (attn_part, VMEM), (vecs, VMEM)]
            + [(first, VMEM) for first in firsts]
            + [(array, ANY) for array in refs.arrays],
            outs,
            [dma(1)] * len(firsts),
            flops=len(firsts) * turn_flops,
            name="attn_2" if last else "attn_13",
        )
        for index in range(len(firsts)):
            for values, value in zip(
                (qkvs, softs, ctxs, bias_ins, attn_wholes), results[5 * index : 5 * index + 5]
            ):
                values.append(value)
        others = results[5 * len(firsts) :]
        attn_part = others[0]
    hat1, inv1, normed = others

    ffn_flops = 2 * rows * model * hidden * 2
    act_own, slope_own, ffn_part = call(
        ffn_own_kernel,
        [(normed, VMEM), (w_in, VMEM), (w_back, VMEM), (bias_pack, VMEM)],
        [shape(rows, hidden, BF), shape(rows, hidden, BF), shape(rows, model)],
        flops=ffn_flops,
        name="ffn_own",
    )
    near_f2, far_f3_f2, other_f1, ffn_part = sync(near_f2, far_f3_f2, other_f1, ffn_part)
    own_f3 = (Block(ffn3), Block(near_f3), Block(far_f1_f3, piece, piece), Block(far_f3_f2, 0, piece))
    (other_f3,) = mix(own_f3, name="mix_6")
    far_f2, other_f3 = moves.far(near_f2), moves.core(other_f3)
    acts, slopes, ffn_wholes = [], [], []
    for index in range(count):
        last = index == count - 1
        if index == 0:
            blocks = parts(own_f1, other_f1)
        elif index == 1:
            far_f2, other_f3, ffn_part = sync(far_f2, other_f3, ffn_part)
            own_f2 = (Block(ffn2), Block(near_f2), Block(far_f3_f2, piece, piece), Block(far_f2))
            (other_f2,) = mix(own_f2, name="mix_7")
            other_f2 = moves.core(other_f2)
            blocks = parts(own_f3, other_f3)
        else:
            blocks = parts(own_f2, other_f2)
        refs = Refs()
        layout = tuple(refs.add(block) for block in blocks)
        ins = [(normed, VMEM), (ffn_part, VMEM), (bias_ins[index], VMEM)]
        outs = [shape(rows, hidden, BF)] * 2 + [shape(2 * model, model, BF)]
        if last:
            ins += [(hat1, VMEM), (vecs, VMEM), (cotangent, VMEM)]
            outs += [shape(rows, model, BF), shape(rows, model), shape(rows, model, BF), shape(8, model)]
        else:
            outs += [shape(rows, model)]
        act, slope, whole, *others = call(
            functools.partial(ffn_rest_kernel, piece, layout, last, len(refs.arrays)),
            ins + [(array, ANY) for array in refs.arrays],
            outs,
            [dma(1)],
            flops=ffn_flops,
            name=f"ffn_{turns[index]}",
        )
        for values, value in zip((acts, slopes, ffn_wholes), (act, slope, whole)):
            values.append(value)
        if last:
            layer_out, grad_second, grad_low, small_ffn = others
        else:
            (ffn_part,) = others

    def ffn_back(part, *turns_in, name):
        kinds = tuple(len(turn) - 2 for turn in turns_in)
        *kepts, given, part, bias = call(
            functools.partial(ffn_back_kernel, kinds, piece),
            [(v, VMEM) for v in (grad_low, normed, part)] + [(v, VMEM) for turn in turns_in for v in turn],
            [shape(4 * piece, model, BF)] * len(kinds)
            + [shape(4 * len(kinds) * piece, model, BF), shape(rows, model), shape(8, model)],
            [pltpu.VMEM((2 * model, model), BF)],
            flops=2 * len(kinds) * ffn_flops,
            name=name,
        )
        return kepts, given, part, bias

    def attn_back(part, grad_low, *turns_in, own=False, name):
        first = grad_low is None
        kinds = tuple(len(turn) - 3 for turn in turns_in)
        ins = [(mixed, VMEM), (part, VMEM)]
        ins += [(v, VMEM) for v in (hat1, inv1, vecs)] if first else [(grad_low, VMEM)]
        if own:
            ins += [(span_start, SMEM), (span_len, SMEM)]
        ins += [(v, VMEM) for turn in turns_in for v in turn]
        outs = [shape(4 * half, model, BF)] * len(kinds)
        outs += [shape(4 * len(kinds) * half, model, BF)]
        outs += [shape(rows, model, BF if own else F32), shape(8, model)]
        if first:
            outs += [shape(rows, model, BF), shape(8, model)]
        return call(
            functools.partial(attn_back_kernel, width, seq, own, first, half, kinds),
            ins,
            outs,
            [pltpu.VMEM((3 * width, rows), BF), pltpu.VMEM((model, model), BF)],
            flops=2 * len(kinds) * turn_flops,
            name=name,
        )

    def ffn_turn(index):
        return (acts[index], slopes[index], ffn_wholes[index])

    def attn_turn(index):
        return (qkvs[index], softs[index], ctxs[index], attn_wholes[index])

    class Slots:
        def __init__(self, kept, come, row=0, more=()):
            self.rows = kept.shape[0] // 4
            self.pieces = [(kept, 0), (come, row), *more]

        def slot(self, index):
            start = index * self.rows
            return [Block(array, row + start, self.rows) for array, row in self.pieces]

        def passed(self, index, *arrived):
            return [self.slot(index) + [Block(array, row, self.rows) for array, row in arrived]]

    (kept2,), given2, part, bias2 = ffn_back(grad_second, ffn_turn(2), name="ffn_back_2")
    come2 = moves.core(given2)
    (kept1,), given1, part, bias1 = ffn_back(part, ffn_turn(0), name="ffn_back_1")
    come2, given1, part = sync(come2, given1, part)

    f2 = Slots(kept2, come2)
    (far,) = mix([f2.slot(2), f2.slot(1)], name="mix_8")
    far, part, given1 = sync(far, part, given1)
    far_f2, come1 = moves.far(far), moves.core(given1)
    (kept3, kept0), given30, part, bias30 = ffn_back(
        part, ffn_turn(1), (act_own, slope_own, w_in, w_back), name="ffn_back_30"
    )
    far_f2, come1, given30, part = sync(far_f2, come1, given30, part)

    f1 = Slots(kept1, come1)
    near, far = mix(f2.passed(0, (far_f2, 0)), [f1.slot(2), f1.slot(1)], name="mix_9")
    near, far, given30, part = sync(near, far, given30, part)
    near_f2, far_f1, come30 = moves.near(near), moves.far(far), moves.core(given30)
    a_kept2, a_kept3, a_given23, part, a_bias23, attn_low, small_attn = attn_back(
        part, None, attn_turn(2), attn_turn(1), name="attn_back_23"
    )
    near_f2, far_f1, come30, a_given23, part = sync(near_f2, far_f1, come30, a_given23, part)

    f3, f0 = Slots(kept3, come30), Slots(kept0, come30, 4 * piece)
    done2, near, far = mix(
        f2.passed(3, (near_f2, 0), (far_f2, piece)),
        f1.passed(0, (far_f1, 0)),
        [f3.slot(2), f3.slot(1)],
        name="mix_10",
    )
    done2, near, far, a_given23, part = sync(done2, near, far, a_given23, part)
    done2, near_f1, far_f3 = moves.hand_on(done2), moves.near(near), moves.far(far)
    a_come23 = moves.core(a_given23)
    a_kept1, a_given1, part, a_bias1 = attn_back(part, attn_low, attn_turn(0), name="attn_back_1")
    near_f1, far_f3, a_come23, done2, a_given1, part = sync(near_f1, far_f3, a_come23, done2, a_given1, part)

    for_one, for_three = split(done2)
    a2, a3 = Slots(a_kept2, a_come23), Slots(a_kept3, a_come23, 4 * half)
    done1, near, far = mix(
        f1.passed(3, (near_f1, 0), (far_f1, piece), (for_one, 0)),
        f3.passed(0, (far_f3, 0)),
        [a2.slot(2), a3.slot(2), a2.slot(1), a3.slot(1)],
        name="mix_11",
    )
    done1, near, far, a_given1, part = sync(done1, near, far, a_given1, part)
    done1, near_f3, far_a23 = moves.give(done1, 1), moves.near(near), moves.far(far)
    a_come1 = moves.core(a_given1)
    a_kept0, a_given0, grad_input, a_bias0 = attn_back(
        part, attn_low, (qkv_own, soft_own, ctx_own, *own_mats), own=True, name="attn_back_0"
    )
    near_f3, far_a23, a_come1, done1, a_given0, grad_input, a_bias0 = sync(
        near_f3, far_a23, a_come1, done1, a_given0, grad_input, a_bias0
    )

    a1 = Slots(a_kept1, a_come1)
    wide = piece + half
    done3, near, far = mix(
        f3.passed(3, (near_f3, 0), (far_f3, piece), (for_three, 0)),
        a2.passed(0, (far_a23, 0)) + a3.passed(0, (far_a23, half)),
        [f0.slot(2), a1.slot(2), f0.slot(1), a1.slot(1)],
        name="mix_12",
    )
    biases = (bias30, bias1, bias2, a_bias0, a_bias1, a_bias23)
    rows_of = ((0, 1), (1, 0), (2, 0), (0, 0), (3, 0), (4, 0), (5, 0), (5, 1), (3, 1))
    (small,) = call(
        functools.partial(small_kernel, group, rows_of),
        [(v, VMEM) for v in (small_ffn, small_attn, *biases)],
        [shape(8 + 2 * group, model)],
        vmem=4,
        name="small",
    )
    flips = [(1 << bit, 0) for bit in range(dp_size.bit_length() - 1)]
    flips += [(0, 1 << bit) for bit in range(group.bit_length() - 1)]

    def small_step(value):
        return value + moves.flip(value, *flips.pop(0))

    done3, near, far, a_given0, small = sync(done3, near, far, a_given0, small)
    done3, near_a23, far_f0_a1 = moves.give(done3, 3), moves.near(near), moves.far(far)
    a_come0 = moves.core(a_given0)
    small = small_step(small_step(small))
    done3, near_a23, far_f0_a1, a_come0, small = sync(done3, near_a23, far_f0_a1, a_come0, small)

    a0 = Slots(a_kept0, a_come0)
    a_done2, near, far = mix(
        a2.passed(3, (near_a23, 0), (far_a23, 2 * half)),
        f0.passed(0, (far_f0_a1, 0)) + a1.passed(0, (far_f0_a1, piece)),
        [a0.slot(2), a0.slot(1)],
        name="mix_13",
    )
    a_done2, near, far, small = sync(a_done2, near, far, small)
    a_done2, near_f0_a1, far_a0 = moves.hand_on(a_done2), moves.near(near), moves.far(far)
    small = small_step(small)
    a_done2, near_f0_a1, far_a0, small = sync(a_done2, near_f0_a1, far_a0, small)

    a_for_one, a_for_three = split(a_done2)
    arrived = ((near_f0_a1, 0), (far_f0_a1, wide), (done1, 0), (done3, 0))
    (ffn_final,) = mix(f0.passed(3, *arrived), name="mix_14")
    if dp_size > 8:
        ffn_final = over_rest(ffn_final, dp_size)
    a_done3, a_done1, near = mix(
        a3.passed(3, (near_a23, half), (far_a23, 3 * half), (a_for_three, 0)),
        a1.passed(3, (near_f0_a1, piece), (far_f0_a1, wide + piece), (a_for_one, 0)),
        a0.passed(0, (far_a0, 0)) + [Block(ffn_final)],
        name="mix_15",
    )
    ffn_final, near, a_done3, a_done1, small = sync(ffn_final, near, a_done3, a_done1, small)
    near_a0_f, ffn_over = moves.near(near), moves.far(ffn_final)
    a_done3, a_done1 = moves.give(a_done3, 3), moves.give(a_done1, 1)
    small = small_step(small)
    near_a0_f, ffn_over, a_done3, a_done1, small = sync(near_a0_f, ffn_over, a_done3, a_done1, small)

    arrived = ((near_a0_f, 0), (far_a0, half), (a_done1, 0), (a_done3, 0))
    (attn_final,) = mix(a0.passed(3, *arrived), name="mix_16")
    if dp_size > 8:
        attn_final = over_rest(attn_final, dp_size)
    (far,) = mix([Block(near_a0_f, half, piece), Block(attn_final)], name="mix_17")
    attn_final, far, small = sync(attn_final, far, small)
    attn_near, far_f_a = moves.near(attn_final), moves.far(far)
    small = small_step(small)
    attn_near, far_f_a, small = sync(attn_near, far_f_a, small)

    own_ffn = (Block(ffn_final), Block(near_a0_f, half, piece), Block(ffn_over), Block(far_f_a, 0, piece))
    (other_ffn,) = mix(own_ffn, name="mix_18")
    attn_near, other_ffn, small = sync(attn_near, other_ffn, small)
    other_ffn = moves.core(other_ffn)
    while flips:
        small = small_step(small)
    attn_corner = moves.far(attn_near)

    def out(kernel, rows_in, own, other, outs, name):
        refs = Refs()
        layout = tuple(refs.add(block) for block in parts(own, other))
        return call(
            functools.partial(kernel, rows_in, layout, len(refs.arrays)),
            [(array, VMEM) for array in refs.arrays],
            outs,
            name=name,
        )

    outs = [shape(model, hidden), shape(hidden, model)]
    grad_w_in, grad_w_back = out(ffn_out_kernel, piece, own_ffn, other_ffn, outs, "ffn_out")
    attn_corner, grad_w_in, grad_w_back, small = sync(attn_corner, grad_w_in, grad_w_back, small)
    own_attn = (Block(attn_final), Block(attn_near), Block(far_f_a, piece, half), Block(attn_corner))
    (other_attn,) = mix(own_attn, name="mix_17")
    other_attn = moves.core(other_attn)
    attn_grads = out(attn_out_kernel, half, own_attn, other_attn, [shape(width, model)] * 4, "attn_out")
    grad_w_query, grad_w_key, grad_w_value = (v.T for v in attn_grads[:3])
    my_in = lax.dynamic_index_in_dim(small, 8 + rank, keepdims=False)
    my_attn = lax.dynamic_index_in_dim(small, 8 + group + rank, keepdims=False)
    return (
        layer_out,
        grad_input,
        small[6],
        grad_w_query,
        my_attn[:width],
        grad_w_key,
        grad_w_value,
        my_attn[width : 2 * width],
        attn_grads[3],
        small[5],
        small[3],
        small[4],
        grad_w_in,
        my_in,
        grad_w_back,
        small[2],
        small[0],
        small[1],
    )


def solution(mesh):
    rows = P(("dp", "tensor"), None)
    placed = (
        rows,
        P("dp"),
        P("dp"),
        P("dp"),
        P(),
        P(None, "tensor"),
        P("tensor"),
        P(None, "tensor"),
        P(None, "tensor"),
        P("tensor"),
        P("tensor", None),
        P(),
        P(),
        P(),
        P(None, "tensor"),
        P("tensor"),
        P("tensor", None),
        P(),
        P(),
        P(),
        rows,
    )
    return jax.shard_map(
        on_device,
        mesh=mesh,
        in_specs=placed,
        out_specs=(
            rows,
            rows,
            P(),
            P(None, "tensor"),
            P("tensor"),
            P(None, "tensor"),
            P(None, "tensor"),
            P("tensor"),
            P("tensor", None),
            P(),
            P(),
            P(),
            P(None, "tensor"),
            P("tensor"),
            P("tensor", None),
            P(),
            P(),
            P(),
        ),
        check_vma=False,
    )
```

```python
import functools

import jax
import jax.numpy as jnp
from jax import lax
from jax.experimental import pallas as pl
from jax.experimental.pallas import tpu as pltpu
from jax.sharding import PartitionSpec as P

HEAD_DIM = 64
EPSILON = 1e-05
MASKED = -1000000000.0
AXES = ("dp", "tensor")
BF = jnp.bfloat16
F32 = jnp.float32
MIB = 1024 * 1024
BIAS_ROWS = 16


class Moves:
    def __init__(self, dp_size, group):
        self.dp_size, self.group = dp_size, group

    def build(self, value, source):
        pairs = []
        for d in range(self.dp_size):
            for t in range(self.group):
                sd, st = source(d, t)
                pairs.append((sd * self.group + st, d * self.group + t))
        return lax.ppermute(value, AXES, pairs)

    def core(self, value):
        return self.build(value, lambda d, t: (d ^ 1, t))

    def near(self, value):
        return self.build(value, lambda d, t: (d ^ (4 if d & 1 else 2), t))

    def far(self, value):
        return self.build(value, lambda d, t: (d ^ (2 if d & 1 else 4), t))

    def fetch(self, value, turn):
        return self.build(value, lambda d, t: (d, (t + turn) % self.group))

    def pass_on(self, value):
        return self.build(value, lambda d, t: (d, (t + (-1 if d & 1 else 1)) % self.group))

    def hand_on(self, value):
        return self.build(value, lambda d, t: (d, (t + (1 if d & 1 else -1)) % self.group))

    def give(self, value, turn):
        return self.build(value, lambda d, t: (d, (t - turn) % self.group))

    def flip(self, value, mask_dp, mask_t):
        return self.build(value, lambda d, t: (d ^ mask_dp, t ^ mask_t))


def after(value, *first):
    return lax.optimization_barrier((value, *first))[0]


def over_rest(values, dp_size):
    groups = [list(range(i, dp_size, 8)) for i in range(8)]
    return lax.psum(values.astype(F32), "dp", axis_index_groups=groups).astype(BF)


def sync(*values):
    return lax.optimization_barrier(values)


def gather_places(core, chip):
    near, over = chip ^ (1 + core), chip ^ (2 - core)
    own = ((core, chip), (core, near), (core, over), (core, chip ^ 3))
    return own + ((1 - core, chip), (1 - core, over), (1 - core, near), (1 - core, chip ^ 3))


class Block:
    def __init__(self, array, row=0, rows=None):
        self.array, self.row = array, row
        self.rows = array.shape[0] - row if rows is None else rows

    def at(self, row, rows):
        return Block(self.array, self.row + row, rows)


class Refs:
    def __init__(self):
        self.arrays = []

    def add(self, block):
        for index, array in enumerate(self.arrays):
            if array is block.array:
                return index, block.row
        self.arrays.append(block.array)
        return len(self.arrays) - 1, block.row


def dot_nn(left, right):
    return jnp.dot(left, right, preferred_element_type=F32)


def dot_nt(left, right):
    return lax.dot_general(left, right, (((1,), (1,)), ((), ())), preferred_element_type=F32)


def dot_tn(left, right):
    return lax.dot_general(left, right, (((0,), (0,)), ((), ())), preferred_element_type=F32)


def row_sum(values):
    return jnp.sum(values, axis=0, keepdims=True)


def where_am_i():
    dp = lax.axis_index("dp")
    return dp & 1, (dp >> 1) & 3


def copy_in(refs, layout, rows, out_ref, sems, place):
    started = []
    for index, ((part, where), (array, row)) in enumerate(zip(gather_places(*where_am_i()), layout)):
        start = pl.multiple_of(place(part, where), rows)
        copy = pltpu.make_async_copy(
            refs[array].at[pl.ds(row, rows)], out_ref.at[pl.ds(start, rows)], sems.at[index]
        )
        copy.start()
        started.append(copy)
    return started


def attn_place(rows):
    return lambda part, where: (2 * where + part) * rows


def ffn_place(rows):
    return lambda part, where: (part * 4 + where) * rows


def scatter_out(source_ref, rows, kept_ref, given_ref, base, place):
    core, chip = where_am_i()
    for ref, mine, first in ((kept_ref, core, 0), (given_ref, 1 - core, base)):
        for slot, where in enumerate((chip ^ (1 + mine), chip ^ (2 - mine), chip ^ 3, chip)):
            start = pl.multiple_of(place(mine, where), rows)
            begin = first + slot * rows
            ref[begin : begin + rows, :] = source_ref[pl.ds(start, rows), :]


def block_of(values, chain, head, seq):
    return values[head * HEAD_DIM : (head + 1) * HEAD_DIM, chain * seq : (chain + 1) * seq]


def attend(width, seq, lengths, mixed, mats, bias, qkv, soft, ctx):
    chains = mixed.shape[0] // seq
    heads = width // HEAD_DIM
    base = lax.axis_index("tensor") * chains
    column = jnp.broadcast_to(bias, (8, bias.shape[1])).T[:, :1]
    scale = HEAD_DIM**-0.5
    parts = []
    for index in range(3):
        cut = slice(index * width, (index + 1) * width)
        values = dot_nt(mats[index], mixed)
        if index != 1:
            values = values + column[cut]
        parts.append(values.astype(BF))
    scaled = (parts[0].astype(F32) * scale).astype(BF)
    for index, values in enumerate((scaled, parts[1], parts[2])):
        qkv[index * width : (index + 1) * width, :] = values
    position = lax.broadcasted_iota(jnp.int32, (seq, 1), 0)
    blocks = [(chain, head) for chain in range(chains) for head in range(heads)]
    scores = [
        jnp.where(
            position < lengths[base + chain],
            dot_tn(block_of(parts[1], chain, head, seq), block_of(scaled, chain, head, seq)),
            MASKED,
        )
        for chain, head in blocks
    ]
    shifted = [jnp.exp(value - jnp.max(value, axis=0, keepdims=True)) for value in scores]
    weights = [(value * (1.0 / row_sum(value))).astype(BF) for value in shifted]
    for index, (chain, head) in enumerate(blocks):
        soft[index] = weights[index]
        ctx[head * HEAD_DIM : (head + 1) * HEAD_DIM, chain * seq : (chain + 1) * seq] = dot_nn(
            block_of(parts[2], chain, head, seq), weights[index]
        ).astype(BF)
    return dot_tn(ctx[...], mats[3])


def norm_back(grad, hat, inv, gain):
    scaled = grad * gain
    mean_one = jnp.mean(scaled, axis=1, keepdims=True)
    mean_two = jnp.mean(scaled * hat, axis=1, keepdims=True)
    return inv * (scaled - mean_one - hat * mean_two)


def norm_parts(values):
    centred = values - jnp.mean(values, axis=1, keepdims=True)
    inv = lax.rsqrt(jnp.mean(centred * centred, axis=1, keepdims=True) + EPSILON)
    return centred * inv, inv


def in_span(starts, counts, chain, chains, seq):
    index = lax.axis_index("tensor") * chains + chain
    position = lax.broadcasted_iota(jnp.int32, (seq, 1), 0)
    return (position >= starts[index]) & (position < starts[index] + counts[index])


EMBED, B_OUT, G_ATTN, S_ATTN, B_BACK, G_FFN, S_FFN = range(7)


def prep_kernel(width, half, b_in, b_query, b_value, wq, wk, wv, wo, attn_mine, bias, rows, sems):
    core, chip = where_am_i()
    for index, ref in enumerate((wq, wk, wv, wo)):
        start = pl.multiple_of(core * half, half)
        copy = pltpu.make_async_copy(
            ref.at[pl.ds(start, half)], attn_mine.at[pl.ds(0, half)], sems.at[0]
        )
        pl.when(chip == index)(copy.start)
    as_row = lambda ref: ref[...].astype(F32).reshape(1, -1)
    rows[...] = jnp.zeros_like(rows)
    rows[0:1, :] = as_row(b_in)
    rows[1:2, :width] = as_row(b_query)
    rows[1:2, 2 * width : 3 * width] = as_row(b_value)
    bias[...] = rows[...].astype(BF)
    copy.wait()
    attn_mine[half : half + BIAS_ROWS, :] = rows[...].astype(BF)


def more_kernel(piece, *refs):
    vectors = refs[:7]
    w_in, w_back, ffn_mine, vecs, sems = refs[7:]
    core, chip = where_am_i()
    for index, ref in enumerate((w_in, w_back)):
        start = pl.multiple_of(chip * piece, piece)
        copy = pltpu.make_async_copy(ref.at[pl.ds(start, piece)], ffn_mine, sems.at[0])
        pl.when(core == index)(copy.start)
    for index, ref in enumerate(vectors):
        vecs[index : index + 1, :] = ref[...].astype(F32).reshape(1, -1)
    vecs[7:8, :] = jnp.zeros((1, vecs.shape[1]), F32)
    copy.wait()


def pick_kernel(own, other, out):
    core, _ = where_am_i()

    @pl.when(core == 0)
    def _():
        out[...] = own[...]

    @pl.when(core == 1)
    def _():
        out[...] = other[...]


def attn_own_kernel(
    width, seq, lengths, starts, counts, hidden, vecs, bias, wq, wk, wv, wo, mixed, qkv, soft, ctx, part
):
    chains = hidden.shape[0] // seq
    for chain in range(chains):
        rows = slice(chain * seq, (chain + 1) * seq)
        span = in_span(starts, counts, chain, chains, seq)
        mixed[rows, :] = jnp.where(span, vecs[EMBED : EMBED + 1, :], hidden[rows, :].astype(F32)).astype(BF)
    mats = (wq[...], wk[...], wv[...], wo[...])
    part[...] = attend(
        width, seq, lengths, mixed[...], mats, bias[1:2, :].astype(F32), qkv, soft, ctx
    )


def attn_mats(mats, width):
    return [mats[i * width : (i + 1) * width, :] for i in range(4)]


def attn_turn_kernel(width, seq, layouts, last, part_rows, count, lengths, mixed, part, vecs, *refs):
    turns = len(layouts)
    firsts, refs = refs[:turns], refs[turns:]
    pieces, refs = refs[:count], refs[count:]
    results, refs = refs[: 5 * turns], refs[5 * turns :]
    all_sems = refs[-turns:]
    started = [
        copy_in(pieces, layouts[turn], part_rows, results[5 * turn + 4], all_sems[turn], attn_place(part_rows))
        for turn in range(turns)
    ]
    total = part[...]
    for turn in range(turns):
        qkv, soft, ctx, bias_in, mats = results[5 * turn : 5 * turn + 5]
        first = firsts[turn]
        bias_in[...] = jnp.broadcast_to(first[part_rows : part_rows + 1, :].astype(F32), bias_in.shape)
        for copy in started[turn]:
            copy.wait()
        bias = first[part_rows + 1 : part_rows + 2, :].astype(F32)
        total = total + attend(
            width, seq, lengths, mixed[...], attn_mats(mats, width), bias, qkv, soft, ctx
        )
    if not last:
        refs[0][...] = total
        return
    hat, inv, normed = refs[:3]
    ahat, ainv = norm_parts(total + mixed[...].astype(F32) + vecs[B_OUT : B_OUT + 1, :])
    hat[...] = ahat
    inv[...] = jnp.broadcast_to(ainv, inv.shape)
    normed[...] = (ahat * vecs[G_ATTN : G_ATTN + 1, :] + vecs[S_ATTN : S_ATTN + 1, :]).astype(BF)


def gelu_both(pre):
    cdf = 0.5 * (1.0 + lax.erf(pre * (0.5**0.5)))
    pdf = jnp.exp(-0.5 * pre * pre) * (0.5 / 3.141592653589793) ** 0.5
    return pre * cdf, cdf + pre * pdf


def ffn_step(normed, mat_in, mat_back, bias, act, slope):
    pre = dot_nn(normed[...], mat_in) + bias
    value, rate = gelu_both(pre)
    act[...] = value.astype(BF)
    slope[...] = rate.astype(BF)
    return dot_nn(act[...], mat_back)


def ffn_own_kernel(normed, mat_in, mat_back, bias, act, slope, total):
    total[...] = ffn_step(
        normed, mat_in[...], mat_back[...], bias[0:1, :].astype(F32), act, slope
    )


def ffn_rest_kernel(part_rows, layout, last, count, normed, part, bias_in, *refs):
    if last:
        (hat1, vecs, cot), refs = refs[:3], refs[3:]
    pieces, refs = refs[:count], refs[count:]
    act, slope, mats = refs[:3]
    sems = refs[-1]
    copies = copy_in(pieces, layout, part_rows, mats, sems, ffn_place(part_rows))
    height = 4 * part_rows
    for copy in copies:
        copy.wait()
    value = part[...] + ffn_step(
        normed, mats[:height, :], mats[height:, :], bias_in[0:1, :], act, slope
    )
    if not last:
        refs[3][...] = value
        return
    layer_out, grad_second, grad_low, small = refs[3:7]
    first = hat1[...] * vecs[G_ATTN : G_ATTN + 1, :] + vecs[S_ATTN : S_ATTN + 1, :]
    hat, inv = norm_parts(first + value + vecs[B_BACK : B_BACK + 1, :])
    gain = vecs[G_FFN : G_FFN + 1, :]
    layer_out[...] = (hat * gain + vecs[S_FFN : S_FFN + 1, :]).astype(BF)
    grad = cot[...].astype(F32)
    back = norm_back(grad, hat, inv, gain)
    grad_second[...] = back
    grad_low[...] = back.astype(BF)
    small[0:1, :] = row_sum(grad * hat)
    small[1:2, :] = row_sum(grad)
    small[2:3, :] = row_sum(back)
    small[3:, :] = jnp.zeros_like(small[3:, :])


def ffn_back_kernel(counts, late, part_rows, grad_low, normed, *refs):
    if late is not None:
        part, refs = refs[0], refs[1:]
        earlier, refs = refs[: 2 * late], refs[2 * late :]
    turns = []
    for count in counts:
        act, slope, *mats = refs[: 2 + count]
        refs = refs[2 + count :]
        turns.append((act, slope, mats))
    kepts, refs = refs[: len(turns)], refs[len(turns) :]
    given, total, bias_grad, whole = refs
    height = 4 * part_rows
    if late is not None:
        value = part[...]
        for index in range(late):
            value = value + dot_nt(earlier[2 * index][...], earlier[2 * index + 1][:height, :])
    bias_grad[...] = jnp.zeros_like(bias_grad)
    for index, (act, slope, mats) in enumerate(turns):
        if len(mats) == 2:
            mat_in, mat_back = mats[0][...], mats[1][...]
        else:
            mat_in, mat_back = mats[0][:height, :], mats[0][height:, :]
        whole[height:, :] = dot_tn(act[...], grad_low[...]).astype(BF)
        grad_act = dot_nt(grad_low[...], mat_back)
        grad_pre = (grad_act * slope[...].astype(F32)).astype(BF)
        bias_grad[index : index + 1, :] = row_sum(grad_pre.astype(F32))
        whole[:height, :] = dot_tn(normed[...], grad_pre).astype(BF)
        if late is None:
            total[...] = grad_pre
        else:
            value = value + dot_nt(grad_pre, mat_in)
        base = index * 4 * part_rows
        scatter_out(whole, part_rows, kepts[index], given, base, ffn_place(part_rows))
    if late is not None:
        total[...] = value


def attend_back(width, seq, grad_low, mats, mixed, qkv, soft, ctx, grad_qkv, whole):
    chains = grad_low.shape[0] // seq
    heads = width // HEAD_DIM
    scale = HEAD_DIM**-0.5
    whole[3 * width :, :] = dot_nn(ctx[...], grad_low).astype(BF)
    grad_ctx = dot_nt(mats[3], grad_low).astype(BF)
    queries, keys, values = (qkv[i * width : (i + 1) * width, :] for i in range(3))
    blocks = [(chain, head) for chain in range(chains) for head in range(heads)]
    grad_weights = [
        dot_tn(block_of(values, chain, head, seq), block_of(grad_ctx, chain, head, seq))
        for chain, head in blocks
    ]
    grad_scores = []
    for index, value in enumerate(grad_weights):
        wide = soft[index].astype(F32)
        product = wide * value
        grad_scores.append((product - wide * row_sum(product)).astype(BF))
    for index, (chain, head) in enumerate(blocks):
        columns = slice(chain * seq, (chain + 1) * seq)
        for slot, value in enumerate(
            (
                dot_nn(block_of(keys, chain, head, seq), grad_scores[index]) * scale,
                dot_nt(block_of(queries, chain, head, seq), grad_scores[index]),
                dot_nt(block_of(grad_ctx, chain, head, seq), soft[index]),
            )
        ):
            start = slot * width + head * HEAD_DIM
            grad_qkv[start : start + HEAD_DIM, columns] = value.astype(BF)
    whole[: 3 * width, :] = dot_nn(grad_qkv[...], mixed).astype(BF)
    ones = jnp.ones((8, grad_low.shape[0]), BF)
    back = dot_tn(grad_qkv[:width, :], mats[0])
    back = back + dot_tn(grad_qkv[width : 2 * width, :], mats[1])
    back = back + dot_tn(grad_qkv[2 * width :, :], mats[2])
    return back, dot_nt(ones, grad_qkv[...])


def attn_back_kernel(width, seq, own, first, part_rows, counts, mixed, part, *refs):
    if first:
        (hat, inv, vecs), refs = refs[:3], refs[3:]
    else:
        (grad_low,), refs = refs[:1], refs[1:]
    if own:
        (starts, counts_ref), refs = refs[:2], refs[2:]
    turns = []
    for count in counts:
        qkv, soft, ctx, *mats = refs[: 3 + count]
        refs = refs[3 + count :]
        turns.append((qkv, soft, ctx, mats))
    kepts, refs = refs[: len(turns)], refs[len(turns) :]
    given, total, bias_grad = refs[:3]
    refs = refs[3:]
    if first:
        (grad_low, small), refs = refs[:2], refs[2:]
    grad_qkv, whole = refs
    if first:
        grad = part[...]
        value = norm_back(grad, hat[...], inv[:, :1], vecs[G_ATTN : G_ATTN + 1, :])
        grad_low[...] = value.astype(BF)
        small[0:1, :] = row_sum(grad * hat[...])
        small[1:2, :] = row_sum(grad)
        small[2:3, :] = row_sum(value)
        small[3:, :] = jnp.zeros_like(small[3:, :])
    else:
        value = part[...]
    bias_grad[...] = jnp.zeros_like(bias_grad)
    for index, (qkv, soft, ctx, refs_in) in enumerate(turns):
        mats = [ref[...] for ref in refs_in] if len(refs_in) == 4 else attn_mats(refs_in[0], width)
        back, sums = attend_back(
            width, seq, grad_low[...], mats, mixed[...], qkv, soft, ctx, grad_qkv, whole
        )
        value = value + back
        bias_grad[index : index + 1, :width] = sums[0:1, :width]
        bias_grad[index : index + 1, width : 2 * width] = sums[0:1, 2 * width :]
        base = index * 4 * part_rows
        scatter_out(whole, part_rows, kepts[index], given, base, attn_place(part_rows))
    if not own:
        total[...] = value
        return
    chains = value.shape[0] // seq
    embed_sum = jnp.zeros((1, value.shape[1]), F32)
    for chain in range(chains):
        rows = slice(chain * seq, (chain + 1) * seq)
        span = in_span(starts, counts_ref, chain, chains, seq)
        total[rows, :] = jnp.where(span, 0.0, value[rows, :]).astype(BF)
        embed_sum = embed_sum + row_sum(jnp.where(span, value[rows, :], 0.0))
    bias_grad[1:2, :] = embed_sum


def split_kernel(value, at_zero, at_one):
    core, _ = where_am_i()
    for index, out in enumerate((at_zero, at_one)):

        @pl.when(core == index)
        def _():
            out[...] = value[...]

        @pl.when(core != index)
        def _():
            out[...] = jnp.zeros_like(out)


def mix_kernel(count, plan, *refs):
    for out, blocks in zip(refs[count:], plan):
        start = 0
        for rows, sources in blocks:
            array, row = sources[0]
            value = refs[array][row : row + rows, :]
            if len(sources) > 1:
                value = value.astype(F32)
                for array, row in sources[1:]:
                    value = value + refs[array][row : row + rows, :].astype(F32)
                value = value.astype(BF)
            out[start : start + rows, :] = value
            start += rows


def ffn_out_kernel(part_rows, layout, count, *refs):
    outs = refs[count:]
    for (array, row), (part, where) in zip(layout, gather_places(*where_am_i())):
        start = pl.multiple_of(where * part_rows, part_rows)
        for index in range(2):

            @pl.when(part == index)
            def _():
                block = refs[array][row : row + part_rows, :]
                outs[index][pl.ds(start, part_rows), :] = block.astype(F32)


def attn_out_kernel(part_rows, layout, count, *refs):
    outs = refs[count:]
    for (array, row), (part, where) in zip(layout, gather_places(*where_am_i())):
        start = pl.multiple_of(part * part_rows, part_rows)
        for index in range(4):

            @pl.when(where == index)
            def _():
                block = refs[array][row : row + part_rows, :]
                outs[index][pl.ds(start, part_rows), :] = block.astype(F32)


def small_kernel(group, rows_of, small_ffn, small_attn, *refs):
    out = refs[-1]
    rank = lax.axis_index("tensor")
    out[...] = jnp.zeros_like(out)
    out[0:3, :] = small_ffn[0:3, :]
    out[3:6, :] = small_attn[0:3, :]
    for index, (array, source) in enumerate(rows_of[:-1]):
        row = 8 + index // group * group + lax.rem(index % group + rank, group)
        out[pl.ds(row, 1), :] = refs[array][source : source + 1, :]
    array, source = rows_of[-1]
    out[6:7, :] = refs[array][source : source + 1, :]


SMEM = pl.BlockSpec(memory_space=pltpu.SMEM)
VMEM = pl.BlockSpec(memory_space=pltpu.VMEM)
ANY = pl.BlockSpec(memory_space=pl.ANY)


def call(kernel, ins, outs, scratch=(), flops=0, vmem=16, name=None):
    arrays = [array for array, _ in ins]
    moved = sum(a.size * a.dtype.itemsize for a in arrays) + sum(
        o.size * o.dtype.itemsize for o in outs
    )
    return pl.pallas_call(
        kernel,
        in_specs=[spec for _, spec in ins],
        out_specs=[VMEM] * len(outs),
        out_shape=list(outs),
        scratch_shapes=list(scratch),
        compiler_params=pltpu.CompilerParams(vmem_limit_bytes=vmem * MIB),
        cost_estimate=pl.CostEstimate(flops=flops // 100, bytes_accessed=moved // 100, transcendentals=0),
        name=name,
    )(*arrays)


def shape(rows, columns, kind=F32):
    return jax.ShapeDtypeStruct((rows, columns), kind)


def pick(own, other):
    return call(
        pick_kernel,
        [(own, VMEM), (other, VMEM)],
        [shape(*own.shape, own.dtype)],
        vmem=4,
        name="pick",
    )[0]


def split(value):
    return call(
        split_kernel,
        [(value, VMEM)],
        [shape(*value.shape, value.dtype)] * 2,
        vmem=4,
        name="split",
    )


def mix(*outs, first=(), name=None):
    refs, plan, shapes = Refs(), [], []
    for blocks in outs:
        mine = []
        for block in blocks:
            sources = block if isinstance(block, list) else [block]
            mine.append((sources[0].rows, tuple(refs.add(source) for source in sources)))
        plan.append(tuple(mine))
        top = blocks[0][0] if isinstance(blocks[0], list) else blocks[0]
        shapes.append(shape(sum(rows for rows, _ in mine), top.array.shape[1], BF))
    if first:
        refs.arrays[0] = after(refs.arrays[0], *first)
    return call(
        functools.partial(mix_kernel, len(refs.arrays), tuple(plan)),
        [(array, VMEM) for array in refs.arrays],
        shapes,
        vmem=4,
        name=name,
    )


def on_device(
    hidden_in,
    lengths,
    span_start,
    span_len,
    mask_embed,
    w_query,
    b_query,
    w_key,
    w_value,
    b_value,
    w_out,
    b_out,
    g_attn,
    s_attn,
    w_in,
    b_in,
    w_back,
    b_back,
    g_ffn,
    s_ffn,
    cotangent,
):
    group = lax.axis_size("tensor")
    dp_size = lax.axis_size("dp")
    moves = Moves(dp_size, group)
    rank = lax.axis_index("tensor")
    rows, model = hidden_in.shape
    seq = rows * group // lengths.shape[0]
    chains = rows // seq
    width = w_query.shape[1]
    heads = width // HEAD_DIM
    hidden = w_in.shape[1]
    piece = model // 4
    half = piece // 2
    turns = (1, 3, 2)
    count = len(turns)

    own_mats = (w_query.T, w_key.T, w_value.T, w_out)
    dma = lambda n: pltpu.SemaphoreType.DMA((8 * n,))

    attn_mine, bias_pack = call(
        functools.partial(prep_kernel, width, half),
        [(v, VMEM) for v in (b_in, b_query, b_value)] + [(v, ANY) for v in own_mats],
        [shape(half + BIAS_ROWS, model, BF), shape(BIAS_ROWS, model, BF)],
        [pltpu.VMEM((BIAS_ROWS, model), F32), pltpu.SemaphoreType.DMA((1,))],
        vmem=60,
        name="prep",
    )
    ffn_mine, vecs = call(
        functools.partial(more_kernel, piece),
        [(v, VMEM) for v in (mask_embed, after(b_out, attn_mine), g_attn, s_attn, b_back, g_ffn, s_ffn)]
        + [(v, ANY) for v in (w_in, w_back)],
        [shape(piece, model, BF), shape(8, model)],
        [pltpu.SemaphoreType.DMA((1,))],
        vmem=60,
        name="more",
    )
    first1, first3 = (moves.fetch(attn_mine, turn) for turn in turns[:2])

    soft_shape = jax.ShapeDtypeStruct((chains * heads, seq, seq), BF)
    turn_flops = 2 * rows * model * 4 * width
    mixed, qkv_own, soft_own, ctx_own, attn_part = call(
        functools.partial(attn_own_kernel, width, seq),
        [(v, SMEM) for v in (lengths, span_start, span_len)]
        + [(v, VMEM) for v in (hidden_in, vecs, bias_pack, *own_mats)],
        [
            shape(rows, model, BF),
            shape(3 * width, rows, BF),
            soft_shape,
            shape(width, rows, BF),
            shape(rows, model),
        ],
        flops=turn_flops,
        name="attn_own",
    )
    first1, first3, mixed, attn_mine, ffn_mine = sync(first1, first3, mixed, attn_mine, ffn_mine)
    first2 = moves.pass_on(pick(first1, first3))
    (mine13,) = mix([Block(first1, 0, half), Block(first3, 0, half)], name="mix_1")
    near13, over13 = moves.near(mine13), moves.far(mine13)

    first2, near13, over13, ffn_mine = sync(first2, near13, over13, ffn_mine)
    ffn1 = moves.fetch(ffn_mine, 1)
    mine2, far = mix([Block(first2, 0, half)], [Block(near13), Block(first2, 0, half)], name="mix_2")
    near2, far13_2 = moves.near(mine2), moves.far(far)

    ffn1, near2, far13_2, ffn_mine = sync(ffn1, near2, far13_2, ffn_mine)
    ffn3 = moves.fetch(ffn_mine, 3)
    own13 = (Block(mine13), Block(near13), Block(over13), Block(far13_2, 0, 2 * half))
    far, other13 = mix([Block(near2), Block(ffn1)], own13, name="mix_3")
    near_f1, far2_f1, other13 = moves.near(ffn1), moves.far(far), moves.core(other13)

    ffn3, near_f1, far2_f1, other13, ffn_mine = sync(ffn3, near_f1, far2_f1, other13, ffn_mine)
    ffn2 = moves.pass_on(pick(ffn1, ffn3))
    own2 = (Block(mine2), Block(near2), Block(far13_2, 2 * half, half), Block(far2_f1, 0, half))
    far, other2 = mix([Block(near_f1), Block(ffn3)], own2, name="mix_4")
    near_f3, far_f1_f3, other2 = moves.near(ffn3), moves.far(far), moves.core(other2)

    def parts(own, other, turn=0, rows=None):
        rows = own[0].rows if rows is None else rows
        blocks = [block.at(turn * rows, rows) for block in own]
        count_turns = own[0].rows // rows
        return blocks + [Block(other, (i * count_turns + turn) * rows, rows) for i in range(4)]

    qkvs, softs, ctxs, bias_ins, attn_wholes = [], [], [], [], []
    for last, firsts in ((False, (first1, first3)), (True, (first2,))):
        if last:
            ffn2, near_f3, far_f1_f3, other2, attn_part = sync(ffn2, near_f3, far_f1_f3, other2, attn_part)
            own_f1 = (Block(ffn1), Block(near_f1), Block(far2_f1, half, piece), Block(far_f1_f3, 0, piece))
            far, other_f1 = mix([Block(near_f3), Block(ffn2)], own_f1, name="mix_5")
            near_f2, far_f3_f2, other_f1 = moves.near(ffn2), moves.far(far), moves.core(other_f1)
        refs = Refs()
        layouts = []
        for index in range(len(firsts)):
            blocks = parts(own2, other2) if last else parts(own13, other13, index, half)
            layouts.append(tuple(refs.add(block) for block in blocks))
        outs = [
            shape(3 * width, rows, BF),
            soft_shape,
            shape(width, rows, BF),
            shape(8, model),
            shape(model, model, BF),
        ] * len(firsts)
        outs += [shape(rows, model)]
        if last:
            outs += [shape(rows, 128), shape(rows, model, BF)]
        results = call(
            functools.partial(attn_turn_kernel, width, seq, tuple(layouts), last, half, len(refs.arrays)),
            [(lengths, SMEM), (mixed, VMEM), (attn_part, VMEM), (vecs, VMEM)]
            + [(first, VMEM) for first in firsts]
            + [(array, ANY) for array in refs.arrays],
            outs,
            [dma(1)] * len(firsts),
            flops=len(firsts) * turn_flops,
            name="attn_2" if last else "attn_13",
        )
        for index in range(len(firsts)):
            for values, value in zip(
                (qkvs, softs, ctxs, bias_ins, attn_wholes), results[5 * index : 5 * index + 5]
            ):
                values.append(value)
        others = results[5 * len(firsts) :]
        attn_part = others[0]
    hat1, inv1, normed = others

    ffn_flops = 2 * rows * model * hidden * 2
    act_own, slope_own, ffn_part = call(
        ffn_own_kernel,
        [(normed, VMEM), (w_in, VMEM), (w_back, VMEM), (bias_pack, VMEM)],
        [shape(rows, hidden, BF), shape(rows, hidden, BF), shape(rows, model)],
        flops=ffn_flops,
        name="ffn_own",
    )
    near_f2, far_f3_f2, other_f1, ffn_part = sync(near_f2, far_f3_f2, other_f1, ffn_part)
    own_f3 = (Block(ffn3), Block(near_f3), Block(far_f1_f3, piece, piece), Block(far_f3_f2, 0, piece))
    (other_f3,) = mix(own_f3, name="mix_6")
    far_f2, other_f3 = moves.far(near_f2), moves.core(other_f3)
    acts, slopes, ffn_wholes = [], [], []
    for index in range(count):
        last = index == count - 1
        if index == 0:
            blocks = parts(own_f1, other_f1)
        elif index == 1:
            far_f2, other_f3, ffn_part = sync(far_f2, other_f3, ffn_part)
            own_f2 = (Block(ffn2), Block(near_f2), Block(far_f3_f2, piece, piece), Block(far_f2))
            (other_f2,) = mix(own_f2, name="mix_7")
            other_f2 = moves.core(other_f2)
            blocks = parts(own_f3, other_f3)
        else:
            blocks = parts(own_f2, other_f2)
        refs = Refs()
        layout = tuple(refs.add(block) for block in blocks)
        ins = [(normed, VMEM), (ffn_part, VMEM), (bias_ins[index], VMEM)]
        outs = [shape(rows, hidden, BF)] * 2 + [shape(2 * model, model, BF)]
        if last:
            ins += [(hat1, VMEM), (vecs, VMEM), (cotangent, VMEM)]
            outs += [shape(rows, model, BF), shape(rows, model), shape(rows, model, BF), shape(8, model)]
        else:
            outs += [shape(rows, model)]
        act, slope, whole, *others = call(
            functools.partial(ffn_rest_kernel, piece, layout, last, len(refs.arrays)),
            ins + [(array, ANY) for array in refs.arrays],
            outs,
            [dma(1)],
            flops=ffn_flops,
            name=f"ffn_{turns[index]}",
        )
        for values, value in zip((acts, slopes, ffn_wholes), (act, slope, whole)):
            values.append(value)
        if last:
            layer_out, grad_second, grad_low, small_ffn = others
        else:
            (ffn_part,) = others

    def ffn_back(*turns_in, part=None, earlier=(), after_this=None, name):
        kinds = tuple(len(turn) - 2 for turn in turns_in)
        late = None if part is None else len(earlier)
        first = grad_low if after_this is None else after(grad_low, after_this)
        ins = [first, normed]
        if part is not None:
            ins += [part] + [v for pair in earlier for v in pair]
        *kepts, given, total, bias = call(
            functools.partial(ffn_back_kernel, kinds, late, piece),
            [(v, VMEM) for v in ins] + [(v, VMEM) for turn in turns_in for v in turn],
            [shape(4 * piece, model, BF)] * len(kinds)
            + [
                shape(4 * len(kinds) * piece, model, BF),
                shape(rows, model, BF if part is None else F32),
                shape(8, model),
            ],
            [pltpu.VMEM((2 * model, model), BF)],
            flops=2 * len(kinds) * ffn_flops,
            name=name,
        )
        return kepts, given, total, bias

    def attn_back(part, grad_low, *turns_in, own=False, name):
        first = grad_low is None
        kinds = tuple(len(turn) - 3 for turn in turns_in)
        ins = [(mixed, VMEM), (part, VMEM)]
        ins += [(v, VMEM) for v in (hat1, inv1, vecs)] if first else [(grad_low, VMEM)]
        if own:
            ins += [(span_start, SMEM), (span_len, SMEM)]
        ins += [(v, VMEM) for turn in turns_in for v in turn]
        outs = [shape(4 * half, model, BF)] * len(kinds)
        outs += [shape(4 * len(kinds) * half, model, BF)]
        outs += [shape(rows, model, BF if own else F32), shape(8, model)]
        if first:
            outs += [shape(rows, model, BF), shape(8, model)]
        return call(
            functools.partial(attn_back_kernel, width, seq, own, first, half, kinds),
            ins,
            outs,
            [pltpu.VMEM((3 * width, rows), BF), pltpu.VMEM((model, model), BF)],
            flops=2 * len(kinds) * turn_flops,
            name=name,
        )

    def ffn_turn(index):
        return (acts[index], slopes[index], ffn_wholes[index])

    def attn_turn(index):
        return (qkvs[index], softs[index], ctxs[index], attn_wholes[index])

    class Slots:
        def __init__(self, kept, come, row=0, more=()):
            self.rows = kept.shape[0] // 4
            self.pieces = [(kept, 0), (come, row), *more]

        def slot(self, index):
            start = index * self.rows
            return [Block(array, row + start, self.rows) for array, row in self.pieces]

        def passed(self, index, *arrived):
            return [self.slot(index) + [Block(array, row, self.rows) for array, row in arrived]]

    (kept2,), given2, pre2, bias2 = ffn_back(ffn_turn(2), name="ffn_back_2")
    come2 = moves.core(given2)
    (kept1,), given1, pre1, bias1 = ffn_back(ffn_turn(0), after_this=pre2, name="ffn_back_1")
    come2, given1, pre1 = sync(come2, given1, pre1)

    f2 = Slots(kept2, come2)
    (far,) = mix([f2.slot(2), f2.slot(1)], name="mix_8")
    far, pre1, given1 = sync(far, pre1, given1)
    far_f2, come1 = moves.far(far), moves.core(given1)
    (kept3, kept0), given30, part, bias30 = ffn_back(
        ffn_turn(1),
        (act_own, slope_own, w_in, w_back),
        part=grad_second,
        earlier=((pre2, ffn_wholes[2]), (pre1, ffn_wholes[0])),
        name="ffn_back_30",
    )
    far_f2, come1, given30, part = sync(far_f2, come1, given30, part)

    f1 = Slots(kept1, come1)
    near, far = mix(f2.passed(0, (far_f2, 0)), [f1.slot(2), f1.slot(1)], name="mix_9")
    near, far, given30, part = sync(near, far, given30, part)
    near_f2, far_f1, come30 = moves.near(near), moves.far(far), moves.core(given30)
    a_kept2, a_kept3, a_given23, part, a_bias23, attn_low, small_attn = attn_back(
        part, None, attn_turn(2), attn_turn(1), name="attn_back_23"
    )
    near_f2, far_f1, come30, a_given23, part = sync(near_f2, far_f1, come30, a_given23, part)

    f3, f0 = Slots(kept3, come30), Slots(kept0, come30, 4 * piece)
    done2, near, far = mix(
        f2.passed(3, (near_f2, 0), (far_f2, piece)),
        f1.passed(0, (far_f1, 0)),
        [f3.slot(2), f3.slot(1)],
        name="mix_10",
    )
    done2, near, far, a_given23, part = sync(done2, near, far, a_given23, part)
    done2, near_f1, far_f3 = moves.hand_on(done2), moves.near(near), moves.far(far)
    a_come23 = moves.core(a_given23)
    a_kept1, a_given1, part, a_bias1 = attn_back(part, attn_low, attn_turn(0), name="attn_back_1")
    near_f1, far_f3, a_come23, done2, a_given1, part = sync(near_f1, far_f3, a_come23, done2, a_given1, part)

    for_one, for_three = split(done2)
    a2, a3 = Slots(a_kept2, a_come23), Slots(a_kept3, a_come23, 4 * half)
    done1, near, far = mix(
        f1.passed(3, (near_f1, 0), (far_f1, piece), (for_one, 0)),
        f3.passed(0, (far_f3, 0)),
        [a2.slot(2), a3.slot(2), a2.slot(1), a3.slot(1)],
        name="mix_11",
    )
    done1, near, far, a_given1, part = sync(done1, near, far, a_given1, part)
    done1, near_f3, far_a23 = moves.give(done1, 1), moves.near(near), moves.far(far)
    a_come1 = moves.core(a_given1)
    a_kept0, a_given0, grad_input, a_bias0 = attn_back(
        part, attn_low, (qkv_own, soft_own, ctx_own, *own_mats), own=True, name="attn_back_0"
    )
    near_f3, far_a23, a_come1, done1, a_given0, grad_input, a_bias0 = sync(
        near_f3, far_a23, a_come1, done1, a_given0, grad_input, a_bias0
    )

    a1 = Slots(a_kept1, a_come1)
    wide = piece + half
    done3, near, far = mix(
        f3.passed(3, (near_f3, 0), (far_f3, piece), (for_three, 0)),
        a2.passed(0, (far_a23, 0)) + a3.passed(0, (far_a23, half)),
        [f0.slot(2), a1.slot(2), f0.slot(1), a1.slot(1)],
        name="mix_12",
    )
    biases = (bias30, bias1, bias2, a_bias0, a_bias1, a_bias23)
    rows_of = ((0, 1), (1, 0), (2, 0), (0, 0), (3, 0), (4, 0), (5, 0), (5, 1), (3, 1))
    (small,) = call(
        functools.partial(small_kernel, group, rows_of),
        [(v, VMEM) for v in (small_ffn, small_attn, *biases)],
        [shape(8 + 2 * group, model)],
        vmem=4,
        name="small",
    )
    flips = [(1 << bit, 0) for bit in range(dp_size.bit_length() - 1)]
    flips += [(0, 1 << bit) for bit in range(group.bit_length() - 1)]

    def small_step(value):
        return value + moves.flip(value, *flips.pop(0))

    done3, near, far, a_given0, small = sync(done3, near, far, a_given0, small)
    done3, near_a23, far_f0_a1 = moves.give(done3, 3), moves.near(near), moves.far(far)
    a_come0 = moves.core(a_given0)
    small = small_step(small_step(small))
    done3, near_a23, far_f0_a1, a_come0, small = sync(done3, near_a23, far_f0_a1, a_come0, small)

    a0 = Slots(a_kept0, a_come0)
    a_done2, near, far = mix(
        a2.passed(3, (near_a23, 0), (far_a23, 2 * half)),
        f0.passed(0, (far_f0_a1, 0)) + a1.passed(0, (far_f0_a1, piece)),
        [a0.slot(2), a0.slot(1)],
        name="mix_13",
    )
    a_done2, near, far, small = sync(a_done2, near, far, small)
    a_done2, near_f0_a1, far_a0 = moves.hand_on(a_done2), moves.near(near), moves.far(far)
    small = small_step(small)
    a_done2, near_f0_a1, far_a0, small = sync(a_done2, near_f0_a1, far_a0, small)

    a_for_one, a_for_three = split(a_done2)
    arrived = ((near_f0_a1, 0), (far_f0_a1, wide), (done1, 0), (done3, 0))
    (ffn_final,) = mix(f0.passed(3, *arrived), name="mix_14")
    if dp_size > 8:
        ffn_final = over_rest(ffn_final, dp_size)
    a_done3, a_done1, near = mix(
        a3.passed(3, (near_a23, half), (far_a23, 3 * half), (a_for_three, 0)),
        a1.passed(3, (near_f0_a1, piece), (far_f0_a1, wide + piece), (a_for_one, 0)),
        a0.passed(0, (far_a0, 0)) + [Block(ffn_final)],
        name="mix_15",
    )
    ffn_final, near, a_done3, a_done1, small = sync(ffn_final, near, a_done3, a_done1, small)
    near_a0_f, ffn_over = moves.near(near), moves.far(ffn_final)
    a_done3, a_done1 = moves.give(a_done3, 3), moves.give(a_done1, 1)
    small = small_step(small)
    near_a0_f, ffn_over, a_done3, a_done1, small = sync(near_a0_f, ffn_over, a_done3, a_done1, small)

    arrived = ((near_a0_f, 0), (far_a0, half), (a_done1, 0), (a_done3, 0))
    (attn_final,) = mix(a0.passed(3, *arrived), name="mix_16")
    if dp_size > 8:
        attn_final = over_rest(attn_final, dp_size)
    (far,) = mix([Block(near_a0_f, half, piece), Block(attn_final)], name="mix_17")
    attn_final, far, small = sync(attn_final, far, small)
    attn_near, far_f_a = moves.near(attn_final), moves.far(far)
    small = small_step(small)
    attn_near, far_f_a, small = sync(attn_near, far_f_a, small)

    own_ffn = (Block(ffn_final), Block(near_a0_f, half, piece), Block(ffn_over), Block(far_f_a, 0, piece))
    (other_ffn,) = mix(own_ffn, name="mix_18")
    attn_near, other_ffn, small = sync(attn_near, other_ffn, small)
    other_ffn = moves.core(other_ffn)
    while flips:
        small = small_step(small)
    attn_corner = moves.far(attn_near)

    def out(kernel, rows_in, own, other, outs, name):
        refs = Refs()
        layout = tuple(refs.add(block) for block in parts(own, other))
        return call(
            functools.partial(kernel, rows_in, layout, len(refs.arrays)),
            [(array, VMEM) for array in refs.arrays],
            outs,
            name=name,
        )

    outs = [shape(model, hidden), shape(hidden, model)]
    grad_w_in, grad_w_back = out(ffn_out_kernel, piece, own_ffn, other_ffn, outs, "ffn_out")
    attn_corner, grad_w_in, grad_w_back, small = sync(attn_corner, grad_w_in, grad_w_back, small)
    own_attn = (Block(attn_final), Block(attn_near), Block(far_f_a, piece, half), Block(attn_corner))
    (other_attn,) = mix(own_attn, name="mix_17")
    other_attn = moves.core(other_attn)
    attn_grads = out(attn_out_kernel, half, own_attn, other_attn, [shape(width, model)] * 4, "attn_out")
    grad_w_query, grad_w_key, grad_w_value = (v.T for v in attn_grads[:3])
    my_in = lax.dynamic_index_in_dim(small, 8 + rank, keepdims=False)
    my_attn = lax.dynamic_index_in_dim(small, 8 + group + rank, keepdims=False)
    return (
        layer_out,
        grad_input,
        small[6],
        grad_w_query,
        my_attn[:width],
        grad_w_key,
        grad_w_value,
        my_attn[width : 2 * width],
        attn_grads[3],
        small[5],
        small[3],
        small[4],
        grad_w_in,
        my_in,
        grad_w_back,
        small[2],
        small[0],
        small[1],
    )


def solution(mesh):
    rows = P(("dp", "tensor"), None)
    placed = (
        rows,
        P("dp"),
        P("dp"),
        P("dp"),
        P(),
        P(None, "tensor"),
        P("tensor"),
        P(None, "tensor"),
        P(None, "tensor"),
        P("tensor"),
        P("tensor", None),
        P(),
        P(),
        P(),
        P(None, "tensor"),
        P("tensor"),
        P("tensor", None),
        P(),
        P(),
        P(),
        rows,
    )
    return jax.shard_map(
        on_device,
        mesh=mesh,
        in_specs=placed,
        out_specs=(
            rows,
            rows,
            P(),
            P(None, "tensor"),
            P("tensor"),
            P(None, "tensor"),
            P(None, "tensor"),
            P("tensor"),
            P("tensor", None),
            P(),
            P(),
            P(),
            P(None, "tensor"),
            P("tensor"),
            P("tensor", None),
            P(),
            P(),
            P(),
        ),
        check_vma=False,
    )
```
